256 devices in a mesh: expert: 8 (over x_lo, y), dp: 32 (over z, x_hi, core).
Axes of the slice: x: 4 (x_hi: 2, x_lo: 2; x = x_hi * 2 + x_lo), y: 4, z: 8, core: 2. Of those that a mesh axis runs over, the one named last changes fastest.
Arguments:
- activations: bfloat16 [4096, 3584], P('dp'), may hold values from -6 to 6
- cotangent: bfloat16 [4096, 3584], P('dp'), may hold values from -6 to 6
- expert_ids: int32 [32, 2], P('dp'), may hold values from 0 to 7, all different within a row
- slot_rows: int32 [32, 2, 128], P('dp'), may hold values from 0 to 127, as said below
- slot_counts: int32 [32, 2], P('dp'), may hold values from 32 to 128, as said below
- route_probs: float32 [32, 2, 128], P('dp'), may hold values from 0.05 to 1
- w_gate: bfloat16 [8, 3584, 2432], P(None, 'dp', 'expert'), may hold values from -0.09375 to 0.09375
- w_up: bfloat16 [8, 3584, 2432], P(None, 'dp', 'expert'), may hold values from -0.09375 to 0.09375
- w_down: bfloat16 [8, 2432, 3584], P(None, 'expert', 'dp'), may hold values from -0.125 to 0.125
Outputs:
- grad_activations: float32 [4096, 3584], P('dp', 'expert')
- grad_gate: float32 [8, 3584, 2432], P(None, 'dp', 'expert')
- grad_up: float32 [8, 3584, 2432], P(None, 'dp', 'expert')
- grad_down: float32 [8, 2432, 3584], P(None, 'expert', 'dp')
The draws below stay inside these ranges and needn't reach their ends.
Inputs may be any that keep to these rules, and one draw needn't show every extreme that they name: `slot_rows`: each group's list for one slot is a permutation of the 128 row indices of that group. `slot_counts`: some slot of some group uses all 128 rows. `expert_ids`: the 2 ids of one group are distinct, and every expert is named by some group.
All inputs are finite; a program needn't handle non-finite values.
Results may differ from the reference program's by a relative error of at most 0.005.
Values may be sent and summed in bfloat16 or wider, within the bound.
A program may use at most 128 MiB of HBM per device.

```python
import jax
import jax.numpy as jnp
from jax import lax

D = 3584
FF = 2432
EXPERTS = 8
SLOTS = 2
TOK_DEV = 128
TOKENS = 4096
ROUTE_GROUPS = 32


def draw_slot_rows(key, part):
    key = jax.random.fold_in(key, 11)
    keys = jax.random.split(key, ROUTE_GROUPS * SLOTS)
    perms = jax.vmap(lambda single: jax.random.permutation(single, TOK_DEV))(keys)
    return perms.reshape(ROUTE_GROUPS, SLOTS, TOK_DEV).astype(jnp.int32)


def draw_slot_counts(key, part):
    key = jax.random.fold_in(key, 23)
    key_counts, key_pick = jax.random.split(key)
    counts = jax.random.randint(key_counts, (ROUTE_GROUPS * SLOTS,), TOK_DEV // 4, TOK_DEV + 1, dtype=jnp.int32)
    chosen = jax.random.randint(key_pick, (), 0, ROUTE_GROUPS * SLOTS, dtype=jnp.int32)
    counts = jnp.where(jnp.arange(ROUTE_GROUPS * SLOTS, dtype=jnp.int32) == chosen, jnp.int32(TOK_DEV), counts)
    return counts.reshape(ROUTE_GROUPS, SLOTS).astype(jnp.int32)


def levels(rng, extent, shards, smallest, high):
    def one(axis_at, parts):
        steps = jax.random.uniform(jax.random.fold_in(jax.random.fold_in(rng, 6), axis_at), (parts,), jnp.float32, smallest / len(shards), high / len(shards))
        return jnp.repeat(jnp.exp(steps), extent[axis_at] // parts).reshape((-1,) + (1,) * (len(extent) - axis_at - 1))

    gain = one(*shards[0])
    for cut in shards[1:]:
        gain = gain * one(*cut)
    return gain


def choose_distinct(own_key, rows, count, top, lift):
    ranking = jax.random.permutation(jax.random.fold_in(own_key, 1), count)
    pull = ranking
    for power in range(3):
        pull = pull * pull // count
    pull = pull * lift // count
    tickets = jax.random.randint(jax.random.fold_in(own_key, 2), (rows, count), 0, 4096) + pull
    sure = jax.random.permutation(jax.random.fold_in(own_key, 3), rows)[jnp.arange(count) % rows]
    tickets = jnp.where(jnp.arange(rows)[:, None] == sure[None, :], 1 << 14, tickets)
    merit = tickets * count + jnp.arange(count)
    return lax.top_k(merit.astype(jnp.int32), top)[1].astype(jnp.int32)


def noise(rng, dims, width, most, cuts=(), kind=jnp.bfloat16):
    loudness = levels(rng, dims, cuts, -0.22, 0.18) if cuts else 1.0
    result = jax.random.normal(rng, dims, jnp.float32) * width * loudness
    return jnp.minimum(jnp.maximum(result, -most), most).astype(kind)


def setup_inputs(seed: int = 0) -> dict:
    seeds = jax.random.split(jax.random.key(seed), 10)
    return {
        "activations": noise(seeds[0], (TOKENS, D), 1.0, 6.0, ((0, 32),)),
        "cotangent": noise(seeds[1], (TOKENS, D), 1.0, 6.0, ((0, 32),)),
        "expert_ids": choose_distinct(seeds[2], ROUTE_GROUPS, EXPERTS, SLOTS, 4096),
        "slot_rows": draw_slot_rows(jax.random.fold_in(seeds[9], 71), 0),
        "slot_counts": draw_slot_counts(jax.random.fold_in(seeds[9], 71), 0),
        "route_probs": jnp.clip(0.05 + 0.95 * jax.random.uniform(seeds[5], (ROUTE_GROUPS, SLOTS, TOK_DEV), jnp.float32) ** levels(seeds[5], (ROUTE_GROUPS, SLOTS, TOK_DEV), ((0, 32),), -0.2, 0.2), 0.05, 1.0),
        "w_gate": noise(seeds[6], (EXPERTS, D, FF), D ** -0.5, 0.09375, ((1, 32), (2, 8))),
        "w_up": noise(seeds[7], (EXPERTS, D, FF), D ** -0.5, 0.09375, ((1, 32), (2, 8))),
        "w_down": noise(seeds[8], (EXPERTS, FF, D), FF ** -0.5, 0.125, ((1, 8), (2, 32))),
    }


def reference(activations, cotangent, expert_ids, slot_rows, slot_counts, route_probs, w_gate, w_up, w_down):
    acts = activations.reshape(ROUTE_GROUPS, TOK_DEV, D)
    cots = cotangent.reshape(ROUTE_GROUPS, TOK_DEV, D)
    position = jnp.arange(TOK_DEV, dtype=jnp.int32)

    def group_step(carry, inputs):
        gate_acc, up_acc, down_acc = carry
        xrows, dyrows, ids, rows, counts, probs = inputs
        grad_rows = jnp.zeros((TOK_DEV, D), jnp.float32)
        for slot in range(SLOTS):
            expert = ids[slot]
            wg = w_gate[expert]
            wu = w_up[expert]
            wd = w_down[expert]
            picked = rows[slot]
            xs = xrows[picked]
            scale = jnp.where(position < counts[slot], probs[slot], jnp.float32(0.0))
            dys = (dyrows[picked].astype(jnp.float32) * scale[:, None]).astype(jnp.bfloat16)
            gval = jnp.dot(xs, wg, preferred_element_type=jnp.float32)
            uval = jnp.dot(xs, wu, preferred_element_type=jnp.float32)
            sig = jax.nn.sigmoid(gval)
            act = gval * sig
            hidden = (act * uval).astype(jnp.bfloat16)
            dhid = jnp.dot(dys, wd.T, preferred_element_type=jnp.float32)
            dgate = (dhid * uval * sig * (1.0 + gval * (1.0 - sig))).astype(jnp.bfloat16)
            dup = (dhid * act).astype(jnp.bfloat16)
            part_gate = lax.optimization_barrier(jnp.dot(xs.T, dgate, preferred_element_type=jnp.float32).astype(jnp.bfloat16))
            part_up = lax.optimization_barrier(jnp.dot(xs.T, dup, preferred_element_type=jnp.float32).astype(jnp.bfloat16))
            part_down = lax.optimization_barrier(jnp.dot(hidden.T, dys, preferred_element_type=jnp.float32).astype(jnp.bfloat16))
            gate_acc = gate_acc.at[expert].add(part_gate.astype(jnp.float32))
            up_acc = up_acc.at[expert].add(part_up.astype(jnp.float32))
            down_acc = down_acc.at[expert].add(part_down.astype(jnp.float32))
            term = jnp.dot(dgate, wg.T, preferred_element_type=jnp.float32) + jnp.dot(dup, wu.T, preferred_element_type=jnp.float32)
            grad_rows = grad_rows.at[picked].add(term)
        return (gate_acc, up_acc, down_acc), grad_rows

    start = (jnp.zeros((EXPERTS, D, FF), jnp.float32), jnp.zeros((EXPERTS, D, FF), jnp.float32), jnp.zeros((EXPERTS, FF, D), jnp.float32))
    carry, grad_rows = lax.scan(group_step, start, (acts, cots, expert_ids, slot_rows, slot_counts, route_probs))
    grad_gate, grad_up, grad_down = carry
    return grad_rows.reshape(TOKENS, D), grad_gate, grad_up, grad_down
```

```python
import functools

import jax
import jax.numpy as jnp
from jax import lax
from jax.experimental import pallas as pl
from jax.experimental.pallas import tpu as pltpu
from jax.sharding import PartitionSpec as P

MESH = pl.DeviceIdType.MESH
F32 = jnp.float32
BF16 = jnp.bfloat16

NZ, NXH, NC, NXL, NY = 8, 2, 2, 2, 4
SLOTS = 2
EXPERTS = 8
TOK = 128
SUB = 112
DZ = 448
FH = 152
F3 = 3 * FH
FP = 464
VMEM_LIMIT = 58 * 1024 * 1024


def place():
    ex = lax.axis_index("expert")
    dp = lax.axis_index("dp")
    return ex // NY, ex % NY, dp // 4, (dp // 2) % 2, dp % 2


def device(xl, y, z, xh, c):
    return (xl * NY + y, z * 4 + xh * 2 + c)


def remote(src, dst, ssem, rsem, dev):
    return pltpu.make_async_remote_copy(
        src_ref=src, dst_ref=dst, send_sem=ssem, recv_sem=rsem, device_id=dev, device_id_type=MESH
    )


def greet(devices):
    barrier = pltpu.get_barrier_semaphore()
    for dev in devices:
        pl.semaphore_signal(barrier, inc=1, device_id=dev, device_id_type=MESH)
    pl.semaphore_wait(barrier, len(devices))


def x_peers(xl, y, z, xh, c):
    pos = xh * 2 + xl
    out = []
    for step in range(1, 4):
        to = (pos + step) % 4
        out.append(device(to % 2, y, z, to // 2, c))
    return out


def y_peers(xl, y, z, xh, c):
    return [device(xl, (y + step) % NY, z, xh, c) for step in range(1, NY)]


def z_peers(xl, y, z, xh, c):
    return [device(xl, y, (z + step) % NZ, xh, c) for step in range(1, NZ)]


def exchange_kernel(
    piece, info, wsend, x_out, info_out, w_out,
    zs, zr, is_, ir, xs, xr, ixs, ixr, ys, yr, ws, wr, loc,
):
    xl, y, z, xh, c = me = place()
    zp, xp, yp = z_peers(*me), x_peers(*me), y_peers(*me)
    far = device(xl, y, z, 1 - xh, c)
    twin = device(xl, y, z, xh, 1 - c)
    greet(zp + xp + yp + [twin])

    cz = []
    for i in range(NZ - 1):
        to = (z + i + 1) % NZ
        cz.append(remote(piece.at[to], x_out.at[xh, xl, y, z], zs.at[i], zr.at[i], zp[i]))
        cz[-1].start()
    ci = []
    for i in range(NZ - 1):
        ci.append(remote(info, info_out.at[xh, z], is_.at[i], ir.at[i], zp[i]))
        ci[-1].start()
    wfar = remote(wsend.at[1 - xh], w_out.at[xh, c], ws.at[0], wr.at[0], far)
    wfar.start()
    wown = remote(wsend.at[xh], w_out.at[xh, c], ws.at[1], wr.at[1], twin)
    wown.start()
    here = [
        pltpu.make_async_copy(piece.at[z], x_out.at[xh, xl, y, z], loc.at[0]),
        pltpu.make_async_copy(info, info_out.at[xh, z], loc.at[1]),
        pltpu.make_async_copy(wsend.at[xh], w_out.at[xh, c], loc.at[2]),
    ]
    for h in here:
        h.start()
    for h in here:
        h.wait()
    for k in cz:
        k.wait()
    cx = []
    for i in range(3):
        cx.append(remote(x_out.at[xh, xl, y], x_out.at[xh, xl, y], xs.at[i], xr.at[i], xp[i]))
        cx[-1].start()
    for k in ci:
        k.wait()
    cinf = remote(info_out.at[xh], info_out.at[xh], ixs.at[0], ixr.at[0], far)
    cinf.start()
    for k in cx:
        k.wait()
    cy = []
    for i in range(3):
        cy.append(remote(x_out.at[:, :, y], x_out.at[:, :, y], ys.at[i], yr.at[i], yp[i]))
        cy[-1].start()
    wfar.wait()
    wpass = remote(w_out.at[1 - xh, c], w_out.at[1 - xh, c], ws.at[2], wr.at[2], twin)
    wpass.start()
    for k in cy:
        k.wait()
    cinf.wait()
    wown.wait()
    wpass.wait()


def exchange(piece, info, wsend):
    dma = pltpu.SemaphoreType.DMA
    anys = pl.BlockSpec(memory_space=pl.ANY)
    return pl.pallas_call(
        exchange_kernel,
        out_shape=(
            jax.ShapeDtypeStruct((NXH, NXL, NY, NZ, SUB, TOK), BF16),
            jax.ShapeDtypeStruct((NXH, NZ, 8, TOK), F32),
            jax.ShapeDtypeStruct((NXH, NC, EXPERTS, SUB, FP), BF16),
        ),
        in_specs=[anys] * 3,
        out_specs=(anys,) * 3,
        scratch_shapes=[dma((7,))] * 4 + [dma((3,))] * 2 + [dma((1,))] * 2 + [dma((3,))] * 2
        + [dma((3,))] * 2 + [dma((3,))],
        compiler_params=pltpu.CompilerParams(collective_id=0, has_side_effects=True),
        name="exchange_in",
    )(piece, info, wsend)


def hidden_kernel(ids, x, w, scale, h, acc, own, rs_s, rs_r, ag_s, ag_r):
    xl, y, z, xh, c = place()
    up = device(xl, y, (z + 1) % NZ, xh, c)
    down = device(xl, y, (z + NZ - 1) % NZ, xh, c)
    greet([up, down])
    to = (up, down)

    def partial(group_z, half, slot):
        e = ids[half * (NZ * SLOTS) + group_z * SLOTS + slot]
        xt = x[half, 0, :, group_z].reshape(DZ, TOK)
        dyt = x[half, 1, :, group_z].reshape(DZ, TOK)
        dys = (dyt.astype(F32) * scale[half, group_z, pl.ds(slot, 1), :]).astype(BF16)
        gu = jnp.dot(w[e, 0 : 2 * FH, :], xt, preferred_element_type=F32)
        dh = jnp.dot(w[e, 2 * FH : FP, :], dys, preferred_element_type=F32)
        return gu, dh[:FH]

    def put(half, slot, gu, dh):
        own[half, slot, 0 : 2 * FH, :] = gu
        own[half, slot, 2 * FH : F3, :] = dh

    def chunk(half, s):
        return (z + NZ - 1 - s) % NZ if half == 0 else (z + 1 + s) % NZ

    def hop(half, slot, s, src):
        return remote(
            src, acc.at[half, s, slot], rs_s.at[half, s, slot], rs_r.at[half, s, slot], to[half]
        )

    for half in range(2):
        for slot in range(SLOTS):
            put(half, slot, *partial(chunk(half, 0), half, slot))
            hop(half, slot, 0, own.at[half, slot]).start()
    for half in range(2):
        for slot in range(SLOTS):
            hop(half, slot, 0, own.at[half, slot]).wait_send()

    def ring(s, carry):
        for half in range(2):
            for slot in range(SLOTS):
                put(half, slot, *partial(chunk(half, s), half, slot))
        for slot in range(SLOTS):
            for half in range(2):
                here = acc.at[half, s - 1, slot]
                hop(half, slot, s - 1, here).wait_recv()
                acc[half, s - 1, slot] = acc[half, s - 1, slot] + own[half, slot]
                hop(half, slot, s, here).start()
        return carry

    lax.fori_loop(1, NZ - 1, ring, 0)

    def gather(half, slot, s, group_z):
        ref = h.at[group_z, half, slot]
        return remote(ref, ref, ag_s.at[half, s, slot], ag_r.at[half, s, slot], to[half])

    def origin(half, s):
        return (z + NZ - s) % NZ if half == 0 else (z + s) % NZ

    for half in range(2):
        for slot in range(SLOTS):
            put(half, slot, *partial(z, half, slot))
    for slot in range(SLOTS):
        for half in range(2):
            last = acc.at[half, NZ - 2, slot]
            hop(half, slot, NZ - 2, last).wait_recv()
            g = acc[half, NZ - 2, slot, 0:FH, :] + own[half, slot, 0:FH, :]
            u = acc[half, NZ - 2, slot, FH : 2 * FH, :] + own[half, slot, FH : 2 * FH, :]
            dh = acc[half, NZ - 2, slot, 2 * FH : F3, :] + own[half, slot, 2 * FH : F3, :]
            sig = 1.0 / (1.0 + jnp.exp(-g))
            act = g * sig
            dg = dh * u * sig * (1.0 + g * (1.0 - sig))
            du = dh * act
            hid = act * u
            h[z, half, slot, 0 : 2 * FH, :] = jnp.concatenate([dg, du], axis=0).astype(BF16)
            h[z, half, slot, 2 * FH : FP, :] = jnp.concatenate(
                [hid, jnp.zeros((FP - F3, TOK), F32)], axis=0
            ).astype(BF16)
            gather(half, slot, 0, z).start()

    def pass_on(s, carry):
        for slot in range(SLOTS):
            for half in range(2):
                gather(half, slot, s - 1, origin(half, s)).wait_recv()
                gather(half, slot, s, origin(half, s)).start()
        return carry

    lax.fori_loop(1, NZ - 1, pass_on, 0)
    for half in range(2):
        for slot in range(SLOTS):
            gather(half, slot, NZ - 2, origin(half, NZ - 1)).wait_recv()

    def drain(s, carry):
        for half in range(2):
            for slot in range(SLOTS):
                hop(half, slot, s, acc.at[half, s - 1, slot]).wait_send()
                gather(half, slot, s, origin(half, s)).wait_send()
        return carry

    lax.fori_loop(1, NZ - 1, drain, 0)
    for half in range(2):
        for slot in range(SLOTS):
            gather(half, slot, 0, z).wait_send()


def hidden_grads(ids, x, w, scale):
    dma = pltpu.SemaphoreType.DMA
    vm = pl.BlockSpec(memory_space=pltpu.VMEM)
    return pl.pallas_call(
        hidden_kernel,
        out_shape=jax.ShapeDtypeStruct((NZ, NXH, SLOTS, FP, TOK), BF16),
        in_specs=[pl.BlockSpec(memory_space=pltpu.SMEM), vm, vm, vm],
        out_specs=vm,
        scratch_shapes=[
            pltpu.VMEM((2, NZ - 1, SLOTS, F3, TOK), F32),
            pltpu.VMEM((2, SLOTS, F3, TOK), F32),
        ]
        + [dma((2, NZ - 1, SLOTS))] * 4,
        compiler_params=pltpu.CompilerParams(
            collective_id=1, has_side_effects=True, vmem_limit_bytes=VMEM_LIMIT
        ),
        name="hidden_grads",
    )(ids, x, w, scale)


def local_kernel(ids, x, w, scale, h, dw, dx):
    def clear(e, carry):
        dw[e] = jnp.zeros((DZ, FP), F32)
        return carry

    lax.fori_loop(0, EXPERTS, clear, 0)
    column = lax.broadcasted_iota(jnp.int32, (DZ, FP), 1)
    nt = (((1,), (1,)), ((), ()))

    def group(i, carry):
        half, gz = i // NZ, i % NZ
        xt = x[half, 0, :, gz].reshape(DZ, TOK)
        dyt = x[half, 1, :, gz].reshape(DZ, TOK).astype(F32)
        total = jnp.zeros((DZ, TOK), F32)
        for slot in range(SLOTS):
            e = ids[i * SLOTS + slot]
            hs = h[gz, half, slot]
            total = total + jnp.dot(
                w[e, :, 0 : 2 * FH], hs[0 : 2 * FH], preferred_element_type=F32
            )
            dys = (dyt * scale[half, gz, pl.ds(slot, 1), :]).astype(BF16)
            gu = lax.dot_general(xt, hs, nt, preferred_element_type=F32)
            dn = lax.dot_general(dys, hs, nt, preferred_element_type=F32)
            dw[e] = dw[e] + jnp.where(column < 2 * FH, gu, dn)
        dx[half, gz] = total
        return carry

    lax.fori_loop(0, NXH * NZ, group, 0)


def local_grads(ids, x, w, scale, h):
    vm = pl.BlockSpec(memory_space=pltpu.VMEM)
    return pl.pallas_call(
        local_kernel,
        out_shape=(
            jax.ShapeDtypeStruct((EXPERTS, DZ, FP), F32),
            jax.ShapeDtypeStruct((NXH, NZ, DZ, TOK), F32),
        ),
        in_specs=[pl.BlockSpec(memory_space=pltpu.SMEM), vm, vm, vm, vm],
        out_specs=(vm, vm),
        compiler_params=pltpu.CompilerParams(vmem_limit_bytes=VMEM_LIMIT),
        name="local_grads",
    )(ids, x, w, scale, h)


def out_kernel(
    dw, dx, wout, xout, wgot, wsnd, wfar, a1, a2, b1, b2, sa, sb, done,
    ts, tr, fs, fr, a1s, a1r, a2s, a2r, b1s, b1r, b2s, b2r, ks, kr,
):
    xl, y, z, xh, c = me = place()
    xp, yp = x_peers(*me), y_peers(*me)
    far = device(xl, y, z, 1 - xh, c)
    twin = device(xl, y, z, xh, 1 - c)
    ex = xl * NY + y
    swap = device(z // NY, z % NY, ex, xh, c)
    barrier = pltpu.get_barrier_semaphore()
    for dev in xp + yp + [twin]:
        pl.semaphore_signal(barrier, inc=1, device_id=dev, device_id_type=MESH)

    @pl.when(ex != z)
    def _():
        pl.semaphore_signal(barrier, inc=1, device_id=swap, device_id_type=MESH)

    pl.semaphore_wait(barrier, 7 + jnp.where(ex != z, 1, 0))

    hd = DZ // 2
    ca = []
    for i in range(3):
        to = (y + i + 1) % NY
        ca.append(
            remote(dx.at[:, :, to, pl.ds(0, hd)], a1.at[i], a1s.at[i], a1r.at[i], yp[i])
        )
        ca[-1].start()
    pos = xh * 2 + xl
    cb = []
    for i in range(3):
        to = (pos + i + 1) % 4
        cb.append(
            remote(
                dx.at[to // 2, to % 2, :, pl.ds(hd, hd)], b1.at[i], b1s.at[i], b1r.at[i], xp[i]
            )
        )
        cb[-1].start()
    ct = []
    for i in range(2):
        blk = (1 - xh) if i == 0 else xh
        ct.append(
            remote(dw.at[:, 2 * blk + 1 - c], wgot.at[i], ts.at[i], tr.at[i], twin)
        )
        ct[-1].start()
    ct[0].wait_recv()

    def add_far(e, carry):
        wsnd[e] = (dw[e, 2 * (1 - xh) + c] + wgot[0, e]).astype(BF16)
        return carry

    lax.fori_loop(0, EXPERTS, add_far, 0)
    cf = remote(wsnd, wfar, fs.at[0], fr.at[0], far)
    cf.start()
    ct[1].wait_recv()

    def add_own(e, carry):
        wout[xh, e] = dw[e, 2 * xh + c] + wgot[1, e]
        return carry

    lax.fori_loop(0, EXPERTS, add_own, 0)

    for k in ca:
        k.wait_recv()
    for i in range(NXH):
        for j in range(NXL):
            sa[i, j] = dx[i, j, y, 0:hd] + a1[0, i, j] + a1[1, i, j] + a1[2, i, j]
    ca2 = []
    for i in range(3):
        to = (pos + i + 1) % 4
        ca2.append(
            remote(sa.at[to // 2, to % 2], a2.at[i], a2s.at[i], a2r.at[i], xp[i])
        )
        ca2[-1].start()
    for k in cb:
        k.wait_recv()
    for j in range(NY):
        sb[j] = dx[xh, xl, j, hd:DZ] + b1[0, j] + b1[1, j] + b1[2, j]
    cb2 = []
    for i in range(3):
        to = (y + i + 1) % NY
        cb2.append(remote(sb.at[to], b2.at[i], b2s.at[i], b2r.at[i], yp[i]))
        cb2[-1].start()
    for k in ca2:
        k.wait_recv()
    done[0:hd] = sa[xh, xl] + a2[0] + a2[1] + a2[2]
    for k in cb2:
        k.wait_recv()
    done[hd:DZ] = sb[y] + b2[0] + b2[1] + b2[2]

    @pl.when(ex != z)
    def _():
        remote(done, xout, ks.at[0], kr.at[0], swap).start()

    @pl.when(ex == z)
    def _():
        xout[...] = done[...]

    cf.wait_recv()

    def widen(e, carry):
        wout[1 - xh, e] = wfar[e].astype(F32)
        return carry

    lax.fori_loop(0, EXPERTS, widen, 0)

    for k in ca + cb + ct + ca2 + cb2 + [cf]:
        k.wait_send()

    @pl.when(ex != z)
    def _():
        remote(done, xout, ks.at[0], kr.at[0], swap).wait()


def exchange_out(dw, dx):
    dma = pltpu.SemaphoreType.DMA
    vm = pl.BlockSpec(memory_space=pltpu.VMEM)
    hd = DZ // 2
    block = (EXPERTS, SUB, FP)
    return pl.pallas_call(
        out_kernel,
        out_shape=(
            jax.ShapeDtypeStruct((NXH, EXPERTS, SUB, FP), F32),
            jax.ShapeDtypeStruct((DZ, TOK), F32),
        ),
        in_specs=[vm, vm],
        out_specs=(vm, vm),
        scratch_shapes=[
            pltpu.VMEM((2,) + block, F32),
            pltpu.VMEM(block, BF16),
            pltpu.VMEM(block, BF16),
            pltpu.VMEM((3, NXH, NXL, hd, TOK), F32),
            pltpu.VMEM((3, hd, TOK), F32),
            pltpu.VMEM((3, NY, hd, TOK), F32),
            pltpu.VMEM((3, hd, TOK), F32),
            pltpu.VMEM((NXH, NXL, hd, TOK), F32),
            pltpu.VMEM((NY, hd, TOK), F32),
            pltpu.VMEM((DZ, TOK), F32),
        ]
        + [dma((2,))] * 2 + [dma((1,))] * 2 + [dma((3,))] * 8 + [dma((1,))] * 2,
        compiler_params=pltpu.CompilerParams(
            collective_id=2, has_side_effects=True, vmem_limit_bytes=VMEM_LIMIT
        ),
        name="exchange_out",
    )(dw, dx)


def shards(
    activations, cotangent, expert_ids, slot_rows, slot_counts, route_probs, w_gate, w_up, w_down
):
    ex = lax.axis_index("expert")
    dp = lax.axis_index("dp")
    xl, y, xh = ex // NY, ex % NY, (dp // 2) % 2

    down_t = w_down.transpose(0, 2, 1)
    wsend = jnp.stack(
        [
            jnp.concatenate(
                [
                    w_gate[:, :, i * FH : (i + 1) * FH],
                    w_up[:, :, i * FH : (i + 1) * FH],
                    down_t[:, :, i * FH : (i + 1) * FH],
                    jnp.zeros((EXPERTS, SUB, FP - F3), BF16),
                ],
                axis=2,
            )
            for i in range(NXH)
        ]
    )

    source = jnp.where(xl == 0, activations, cotangent).reshape(TOK, NZ, NY, SUB)
    piece = lax.dynamic_index_in_dim(source, y, axis=2, keepdims=False).transpose(1, 2, 0)

    position = jnp.arange(TOK, dtype=jnp.int32)
    weight = jnp.where(position[None, :] < slot_counts[0][:, None], route_probs[0], 0.0)
    hit = slot_rows[0][:, :, None] == position[None, None, :]
    row_scale = jnp.sum(jnp.where(hit, weight[:, :, None], 0.0), axis=1)
    info = jnp.concatenate(
        [
            row_scale,
            jnp.broadcast_to(expert_ids[0].astype(F32)[:, None], (SLOTS, TOK)),
            jnp.zeros((4, TOK), F32),
        ]
    )

    x_all, info_all, w_all = exchange(piece, info, wsend)
    ids = info_all[:, :, 2:4, 0].astype(jnp.int32).reshape(-1)
    w_df = w_all.transpose(2, 0, 1, 3, 4).reshape(EXPERTS, DZ, FP)
    w_fd = w_df.transpose(0, 2, 1)
    h = hidden_grads(ids, x_all, w_fd, info_all)
    dw, dx = local_grads(ids, x_all, w_df, info_all, h)
    wout, xout = exchange_out_call(dw, dx)
    grad_gate = jnp.concatenate([wout[0, :, :, 0:FH], wout[1, :, :, 0:FH]], axis=2)
    grad_up = jnp.concatenate(
        [wout[0, :, :, FH : 2 * FH], wout[1, :, :, FH : 2 * FH]], axis=2
    )
    grad_down = jnp.concatenate(
        [wout[0, :, :, 2 * FH : F3], wout[1, :, :, 2 * FH : F3]], axis=2
    ).transpose(0, 2, 1)
    return xout.T, grad_gate, grad_up, grad_down


def exchange_out_call(dw, dx):
    return exchange_out(
        dw.reshape(EXPERTS, NXH * NC, SUB, FP), dx.reshape(NXH, NXL, NY, DZ, TOK)
    )


def solution(mesh):
    return jax.shard_map(
        shards,
        mesh=mesh,
        in_specs=(
            P("dp", None),
            P("dp", None),
            P("dp", None),
            P("dp", None, None),
            P("dp", None),
            P("dp", None, None),
            P(None, "dp", "expert"),
            P(None, "dp", "expert"),
            P(None, "expert", "dp"),
        ),
        out_specs=(
            P("dp", "expert"),
            P(None, "dp", "expert"),
            P(None, "dp", "expert"),
            P(None, "expert", "dp"),
        ),
        check_vma=False,
    )
```

```python
import jax
import jax.numpy as jnp
from jax import lax
from jax.experimental import pallas as pl
from jax.experimental.pallas import tpu as pltpu
from jax.sharding import PartitionSpec as P

MESH = pl.DeviceIdType.MESH
F32 = jnp.float32
BF16 = jnp.bfloat16

NZ, NXH, NC, NXL, NY = 8, 2, 2, 2, 4
SLOTS = 2
EXPERTS = 8
TOK = 128
SUB = 112
DZ = 448
FH = 152
F3 = 3 * FH
FP = 464
VMEM_LIMIT = 58 * 1024 * 1024


def place():
    ex = lax.axis_index("expert")
    dp = lax.axis_index("dp")
    return ex // NY, ex % NY, dp // 4, (dp // 2) % 2, dp % 2


def device(xl, y, z, xh, c):
    return (xl * NY + y, z * 4 + xh * 2 + c)


def remote(src, dst, ssem, rsem, dev):
    return pltpu.make_async_remote_copy(
        src_ref=src, dst_ref=dst, send_sem=ssem, recv_sem=rsem, device_id=dev, device_id_type=MESH
    )


def greet(devices):
    barrier = pltpu.get_barrier_semaphore()
    for dev in devices:
        pl.semaphore_signal(barrier, inc=1, device_id=dev, device_id_type=MESH)
    pl.semaphore_wait(barrier, len(devices))


def x_peers(xl, y, z, xh, c):
    pos = xh * 2 + xl
    out = []
    for step in range(1, 4):
        to = (pos + step) % 4
        out.append(device(to % 2, y, z, to // 2, c))
    return out


def y_peers(xl, y, z, xh, c):
    return [device(xl, (y + step) % NY, z, xh, c) for step in range(1, NY)]


def z_peers(xl, y, z, xh, c):
    return [device(xl, y, (z + step) % NZ, xh, c) for step in range(1, NZ)]


def exchange_kernel(
    piece, info, wsend, x_out, info_out, w_out, wt_out,
    zs, zr, is_, ir, xs, xr, ixs, ixr, fs, fr, os_, or_, ps, pr, loc,
):
    xl, y, z, xh, c = me = place()
    zp, xp = z_peers(*me), x_peers(*me)
    far = device(xl, y, z, 1 - xh, c)
    twin = device(xl, y, z, xh, 1 - c)
    greet(zp + xp + [twin])
    mine = 2 * xh + c
    other = 2 * (1 - xh) + c

    wfar = []
    for e in range(EXPERTS):
        wfar.append(
            remote(wsend.at[1 - xh, e], w_out.at[e, mine], fs.at[e], fr.at[e], far)
        )
        wfar[-1].start()
    cz = []
    for i in range(NZ - 1):
        to = (z + i + 1) % NZ
        cz.append(remote(piece.at[to], x_out.at[xh, xl, z], zs.at[i], zr.at[i], zp[i]))
        cz[-1].start()
    ci = []
    for i in range(NZ - 1):
        ci.append(remote(info, info_out.at[xh, z], is_.at[i], ir.at[i], zp[i]))
        ci[-1].start()
    wown = []
    for e in range(EXPERTS):
        wown.append(
            remote(wsend.at[xh, e], w_out.at[e, mine], os_.at[e], or_.at[e], twin)
        )
        wown[-1].start()
    here = [
        pltpu.make_async_copy(piece.at[z], x_out.at[xh, xl, z], loc.at[0]),
        pltpu.make_async_copy(info, info_out.at[xh, z], loc.at[1]),
        pltpu.make_async_copy(wsend.at[xh], w_out.at[:, mine], loc.at[2]),
    ]
    for h in here:
        h.start()
    for h in here:
        h.wait()
    for k in cz:
        k.wait()
    cx = []
    for i in range(3):
        cx.append(remote(x_out.at[xh, xl], x_out.at[xh, xl], xs.at[i], xr.at[i], xp[i]))
        cx[-1].start()
    for k in ci:
        k.wait()
    cinf = remote(info_out.at[xh], info_out.at[xh], ixs.at[0], ixr.at[0], far)
    cinf.start()
    wpass = []
    for e in range(EXPERTS):
        wfar[e].wait_recv()
        wpass.append(
            remote(w_out.at[e, other], w_out.at[e, other], ps.at[e], pr.at[e], twin)
        )
        wpass[-1].start()
    for e in range(EXPERTS):
        wown[e].wait_recv()
        wpass[e].wait_recv()
        wt_out[e] = w_out[e].reshape(DZ, FP).T
    for k in cx:
        k.wait()
    cinf.wait()
    for k in wfar + wown + wpass:
        k.wait_send()


def exchange(piece, info, wsend):
    dma = pltpu.SemaphoreType.DMA
    vm = pl.BlockSpec(memory_space=pltpu.VMEM)
    return pl.pallas_call(
        exchange_kernel,
        out_shape=(
            jax.ShapeDtypeStruct((NXH, NXL, NZ, SUB, TOK), BF16),
            jax.ShapeDtypeStruct((NXH, NZ, 8, TOK), F32),
            jax.ShapeDtypeStruct((EXPERTS, NXH * NC, SUB, FP), BF16),
            jax.ShapeDtypeStruct((EXPERTS, FP, DZ), BF16),
        ),
        in_specs=[vm] * 3,
        out_specs=(vm,) * 4,
        scratch_shapes=[dma((7,))] * 4 + [dma((3,))] * 2 + [dma((1,))] * 2 + [dma((EXPERTS,))] * 6
        + [dma((3,))],
        compiler_params=pltpu.CompilerParams(
            collective_id=0, has_side_effects=True, vmem_limit_bytes=VMEM_LIMIT
        ),
        name="exchange_in",
    )(piece, info, wsend)


def layer_kernel(
    ids, xin, w, wt, scale, wout, xout,
    x, acc, own, h, xcat, dcat, hcat, dx, dw, wgot, wsnd, wfar, a1, a2, b1, b2, sa, sb, done,
    loc, y_s, y_r, rs_s, rs_r, ag_s, ag_r,
    a1s, a1r, b1s, b1r, a2s, a2r, b2s, b2r, ts, tr, fs, fr, ks, kr,
):
    xl, y, z, xh, c = me = place()
    ex = xl * NY + y
    pos = xh * 2 + xl
    hd = DZ // 2
    xp, yp = x_peers(*me), y_peers(*me)
    up = device(xl, y, (z + 1) % NZ, xh, c)
    down = device(xl, y, (z + NZ - 1) % NZ, xh, c)
    to = (up, down)
    far = device(xl, y, z, 1 - xh, c)
    twin = device(xl, y, z, xh, 1 - c)
    swap = device(z // NY, z % NY, ex, xh, c)
    barrier = pltpu.get_barrier_semaphore()
    for dev in xp + yp + [up, down, twin]:
        pl.semaphore_signal(barrier, inc=1, device_id=dev, device_id_type=MESH)

    @pl.when(ex != z)
    def _():
        pl.semaphore_signal(barrier, inc=1, device_id=swap, device_id_type=MESH)

    pl.semaphore_wait(barrier, 9 + jnp.where(ex != z, 1, 0))

    def chunk(half, s):
        return (z + 2 * NZ - 1 - s) % NZ if half == 0 else (z + 1 + s) % NZ

    def spread(half, s, i):
        gz = chunk(half, s)
        return remote(
            xin.at[half, :, gz], x.at[half, :, y, gz], y_s.at[half, s, i], y_r.at[half, s, i], yp[i]
        )

    def spread_all(s):
        for half in range(2):
            for i in range(3):
                spread(half, s, i).start()

    def await_all(s):
        for half in range(2):
            for i in range(3):
                spread(half, s, i).wait_recv()

    keep = pltpu.make_async_copy(xin, x.at[:, :, y], loc.at[0])
    keep.start()
    spread_all(0)
    spread_all(1)
    keep.wait()

    def partial(half, gz):
        lanes = pl.ds(pl.multiple_of((half * NZ + gz) * TOK, TOK), TOK)
        xt = x[half, 0, :, gz].reshape(DZ, TOK)
        dyt = x[half, 1, :, gz].reshape(DZ, TOK).astype(F32)
        xcat[:, lanes] = xt
        for slot in range(SLOTS):
            e = ids[half * (NZ * SLOTS) + gz * SLOTS + slot]
            dys = (dyt * scale[half, gz, pl.ds(slot, 1), :]).astype(BF16)
            dcat[slot, :, lanes] = dys
            gu = jnp.dot(wt[e, 0 : 2 * FH, :], xt, preferred_element_type=F32)
            dh = jnp.dot(wt[e, 2 * FH : FP, :], dys, preferred_element_type=F32)
            own[half, slot, 0 : 2 * FH, :] = gu
            own[half, slot, 2 * FH : F3, :] = dh[:FH]

    def hop(half, slot, s, src):
        return remote(
            src, acc.at[half, s, slot], rs_s.at[half, s, slot], rs_r.at[half, s, slot], to[half]
        )

    await_all(0)
    for half in range(2):
        partial(half, chunk(half, 0))
        for slot in range(SLOTS):
            hop(half, slot, 0, own.at[half, slot]).start()
    for half in range(2):
        for slot in range(SLOTS):
            hop(half, slot, 0, own.at[half, slot]).wait_send()

    def ring(s, carry):
        spread_all(s + 1)
        await_all(s)
        for half in range(2):
            partial(half, chunk(half, s))
        for slot in range(SLOTS):
            for half in range(2):
                here = acc.at[half, s - 1, slot]
                hop(half, slot, s - 1, here).wait_recv()
                acc[half, s - 1, slot] = acc[half, s - 1, slot] + own[half, slot]
                hop(half, slot, s, here).start()
        return carry

    lax.fori_loop(1, NZ - 1, ring, 0)
    await_all(NZ - 1)

    def gather(half, slot, s, gz):
        ref = h.at[gz, half, slot]
        return remote(ref, ref, ag_s.at[half, s, slot], ag_r.at[half, s, slot], to[half])

    def origin(half, s):
        return (z + NZ - s) % NZ if half == 0 else (z + s) % NZ

    def rows_a(half, gz):
        i = (gz % NY - y + NY) % NY
        src = dx.at[half, gz // NY, gz % NY, pl.ds(0, hd)]
        return i, lambda: remote(
            src, a1.at[i - 1, half, gz // NY], a1s.at[half, gz], a1r.at[i - 1, half, gz // NY],
            device(xl, gz % NY, z, xh, c),
        )

    def rows_b(half, gz):
        i = (half * 2 + gz // NY - pos + 4) % 4
        src = dx.at[half, gz // NY, gz % NY, pl.ds(hd, hd)]
        return i, lambda: remote(
            src, b1.at[i - 1, gz % NY], b1s.at[half, gz], b1r.at[i - 1, gz % NY],
            device(gz // NY, y, z, half, c),
        )

    def rows(half, gz):
        lanes = pl.ds(pl.multiple_of((half * NZ + gz) * TOK, TOK), TOK)
        total = jnp.zeros((DZ, TOK), F32)
        for slot in range(SLOTS):
            e = ids[half * (NZ * SLOTS) + gz * SLOTS + slot]
            hs = h[gz, half, slot]
            hcat[slot, :, lanes] = hs
            total = total + jnp.dot(
                w[e, :, 0 : 2 * FH], hs[0 : 2 * FH], preferred_element_type=F32
            )
        dx[half, gz // NY, gz % NY] = total
        for i, make in (rows_a(half, gz), rows_b(half, gz)):

            @pl.when(i != 0)
            def _(make=make):
                make().start()

    for half in range(2):
        partial(half, z)
    for slot in range(SLOTS):
        for half in range(2):
            last = acc.at[half, NZ - 2, slot]
            hop(half, slot, NZ - 2, last).wait_recv()
            g = acc[half, NZ - 2, slot, 0:FH, :] + own[half, slot, 0:FH, :]
            u = acc[half, NZ - 2, slot, FH : 2 * FH, :] + own[half, slot, FH : 2 * FH, :]
            dh = acc[half, NZ - 2, slot, 2 * FH : F3, :] + own[half, slot, 2 * FH : F3, :]
            sig = 1.0 / (1.0 + jnp.exp(-g))
            act = g * sig
            dg = dh * u * sig * (1.0 + g * (1.0 - sig))
            du = dh * act
            hid = act * u
            h[z, half, slot, 0 : 2 * FH, :] = jnp.concatenate([dg, du], axis=0).astype(BF16)
            h[z, half, slot, 2 * FH : FP, :] = jnp.concatenate(
                [hid, jnp.zeros((FP - F3, TOK), F32)], axis=0
            ).astype(BF16)
            gather(half, slot, 0, z).start()
    for half in range(2):
        rows(half, z)

    def pass_on(s, carry):
        for slot in range(SLOTS):
            for half in range(2):
                gather(half, slot, s - 1, origin(half, s)).wait_recv()
                gather(half, slot, s, origin(half, s)).start()
        for half in range(2):
            rows(half, origin(half, s))
        return carry

    lax.fori_loop(1, NZ - 1, pass_on, 0)
    for half in range(2):
        for slot in range(SLOTS):
            gather(half, slot, NZ - 2, origin(half, NZ - 1)).wait_recv()
        rows(half, origin(half, NZ - 1))

    cols = NXH * NZ * TOK
    def expert_row(slot):
        return jnp.concatenate(
            [
                scale[i // NZ, i % NZ, 2 + slot : 3 + slot, :]
                for i in range(NXH * NZ)
            ],
            axis=1,
        )

    id0, id1 = expert_row(0), expert_row(1)
    nt = (((1,), (1,)), ((), ()))

    def weights(e):
        is0 = jnp.broadcast_to(id0 == e.astype(F32), (16, cols))
        is1 = jnp.broadcast_to(id1 == e.astype(F32), (16, cols))
        zero = jnp.zeros((16, cols), BF16)

        def pick(pair, n):
            return jnp.concatenate(
                [
                    jnp.where(
                        is0,
                        pair[0, r * 16 : (r + 1) * 16, :],
                        jnp.where(is1, pair[1, r * 16 : (r + 1) * 16, :], zero),
                    )
                    for r in range(n // 16)
                ],
                axis=0,
            )

        hs = pick(hcat, FP)
        ds = pick(dcat, DZ)
        gu = lax.dot_general(xcat[...], hs, nt, preferred_element_type=F32)
        dn = lax.dot_general(ds, hs[256:], nt, preferred_element_type=F32)
        column = lax.broadcasted_iota(jnp.int32, (DZ, FP - 256), 1)
        tail = jnp.where(column < 2 * FH - 256, gu[:, 256:], dn)
        for q in range(NXH * NC):
            dw[e, q, :, 0:256] = gu[q * SUB : (q + 1) * SUB, 0:256]
            dw[e, q, :, 256:FP] = tail[q * SUB : (q + 1) * SUB]

    def cross(e, i):
        blk = (1 - xh) if i == 0 else xh
        return remote(dw.at[e, 2 * blk + 1 - c], wgot.at[i, e], ts.at[i, e], tr.at[i, e], twin)

    def away(e):
        return remote(wsnd.at[e], wfar.at[e], fs.at[e], fr.at[e], far)

    def combine(e):
        cross(e, 0).wait_recv()
        wsnd[e] = (dw[e, 2 * (1 - xh) + c] + wgot[0, e]).astype(BF16)
        away(e).start()
        cross(e, 1).wait_recv()
        wout[xh, e] = dw[e, 2 * xh + c] + wgot[1, e]

    def per_expert(e, carry):
        weights(e)
        cross(e, 0).start()
        cross(e, 1).start()

        @pl.when(e > 0)
        def _():
            combine(e - 1)

        return carry

    lax.fori_loop(0, EXPERTS, per_expert, 0)
    combine(EXPERTS - 1)

    for i in range(3):
        for j in range(NXH):
            for k in range(NXL):
                remote(
                    dx.at[0, 0, 0, pl.ds(0, hd)], a1.at[i, j, k], a1s.at[0, 0], a1r.at[i, j, k], up
                ).wait_recv()
    for j in range(NXH):
        for k in range(NXL):
            sa[j, k] = dx[j, k, y, 0:hd] + a1[0, j, k] + a1[1, j, k] + a1[2, j, k]
    ca2 = []
    for i in range(3):
        t = (pos + i + 1) % 4
        ca2.append(remote(sa.at[t // 2, t % 2], a2.at[i], a2s.at[i], a2r.at[i], xp[i]))
        ca2[-1].start()
    for i in range(3):
        for j in range(NY):
            remote(
                dx.at[0, 0, 0, pl.ds(hd, hd)], b1.at[i, j], b1s.at[0, 0], b1r.at[i, j], up
            ).wait_recv()
    for j in range(NY):
        sb[j] = dx[xh, xl, j, hd:DZ] + b1[0, j] + b1[1, j] + b1[2, j]
    cb2 = []
    for i in range(3):
        t = (y + i + 1) % NY
        cb2.append(remote(sb.at[t], b2.at[i], b2s.at[i], b2r.at[i], yp[i]))
        cb2[-1].start()
    for k in ca2:
        k.wait_recv()
    done[0:hd] = sa[xh, xl] + a2[0] + a2[1] + a2[2]
    for k in cb2:
        k.wait_recv()
    done[hd:DZ] = sb[y] + b2[0] + b2[1] + b2[2]

    @pl.when(ex != z)
    def _():
        remote(done, xout, ks.at[0], kr.at[0], swap).start()

    @pl.when(ex == z)
    def _():
        xout[...] = done[...]

    def widen(e, carry):
        away(e).wait_recv()
        wout[1 - xh, e] = wfar[e].astype(F32)
        return carry

    lax.fori_loop(0, EXPERTS, widen, 0)

    def drain_ring(s, carry):
        for half in range(2):
            for slot in range(SLOTS):
                hop(half, slot, s, acc.at[half, s - 1, slot]).wait_send()
                gather(half, slot, s, origin(half, s)).wait_send()
        return carry

    lax.fori_loop(1, NZ - 1, drain_ring, 0)
    for half in range(2):
        for slot in range(SLOTS):
            gather(half, slot, 0, z).wait_send()

    def drain(s, carry):
        for half in range(2):
            for i in range(3):
                spread(half, s, i).wait_send()
            for i, make in (rows_a(half, s), rows_b(half, s)):

                @pl.when(i != 0)
                def _(make=make):
                    make().wait_send()

        cross(s, 0).wait_send()
        cross(s, 1).wait_send()
        away(s).wait_send()
        return carry

    lax.fori_loop(0, NZ, drain, 0)
    for k in ca2 + cb2:
        k.wait_send()

    @pl.when(ex != z)
    def _():
        remote(done, xout, ks.at[0], kr.at[0], swap).wait()


def layer(ids, xin, w, wt, scale):
    dma = pltpu.SemaphoreType.DMA
    vm = pl.BlockSpec(memory_space=pltpu.VMEM)
    hd = DZ // 2
    cols = NXH * NZ * TOK
    block = (EXPERTS, SUB, FP)
    return pl.pallas_call(
        layer_kernel,
        out_shape=(
            jax.ShapeDtypeStruct((NXH, EXPERTS, SUB, FP), F32),
            jax.ShapeDtypeStruct((DZ, TOK), F32),
        ),
        in_specs=[pl.BlockSpec(memory_space=pltpu.SMEM), vm, vm, vm, vm],
        out_specs=(vm, vm),
        scratch_shapes=[
            pltpu.VMEM((NXH, NXL, NY, NZ, SUB, TOK), BF16),
            pltpu.VMEM((2, NZ - 1, SLOTS, F3, TOK), F32),
            pltpu.VMEM((2, SLOTS, F3, TOK), F32),
            pltpu.VMEM((NZ, NXH, SLOTS, FP, TOK), BF16),
            pltpu.VMEM((DZ, cols), BF16),
            pltpu.VMEM((SLOTS, DZ, cols), BF16),
            pltpu.VMEM((SLOTS, FP, cols), BF16),
            pltpu.VMEM((NXH, NXL, NY, DZ, TOK), F32),
            pltpu.VMEM((EXPERTS, NXH * NC, SUB, FP), F32),
            pltpu.VMEM((2,) + block, F32),
            pltpu.VMEM(block, BF16),
            pltpu.VMEM(block, BF16),
            pltpu.VMEM((3, NXH, NXL, hd, TOK), F32),
            pltpu.VMEM((3, hd, TOK), F32),
            pltpu.VMEM((3, NY, hd, TOK), F32),
            pltpu.VMEM((3, hd, TOK), F32),
            pltpu.VMEM((NXH, NXL, hd, TOK), F32),
            pltpu.VMEM((NY, hd, TOK), F32),
            pltpu.VMEM((DZ, TOK), F32),
            dma((1,)),
            dma((2, NZ, 3)),
            dma((2, NZ, 3)),
        ]
        + [dma((2, NZ - 1, SLOTS))] * 4
        + [dma((2, NZ)), dma((3, NXH, NXL)), dma((2, NZ)), dma((3, NY))]
        + [dma((3,))] * 4
        + [dma((2, EXPERTS))] * 2
        + [dma((EXPERTS,))] * 2
        + [dma((1,))] * 2,
        compiler_params=pltpu.CompilerParams(
            collective_id=1, has_side_effects=True, vmem_limit_bytes=VMEM_LIMIT
        ),
        name="layer",
    )(ids, xin, w, wt, scale)


def shards(
    activations, cotangent, expert_ids, slot_rows, slot_counts, route_probs, w_gate, w_up, w_down
):
    ex = lax.axis_index("expert")
    dp = lax.axis_index("dp")
    xl, y, xh = ex // NY, ex % NY, (dp // 2) % 2

    down_t = w_down.transpose(0, 2, 1)
    wsend = jnp.stack(
        [
            jnp.concatenate(
                [
                    w_gate[:, :, i * FH : (i + 1) * FH],
                    w_up[:, :, i * FH : (i + 1) * FH],
                    down_t[:, :, i * FH : (i + 1) * FH],
                    jnp.zeros((EXPERTS, SUB, FP - F3), BF16),
                ],
                axis=2,
            )
            for i in range(NXH)
        ]
    )

    source = jnp.where(xl == 0, activations, cotangent).reshape(TOK, NZ, NY, SUB)
    piece = lax.dynamic_index_in_dim(source, y, axis=2, keepdims=False).transpose(1, 2, 0)

    position = jnp.arange(TOK, dtype=jnp.int32)
    weight = jnp.where(position[None, :] < slot_counts[0][:, None], route_probs[0], 0.0)
    hit = slot_rows[0][:, :, None] == position[None, None, :]
    row_scale = jnp.sum(jnp.where(hit, weight[:, :, None], 0.0), axis=1)
    info = jnp.concatenate(
        [
            row_scale,
            jnp.broadcast_to(expert_ids[0].astype(F32)[:, None], (SLOTS, TOK)),
            jnp.zeros((4, TOK), F32),
        ]
    )

    xin, info_all, w_all, wt = exchange(piece, info, wsend)
    ids = info_all[:, :, 2:4, 0].astype(jnp.int32).reshape(-1)
    wout, xout = layer(ids, xin, w_all.reshape(EXPERTS, DZ, FP), wt, info_all)
    grad_gate = jnp.concatenate([wout[0, :, :, 0:FH], wout[1, :, :, 0:FH]], axis=2)
    grad_up = jnp.concatenate(
        [wout[0, :, :, FH : 2 * FH], wout[1, :, :, FH : 2 * FH]], axis=2
    )
    grad_down = jnp.concatenate(
        [wout[0, :, :, 2 * FH : F3], wout[1, :, :, 2 * FH : F3]], axis=2
    ).transpose(0, 2, 1)
    return xout.T, grad_gate, grad_up, grad_down


def solution(mesh):
    return jax.shard_map(
        shards,
        mesh=mesh,
        in_specs=(
            P("dp", None),
            P("dp", None),
            P("dp", None),
            P("dp", None, None),
            P("dp", None),
            P("dp", None, None),
            P(None, "dp", "expert"),
            P(None, "dp", "expert"),
            P(None, "expert", "dp"),
        ),
        out_specs=(
            P("dp", "expert"),
            P(None, "dp", "expert"),
            P(None, "dp", "expert"),
            P(None, "expert", "dp"),
        ),
        check_vma=False,
    )
```

```python
import jax
import jax.numpy as jnp
from jax import lax
from jax.experimental import pallas as pl
from jax.experimental.pallas import tpu as pltpu
from jax.sharding import PartitionSpec as P

MESH = pl.DeviceIdType.MESH
F32 = jnp.float32
BF16 = jnp.bfloat16

NZ, NXH, NC, NXL, NY = 8, 2, 2, 2, 4
SLOTS = 2
EXPERTS = 8
TOK = 128
SUB = 112
DZ = 448
FH = 152
F3 = 3 * FH
FP = 464
VMEM_LIMIT = 58 * 1024 * 1024


def place():
    ex = lax.axis_index("expert")
    dp = lax.axis_index("dp")
    return ex // NY, ex % NY, dp // 4, (dp // 2) % 2, dp % 2


def device(xl, y, z, xh, c):
    return (xl * NY + y, z * 4 + xh * 2 + c)


def remote(src, dst, ssem, rsem, dev):
    return pltpu.make_async_remote_copy(
        src_ref=src, dst_ref=dst, send_sem=ssem, recv_sem=rsem, device_id=dev, device_id_type=MESH
    )


def greet(devices):
    barrier = pltpu.get_barrier_semaphore()
    for dev in devices:
        pl.semaphore_signal(barrier, inc=1, device_id=dev, device_id_type=MESH)
    pl.semaphore_wait(barrier, len(devices))


def x_peers(xl, y, z, xh, c):
    pos = xh * 2 + xl
    out = []
    for step in range(1, 4):
        to = (pos + step) % 4
        out.append(device(to % 2, y, z, to // 2, c))
    return out


def y_peers(xl, y, z, xh, c):
    return [device(xl, (y + step) % NY, z, xh, c) for step in range(1, NY)]


def z_peers(xl, y, z, xh, c):
    return [device(xl, y, (z + step) % NZ, xh, c) for step in range(1, NZ)]


def exchange_kernel(
    piece, info, wsend, x_out, info_out, w_out, wt_out,
    zs, zr, is_, ir, ys, yr, ixs, ixr, fs, fr, os_, or_, ps, pr, loc,
):
    xl, y, z, xh, c = me = place()
    zp, yp = z_peers(*me), y_peers(*me)
    far = device(xl, y, z, 1 - xh, c)
    twin = device(xl, y, z, xh, 1 - c)
    greet(zp + yp + [far, twin])
    part = pl.ds(pl.multiple_of(y * SUB, SUB), SUB)
    mine = 2 * xh + c
    other = 2 * (1 - xh) + c

    wfar = []
    for e in range(EXPERTS):
        wfar.append(
            remote(wsend.at[1 - xh, e], w_out.at[e, mine], fs.at[e], fr.at[e], far)
        )
        wfar[-1].start()
    cz = []
    for i in range(NZ - 1):
        to = (z + i + 1) % NZ
        cz.append(remote(piece.at[to], x_out.at[z, part], zs.at[i], zr.at[i], zp[i]))
        cz[-1].start()
    ci = []
    for i in range(NZ - 1):
        ci.append(remote(info, info_out.at[xh, z], is_.at[i], ir.at[i], zp[i]))
        ci[-1].start()
    wown = []
    for e in range(EXPERTS):
        wown.append(
            remote(wsend.at[xh, e], w_out.at[e, mine], os_.at[e], or_.at[e], twin)
        )
        wown[-1].start()
    here = [
        pltpu.make_async_copy(piece.at[z], x_out.at[z, part], loc.at[0]),
        pltpu.make_async_copy(info, info_out.at[xh, z], loc.at[1]),
        pltpu.make_async_copy(wsend.at[xh], w_out.at[:, mine], loc.at[2]),
    ]
    for h in here:
        h.start()
    for h in here:
        h.wait()
    for k in cz:
        k.wait()
    cy = []
    for i in range(3):
        cy.append(remote(x_out.at[:, part], x_out.at[:, part], ys.at[i], yr.at[i], yp[i]))
        cy[-1].start()
    for k in ci:
        k.wait()
    cinf = remote(info_out.at[xh], info_out.at[xh], ixs.at[0], ixr.at[0], far)
    cinf.start()
    wpass = []
    for e in range(EXPERTS):
        wfar[e].wait_recv()
        wpass.append(
            remote(w_out.at[e, other], w_out.at[e, other], ps.at[e], pr.at[e], twin)
        )
        wpass[-1].start()
    for e in range(EXPERTS):
        wown[e].wait_recv()
        wpass[e].wait_recv()
        wt_out[e] = w_out[e].reshape(DZ, FP).T
    for k in cy:
        k.wait()
    cinf.wait()
    for k in wfar + wown + wpass:
        k.wait_send()


def exchange(piece, info, wsend):
    dma = pltpu.SemaphoreType.DMA
    vm = pl.BlockSpec(memory_space=pltpu.VMEM)
    return pl.pallas_call(
        exchange_kernel,
        out_shape=(
            jax.ShapeDtypeStruct((NZ, DZ, TOK), BF16),
            jax.ShapeDtypeStruct((NXH, NZ, 8, TOK), F32),
            jax.ShapeDtypeStruct((EXPERTS, NXH * NC, SUB, FP), BF16),
            jax.ShapeDtypeStruct((EXPERTS, FP, DZ), BF16),
        ),
        in_specs=[vm] * 3,
        out_specs=(vm,) * 4,
        scratch_shapes=[dma((7,))] * 4 + [dma((3,))] * 2 + [dma((1,))] * 2 + [dma((EXPERTS,))] * 6
        + [dma((3,))],
        compiler_params=pltpu.CompilerParams(
            collective_id=0, has_side_effects=True, vmem_limit_bytes=VMEM_LIMIT
        ),
        name="exchange_in",
    )(piece, info, wsend)


def layer_kernel(
    ids, xin, w, wt, scale, gate, up_out, down_out, xout,
    x, acc, own, dcat, hcat, dx, dw, wgot, wsnd, wfar, a1, a2, b1, b2, sa, sb, done, back,
    x_s, x_r, rs_s, rs_r, ag_s, ag_r,
    a1s, a1r, b1s, b1r, a2s, a2r, b2s, b2r, ts, tr, fs, fr, ks, kr,
):
    xl, y, z, xh, c = me = place()
    ex = xl * NY + y
    pos = xh * 2 + xl
    hd = DZ // 2
    xp, yp = x_peers(*me), y_peers(*me)
    up = device(xl, y, (z + 1) % NZ, xh, c)
    down = device(xl, y, (z + NZ - 1) % NZ, xh, c)
    to = (up, down)
    far = device(xl, y, z, 1 - xh, c)
    twin = device(xl, y, z, xh, 1 - c)
    swap = device(z // NY, z % NY, ex, xh, c)
    barrier = pltpu.get_barrier_semaphore()
    for dev in xp + yp + [up, down, twin]:
        pl.semaphore_signal(barrier, inc=1, device_id=dev, device_id_type=MESH)

    @pl.when(ex != z)
    def _():
        pl.semaphore_signal(barrier, inc=1, device_id=swap, device_id_type=MESH)

    pl.semaphore_wait(barrier, 9 + jnp.where(ex != z, 1, 0))

    def lanes(half, gz):
        return pl.ds(pl.multiple_of((half * NZ + gz) * TOK, TOK), TOK)

    def chunk(half, s):
        return jnp.where(half == 0, z + 2 * NZ - 1 - s, z + 1 + s) % NZ

    def spread(s, i):
        gz = chunk(xh, s)
        return remote(
            xin.at[gz], x.at[xl, :, lanes(xh, gz)], x_s.at[s, i], x_r.at[s, i], xp[i]
        )

    def spread_all(s):
        for i in range(3):
            spread(s, i).start()

    def await_all(s):
        gz = chunk(xh, s)
        x[xl, :, lanes(xh, gz)] = xin[gz]
        for i in range(3):
            spread(s, i).wait_recv()

    spread_all(0)
    spread_all(1)

    def partial(half, gz):
        at = lanes(half, gz)
        xt = x[0, :, at]
        dyt = x[1, :, at].astype(F32)
        for slot in range(SLOTS):
            e = ids[half * (NZ * SLOTS) + gz * SLOTS + slot]
            dys = (dyt * scale[half, gz, pl.ds(slot, 1), :]).astype(BF16)
            dcat[slot, :, at] = dys
            gu = jnp.dot(wt[e, 0 : 2 * FH, :], xt, preferred_element_type=F32)
            dh = jnp.dot(wt[e, 2 * FH : FP, :], dys, preferred_element_type=F32)
            own[half, slot, 0 : 2 * FH, :] = gu
            own[half, slot, 2 * FH : F3, :] = dh[:FH]

    def hop(half, slot, s, src):
        return remote(
            src, acc.at[half, s, slot], rs_s.at[half, s, slot], rs_r.at[half, s, slot], to[half]
        )

    await_all(0)
    for half in range(2):
        partial(half, chunk(half, 0))
        for slot in range(SLOTS):
            hop(half, slot, 0, own.at[half, slot]).start()
    for half in range(2):
        for slot in range(SLOTS):
            hop(half, slot, 0, own.at[half, slot]).wait_send()

    def ring(s, carry):
        spread_all(s + 1)
        await_all(s)
        for half in range(2):
            partial(half, chunk(half, s))
        for slot in range(SLOTS):
            for half in range(2):
                here = acc.at[half, s - 1, slot]
                hop(half, slot, s - 1, here).wait_recv()
                acc[half, s - 1, slot] = acc[half, s - 1, slot] + own[half, slot]
                hop(half, slot, s, here).start()
        return carry

    lax.fori_loop(1, NZ - 1, ring, 0)
    await_all(NZ - 1)

    def gather(half, slot, s, gz):
        ref = hcat.at[slot, :, lanes(half, gz)]
        return remote(ref, ref, ag_s.at[half, s, slot], ag_r.at[half, s, slot], to[half])

    def origin(half, s):
        return (z + NZ - s) % NZ if half == 0 else (z + s) % NZ

    def rows_a(half, gz):
        i = (gz % NY - y + NY) % NY
        src = dx.at[half, gz // NY, gz % NY, pl.ds(0, hd)]
        return i, lambda: remote(
            src, a1.at[i - 1, half, gz // NY], a1s.at[half, gz], a1r.at[i - 1, half, gz // NY],
            device(xl, gz % NY, z, xh, c),
        )

    def rows_b(half, gz):
        i = (half * 2 + gz // NY - pos + 4) % 4
        src = dx.at[half, gz // NY, gz % NY, pl.ds(hd, hd)]
        return i, lambda: remote(
            src, b1.at[i - 1, gz % NY], b1s.at[half, gz], b1r.at[i - 1, gz % NY],
            device(gz // NY, y, z, half, c),
        )

    def rows(half, gz):
        total = jnp.zeros((DZ, TOK), F32)
        for slot in range(SLOTS):
            e = ids[half * (NZ * SLOTS) + gz * SLOTS + slot]
            hs = hcat[slot, 0 : 2 * FH, lanes(half, gz)]
            total = total + jnp.dot(
                w[e, :, 0 : 2 * FH], hs, preferred_element_type=F32
            )
        dx[half, gz // NY, gz % NY] = total
        for i, make in (rows_a(half, gz), rows_b(half, gz)):

            @pl.when(i != 0)
            def _(make=make):
                make().start()

    for half in range(2):
        partial(half, z)
    for slot in range(SLOTS):
        for half in range(2):
            last = acc.at[half, NZ - 2, slot]
            hop(half, slot, NZ - 2, last).wait_recv()
            g = acc[half, NZ - 2, slot, 0:FH, :] + own[half, slot, 0:FH, :]
            u = acc[half, NZ - 2, slot, FH : 2 * FH, :] + own[half, slot, FH : 2 * FH, :]
            dh = acc[half, NZ - 2, slot, 2 * FH : F3, :] + own[half, slot, 2 * FH : F3, :]
            sig = 1.0 / (1.0 + jnp.exp(-g))
            act = g * sig
            dg = dh * u * sig * (1.0 + g * (1.0 - sig))
            du = dh * act
            hid = act * u
            hcat[slot, 0 : 2 * FH, lanes(half, z)] = jnp.concatenate([dg, du], axis=0).astype(BF16)
            hcat[slot, 2 * FH : FP, lanes(half, z)] = jnp.concatenate(
                [hid, jnp.zeros((FP - F3, TOK), F32)], axis=0
            ).astype(BF16)
            gather(half, slot, 0, z).start()
    for half in range(2):
        rows(half, z)

    def pass_on(s, carry):
        for slot in range(SLOTS):
            for half in range(2):
                gather(half, slot, s - 1, origin(half, s)).wait_recv()
                gather(half, slot, s, origin(half, s)).start()
        for half in range(2):
            rows(half, origin(half, s))
        return carry

    lax.fori_loop(1, NZ - 1, pass_on, 0)
    for half in range(2):
        for slot in range(SLOTS):
            gather(half, slot, NZ - 2, origin(half, NZ - 1)).wait_recv()
        rows(half, origin(half, NZ - 1))

    cols = NXH * NZ * TOK
    def expert_row(slot):
        return jnp.concatenate(
            [
                scale[i // NZ, i % NZ, 2 + slot : 3 + slot, :]
                for i in range(NXH * NZ)
            ],
            axis=1,
        )

    id0, id1 = expert_row(0), expert_row(1)
    nt = (((1,), (1,)), ((), ()))

    def weights(e):
        is0 = jnp.broadcast_to(id0 == e.astype(F32), (16, cols))
        is1 = jnp.broadcast_to(id1 == e.astype(F32), (16, cols))
        zero = jnp.zeros((16, cols), BF16)

        def pick(pair, n):
            return jnp.concatenate(
                [
                    jnp.where(
                        is0,
                        pair[0, r * 16 : (r + 1) * 16, :],
                        jnp.where(is1, pair[1, r * 16 : (r + 1) * 16, :], zero),
                    )
                    for r in range(n // 16)
                ],
                axis=0,
            )

        hs = pick(hcat, FP)
        ds = pick(dcat, DZ)
        gu = lax.dot_general(x[0], hs, nt, preferred_element_type=F32)
        dn = lax.dot_general(ds, hs[256:], nt, preferred_element_type=F32)
        column = lax.broadcasted_iota(jnp.int32, (DZ, FP - 256), 1)
        tail = jnp.where(column < 2 * FH - 256, gu[:, 256:], dn)
        for q in range(NXH * NC):
            dw[e, q, :, 0:256] = gu[q * SUB : (q + 1) * SUB, 0:256]
            dw[e, q, :, 256:FP] = tail[q * SUB : (q + 1) * SUB]

    def cross(e, i):
        blk = (1 - xh) if i == 0 else xh
        return remote(dw.at[e, 2 * blk + 1 - c], wgot.at[i, e], ts.at[i, e], tr.at[i, e], twin)

    def away(e):
        return remote(wsnd.at[e], wfar.at[e], fs.at[e], fr.at[e], far)

    def combine(e):
        cross(e, 0).wait_recv()
        wsnd[e] = (dw[e, 2 * (1 - xh) + c] + wgot[0, e]).astype(BF16)
        away(e).start()
        cross(e, 1).wait_recv()
        wgot[1, e] = dw[e, 2 * xh + c] + wgot[1, e]

    def second(i, kind):
        if kind == 0:
            t = (pos + i + 1) % 4
            return remote(sa.at[t // 2, t % 2], a2.at[i], a2s.at[i], a2r.at[i], xp[i])
        t = (y + i + 1) % NY
        return remote(sb.at[t], b2.at[i], b2s.at[i], b2r.at[i], yp[i])

    def rows_second():
        for i in range(3):
            for j in range(NXH):
                for k in range(NXL):
                    remote(
                        dx.at[0, 0, 0, pl.ds(0, hd)], a1.at[i, j, k], a1s.at[0, 0],
                        a1r.at[i, j, k], up,
                    ).wait_recv()
        for j in range(NXH):
            for k in range(NXL):
                sa[j, k] = dx[j, k, y, 0:hd] + a1[0, j, k] + a1[1, j, k] + a1[2, j, k]
        for i in range(3):
            second(i, 0).start()
        for i in range(3):
            for j in range(NY):
                remote(
                    dx.at[0, 0, 0, pl.ds(hd, hd)], b1.at[i, j], b1s.at[0, 0], b1r.at[i, j], up
                ).wait_recv()
        for j in range(NY):
            sb[j] = dx[xh, xl, j, hd:DZ] + b1[0, j] + b1[1, j] + b1[2, j]
        for i in range(3):
            second(i, 1).start()

    def rows_swap():
        for i in range(3):
            second(i, 0).wait_recv()
        done[0:hd] = sa[xh, xl] + a2[0] + a2[1] + a2[2]
        for i in range(3):
            second(i, 1).wait_recv()
        done[hd:DZ] = sb[y] + b2[0] + b2[1] + b2[2]

        @pl.when(ex != z)
        def _():
            remote(done, back, ks.at[0], kr.at[0], swap).start()

        @pl.when(ex == z)
        def _():
            back[...] = done[...]

    def finish(e):
        away(e).wait_recv()
        ours = wgot[1, e]
        theirs = wfar[e].astype(F32)
        low = jnp.where(xh == 0, ours, theirs)
        high = jnp.where(xh == 0, theirs, ours)
        gate[e] = jnp.concatenate([low[:, 0:FH], high[:, 0:FH]], axis=1)
        up_out[e] = jnp.concatenate([low[:, FH : 2 * FH], high[:, FH : 2 * FH]], axis=1)
        down_out[e] = jnp.concatenate([low[:, 2 * FH : F3].T, high[:, 2 * FH : F3].T], axis=0)

    def per_expert(e, carry):
        weights(e)
        cross(e, 0).start()
        cross(e, 1).start()

        @pl.when(e > 0)
        def _():
            combine(e - 1)

        @pl.when(e == 0)
        def _():
            rows_second()

        @pl.when(e == 3)
        def _():
            rows_swap()

        @pl.when(e > 4)
        def _():
            finish(e - 5)

        return carry

    lax.fori_loop(0, EXPERTS, per_expert, 0)
    combine(EXPERTS - 1)

    def finish_rest(e, carry):
        finish(e)
        return carry

    lax.fori_loop(EXPERTS - 5, EXPERTS, finish_rest, 0)

    def drain_ring(s, carry):
        for half in range(2):
            for slot in range(SLOTS):
                hop(half, slot, s, acc.at[half, s - 1, slot]).wait_send()
                gather(half, slot, s, origin(half, s)).wait_send()
        return carry

    lax.fori_loop(1, NZ - 1, drain_ring, 0)
    for half in range(2):
        for slot in range(SLOTS):
            gather(half, slot, 0, z).wait_send()

    def drain(s, carry):
        for i in range(3):
            spread(s, i).wait_send()
        for half in range(2):
            for i, make in (rows_a(half, s), rows_b(half, s)):

                @pl.when(i != 0)
                def _(make=make):
                    make().wait_send()

        cross(s, 0).wait_send()
        cross(s, 1).wait_send()
        away(s).wait_send()
        return carry

    lax.fori_loop(0, NZ, drain, 0)
    for i in range(3):
        second(i, 0).wait_send()
        second(i, 1).wait_send()

    @pl.when(ex != z)
    def _():
        remote(done, back, ks.at[0], kr.at[0], swap).wait()

    xout[...] = back[...].T


def layer(ids, xin, w, wt, scale):
    dma = pltpu.SemaphoreType.DMA
    vm = pl.BlockSpec(memory_space=pltpu.VMEM)
    hd = DZ // 2
    cols = NXH * NZ * TOK
    block = (EXPERTS, SUB, FP)
    return pl.pallas_call(
        layer_kernel,
        out_shape=(
            jax.ShapeDtypeStruct((EXPERTS, SUB, 2 * FH), F32),
            jax.ShapeDtypeStruct((EXPERTS, SUB, 2 * FH), F32),
            jax.ShapeDtypeStruct((EXPERTS, 2 * FH, SUB), F32),
            jax.ShapeDtypeStruct((TOK, DZ), F32),
        ),
        in_specs=[pl.BlockSpec(memory_space=pltpu.SMEM), vm, vm, vm, vm],
        out_specs=(vm,) * 4,
        scratch_shapes=[
            pltpu.VMEM((2, DZ, cols), BF16),
            pltpu.VMEM((2, NZ - 1, SLOTS, F3, TOK), F32),
            pltpu.VMEM((2, SLOTS, F3, TOK), F32),
            pltpu.VMEM((SLOTS, DZ, cols), BF16),
            pltpu.VMEM((SLOTS, FP, cols), BF16),
            pltpu.VMEM((NXH, NXL, NY, DZ, TOK), F32),
            pltpu.VMEM((EXPERTS, NXH * NC, SUB, FP), F32),
            pltpu.VMEM((2,) + block, F32),
            pltpu.VMEM(block, BF16),
            pltpu.VMEM(block, BF16),
            pltpu.VMEM((3, NXH, NXL, hd, TOK), F32),
            pltpu.VMEM((3, hd, TOK), F32),
            pltpu.VMEM((3, NY, hd, TOK), F32),
            pltpu.VMEM((3, hd, TOK), F32),
            pltpu.VMEM((NXH, NXL, hd, TOK), F32),
            pltpu.VMEM((NY, hd, TOK), F32),
            pltpu.VMEM((DZ, TOK), F32),
            pltpu.VMEM((DZ, TOK), F32),
            dma((NZ, 3)),
            dma((NZ, 3)),
        ]
        + [dma((2, NZ - 1, SLOTS))] * 4
        + [dma((2, NZ)), dma((3, NXH, NXL)), dma((2, NZ)), dma((3, NY))]
        + [dma((3,))] * 4
        + [dma((2, EXPERTS))] * 2
        + [dma((EXPERTS,))] * 2
        + [dma((1,))] * 2,
        compiler_params=pltpu.CompilerParams(
            collective_id=1, has_side_effects=True, vmem_limit_bytes=VMEM_LIMIT
        ),
        name="layer",
    )(ids, xin, w, wt, scale)


def shards(
    activations, cotangent, expert_ids, slot_rows, slot_counts, route_probs, w_gate, w_up, w_down
):
    ex = lax.axis_index("expert")
    dp = lax.axis_index("dp")
    xl, y, xh = ex // NY, ex % NY, (dp // 2) % 2

    down_t = w_down.transpose(0, 2, 1)
    wsend = jnp.stack(
        [
            jnp.concatenate(
                [
                    w_gate[:, :, i * FH : (i + 1) * FH],
                    w_up[:, :, i * FH : (i + 1) * FH],
                    down_t[:, :, i * FH : (i + 1) * FH],
                    jnp.zeros((EXPERTS, SUB, FP - F3), BF16),
                ],
                axis=2,
            )
            for i in range(NXH)
        ]
    )

    source = jnp.where(xl == 0, activations, cotangent).reshape(TOK, NZ, NY, SUB)
    piece = lax.dynamic_index_in_dim(source, y, axis=2, keepdims=False).transpose(1, 2, 0)

    position = jnp.arange(TOK, dtype=jnp.int32)
    weight = jnp.where(position[None, :] < slot_counts[0][:, None], route_probs[0], 0.0)
    hit = slot_rows[0][:, :, None] == position[None, None, :]
    row_scale = jnp.sum(jnp.where(hit, weight[:, :, None], 0.0), axis=1)
    info = jnp.concatenate(
        [
            row_scale,
            jnp.broadcast_to(expert_ids[0].astype(F32)[:, None], (SLOTS, TOK)),
            jnp.zeros((4, TOK), F32),
        ]
    )

    xin, info_all, w_all, wt = exchange(piece, info, wsend)
    ids = info_all[:, :, 2:4, 0].astype(jnp.int32).reshape(-1)
    grad_gate, grad_up, grad_down, rows = layer(
        ids, xin, w_all.reshape(EXPERTS, DZ, FP), wt, info_all
    )
    return rows, grad_gate, grad_up, grad_down


def solution(mesh):
    return jax.shard_map(
        shards,
        mesh=mesh,
        in_specs=(
            P("dp", None),
            P("dp", None),
            P("dp", None),
            P("dp", None, None),
            P("dp", None),
            P("dp", None, None),
            P(None, "dp", "expert"),
            P(None, "dp", "expert"),
            P(None, "expert", "dp"),
        ),
        out_specs=(
            P("dp", "expert"),
            P(None, "dp", "expert"),
            P(None, "dp", "expert"),
            P(None, "expert", "dp"),
        ),
        check_vma=False,
    )
```

```python
import jax
import jax.numpy as jnp
from jax import lax
from jax.experimental import pallas as pl
from jax.experimental.pallas import tpu as pltpu
from jax.sharding import PartitionSpec as P

MESH = pl.DeviceIdType.MESH
F32 = jnp.float32
BF16 = jnp.bfloat16

NZ, NXH, NC, NXL, NY = 8, 2, 2, 2, 4
SLOTS = 2
EXPERTS = 8
TOK = 128
SUB = 112
DZ = 448
FH = 152
F3 = 3 * FH
FP = 464
NB = 3
VMEM_LIMIT = 58 * 1024 * 1024


def place():
    ex = lax.axis_index("expert")
    dp = lax.axis_index("dp")
    return ex // NY, ex % NY, dp // 4, (dp // 2) % 2, dp % 2


def device(xl, y, z, xh, c):
    return (xl * NY + y, z * 4 + xh * 2 + c)


def remote(src, dst, ssem, rsem, dev):
    return pltpu.make_async_remote_copy(
        src_ref=src, dst_ref=dst, send_sem=ssem, recv_sem=rsem, device_id=dev, device_id_type=MESH
    )


def greet(devices):
    barrier = pltpu.get_barrier_semaphore()
    for dev in devices:
        pl.semaphore_signal(barrier, inc=1, device_id=dev, device_id_type=MESH)
    pl.semaphore_wait(barrier, len(devices))


def x_peers(xl, y, z, xh, c):
    pos = xh * 2 + xl
    out = []
    for step in range(1, 4):
        to = (pos + step) % 4
        out.append(device(to % 2, y, z, to // 2, c))
    return out


def y_peers(xl, y, z, xh, c):
    return [device(xl, (y + step) % NY, z, xh, c) for step in range(1, NY)]


def z_peers(xl, y, z, xh, c):
    return [device(xl, y, (z + step) % NZ, xh, c) for step in range(1, NZ)]


def exchange_kernel(
    piece, info, wsend, x_out, info_out, w_out, wt_out,
    zs, zr, is_, ir, ys, yr, ixs, ixr, fs, fr, os_, or_, ps, pr, loc,
):
    xl, y, z, xh, c = me = place()
    zp, yp = z_peers(*me), y_peers(*me)
    far = device(xl, y, z, 1 - xh, c)
    twin = device(xl, y, z, xh, 1 - c)
    greet(zp + yp + [far, twin])
    part = pl.ds(pl.multiple_of(y * SUB, SUB), SUB)
    mine = 2 * xh + c
    other = 2 * (1 - xh) + c

    wfar = []
    for e in range(EXPERTS):
        wfar.append(
            remote(wsend.at[1 - xh, e], w_out.at[e, mine], fs.at[e], fr.at[e], far)
        )
        wfar[-1].start()
    cz = []
    for i in range(NZ - 1):
        to = (z + i + 1) % NZ
        cz.append(remote(piece.at[to], x_out.at[z, part], zs.at[i], zr.at[i], zp[i]))
        cz[-1].start()
    ci = []
    for i in range(NZ - 1):
        ci.append(remote(info, info_out.at[xh, z], is_.at[i], ir.at[i], zp[i]))
        ci[-1].start()
    wown = []
    for e in range(EXPERTS):
        wown.append(
            remote(wsend.at[xh, e], w_out.at[e, mine], os_.at[e], or_.at[e], twin)
        )
        wown[-1].start()
    here = [
        pltpu.make_async_copy(piece.at[z], x_out.at[z, part], loc.at[0]),
        pltpu.make_async_copy(info, info_out.at[xh, z], loc.at[1]),
        pltpu.make_async_copy(wsend.at[xh], w_out.at[:, mine], loc.at[2]),
    ]
    for h in here:
        h.start()
    for h in here:
        h.wait()
    for k in cz:
        k.wait()
    cy = []
    for i in range(3):
        cy.append(remote(x_out.at[:, part], x_out.at[:, part], ys.at[i], yr.at[i], yp[i]))
        cy[-1].start()
    for k in ci:
        k.wait()
    cinf = remote(info_out.at[xh], info_out.at[xh], ixs.at[0], ixr.at[0], far)
    cinf.start()
    wpass = []
    for e in range(EXPERTS):
        wfar[e].wait_recv()
        wpass.append(
            remote(w_out.at[e, other], w_out.at[e, other], ps.at[e], pr.at[e], twin)
        )
        wpass[-1].start()
    for e in range(EXPERTS):
        wown[e].wait_recv()
        wpass[e].wait_recv()
        wt_out[e] = w_out[e].reshape(DZ, FP).T
    for k in cy:
        k.wait()
    cinf.wait()
    for k in wfar + wown + wpass:
        k.wait_send()


def exchange(piece, info, wsend):
    dma = pltpu.SemaphoreType.DMA
    vm = pl.BlockSpec(memory_space=pltpu.VMEM)
    return pl.pallas_call(
        exchange_kernel,
        out_shape=(
            jax.ShapeDtypeStruct((NZ, DZ, TOK), BF16),
            jax.ShapeDtypeStruct((NXH, NZ, 8, TOK), F32),
            jax.ShapeDtypeStruct((EXPERTS, NXH * NC, SUB, FP), BF16),
            jax.ShapeDtypeStruct((EXPERTS, FP, DZ), BF16),
        ),
        in_specs=[vm] * 3,
        out_specs=(vm,) * 4,
        scratch_shapes=[dma((7,))] * 4 + [dma((3,))] * 2 + [dma((1,))] * 2 + [dma((EXPERTS,))] * 6
        + [dma((3,))],
        compiler_params=pltpu.CompilerParams(
            collective_id=0, has_side_effects=True, vmem_limit_bytes=VMEM_LIMIT
        ),
        name="exchange_in",
    )(piece, info, wsend)


def layer_kernel(
    ids, xin, w, wt, scale, gate, up_out, down_out, xout,
    x, early, first, acc, turn, own, dcat, hcat, dx, dxs, dw, wgot, wsnd, wfar, a1, a2, b1, b2, sa, sb, done, mid, back,
    x_s, x_r, rs_s, rs_r, ag_s, ag_r,
    a1s, a1r, b1s, b1r, a2s, a2r, b2s, b2r, ts, tr, fs, fr, ks, kr,
):
    xl, y, z, xh, c = me = place()
    ex = xl * NY + y
    pos = xh * 2 + xl
    hd = DZ // 2
    xp, yp = x_peers(*me), y_peers(*me)
    up = device(xl, y, (z + 1) % NZ, xh, c)
    down = device(xl, y, (z + NZ - 1) % NZ, xh, c)
    to = (up, down)
    far = device(xl, y, z, 1 - xh, c)
    twin = device(xl, y, z, xh, 1 - c)
    pair = (ex + NZ - z) % NZ
    along = device(xl, y, pair, xh, c)
    across = device(pair // NY, pair % NY, z, xh, c)
    before = (ex + z) % NZ
    source = device(before // NY, before % NY, z, xh, c)
    barrier = pltpu.get_barrier_semaphore()
    for dev in xp + yp + [up, down, twin]:
        pl.semaphore_signal(barrier, inc=1, device_id=dev, device_id_type=MESH)

    @pl.when(pair != z)
    def _():
        pl.semaphore_signal(barrier, inc=1, device_id=along, device_id_type=MESH)

    @pl.when(z != 0)
    def _():
        pl.semaphore_signal(barrier, inc=1, device_id=across, device_id_type=MESH)
        pl.semaphore_signal(barrier, inc=1, device_id=source, device_id_type=MESH)

    pl.semaphore_wait(barrier, 9 + jnp.where(pair != z, 1, 0) + jnp.where(z != 0, 2, 0))

    def lanes(half, gz):
        return pl.ds(pl.multiple_of((half * NZ + gz) * TOK, TOK), TOK)

    def chunk(half, s):
        return jnp.where(half == 0, z + 2 * NZ - 1 - s, z + 1 + s) % NZ

    def spread(s, i):
        gz = chunk(xh, s)
        return remote(
            xin.at[gz], x.at[xl, :, lanes(xh, gz)], x_s.at[s, i], x_r.at[s, i], xp[i]
        )

    def spread_all(s):
        for i in range(3):
            spread(s, i).start()

    def await_all(s):
        gz = chunk(xh, s)
        x[xl, :, lanes(xh, gz)] = xin[gz]
        for i in range(3):
            spread(s, i).wait_recv()

    spread_all(0)
    spread_all(1)

    def partial(half, gz):
        at = lanes(half, gz)
        xt = x[0, :, at]
        dyt = x[1, :, at].astype(F32)
        for slot in range(SLOTS):
            e = ids[half * (NZ * SLOTS) + gz * SLOTS + slot]
            dys = (dyt * scale[half, gz, pl.ds(slot, 1), :]).astype(BF16)
            dcat[slot, :, at] = dys
            gu = jnp.dot(wt[e, 0 : 2 * FH, :], xt, preferred_element_type=F32)
            dh = jnp.dot(wt[e, 2 * FH : FP, :], dys, preferred_element_type=F32)
            own[half, slot, 0 : 2 * FH, :] = gu
            own[half, slot, 2 * FH : FP, :] = dh

    def hop(half, slot, s, src, dst):
        return remote(src, dst, rs_s.at[half, s, slot], rs_r.at[half, s, slot], to[half])

    def hop16(half, slot, s, src):
        return hop(half, slot, s, src, early.at[half, s, slot])

    def hop32(half, slot, s, src):
        return hop(half, slot, s, src, acc.at[half, s - NB, slot])

    await_all(0)
    for half in range(2):
        partial(half, chunk(half, 0))
        for slot in range(SLOTS):
            first[half, slot] = own[half, slot].astype(BF16)
            hop16(half, slot, 0, first.at[half, slot]).start()

    def fresh(s):
        spread_all(s + 1)
        await_all(s)
        for half in range(2):
            partial(half, chunk(half, s))

    def ring16(s, carry):
        fresh(s)
        for slot in range(SLOTS):
            for half in range(2):
                here = early.at[half, s - 1, slot]
                hop16(half, slot, s - 1, here).wait_recv()
                total = early[half, s - 1, slot].astype(F32) + own[half, slot]
                early[half, s - 1, slot] = total.astype(BF16)
                hop16(half, slot, s, here).start()
        return carry

    lax.fori_loop(1, NB, ring16, 0)
    fresh(NB)
    for slot in range(SLOTS):
        for half in range(2):
            here = early.at[half, NB - 1, slot]
            hop16(half, slot, NB - 1, here).wait_recv()
            turn[half, slot] = early[half, NB - 1, slot, 0:F3].astype(F32) + own[half, slot, 0:F3]
            hop32(half, slot, NB, turn.at[half, slot]).start()

    def ring32(s, carry):
        fresh(s)
        for slot in range(SLOTS):
            for half in range(2):
                here = acc.at[half, s - 1 - NB, slot]
                hop32(half, slot, s - 1, here).wait_recv()
                acc[half, s - 1 - NB, slot] = acc[half, s - 1 - NB, slot] + own[half, slot, 0:F3]
                hop32(half, slot, s, here).start()
        return carry

    lax.fori_loop(NB + 1, NZ - 1, ring32, 0)
    await_all(NZ - 1)

    def gather(half, slot, s, gz):
        ref = hcat.at[slot, :, lanes(half, gz)]
        return remote(ref, ref, ag_s.at[half, s, slot], ag_r.at[half, s, slot], to[half])

    def origin(half, s):
        return (z + NZ - s) % NZ if half == 0 else (z + s) % NZ

    def spot(gz):
        return (gz + z) % NZ

    def rows_a(half, gz):
        q = spot(gz)
        i = (q % NY - y + NY) % NY
        src = dxs.at[half, q // NY, q % NY, pl.ds(0, hd)]
        return i, lambda: remote(
            src, a1.at[i - 1, half, q // NY], a1s.at[half, gz], a1r.at[i - 1, half, q // NY],
            device(xl, q % NY, z, xh, c),
        )

    def rows_b(half, gz):
        q = spot(gz)
        i = (half * 2 + q // NY - pos + 4) % 4
        src = dxs.at[half, q // NY, q % NY, pl.ds(hd, hd)]
        return i, lambda: remote(
            src, b1.at[i - 1, q % NY], b1s.at[half, gz], b1r.at[i - 1, q % NY],
            device(q // NY, y, z, half, c),
        )

    def rows(half, gz):
        total = jnp.zeros((DZ, TOK), F32)
        for slot in range(SLOTS):
            e = ids[half * (NZ * SLOTS) + gz * SLOTS + slot]
            hs = hcat[slot, 0 : 2 * FH, lanes(half, gz)]
            total = total + jnp.dot(
                w[e, :, 0 : 2 * FH], hs, preferred_element_type=F32
            )
        q = spot(gz)
        dx[half, q // NY, q % NY] = total
        dxs[half, q // NY, q % NY] = total.astype(BF16)
        for i, make in (rows_a(half, gz), rows_b(half, gz)):

            @pl.when(i != 0)
            def _(make=make):
                make().start()

    for half in range(2):
        partial(half, z)
    for slot in range(SLOTS):
        for half in range(2):
            last = acc.at[half, NZ - 2 - NB, slot]
            hop32(half, slot, NZ - 2, last).wait_recv()
            g = acc[half, NZ - 2 - NB, slot, 0:FH, :] + own[half, slot, 0:FH, :]
            u = acc[half, NZ - 2 - NB, slot, FH : 2 * FH, :] + own[half, slot, FH : 2 * FH, :]
            dh = acc[half, NZ - 2 - NB, slot, 2 * FH : F3, :] + own[half, slot, 2 * FH : F3, :]
            sig = 1.0 / (1.0 + jnp.exp(-g))
            act = g * sig
            dg = dh * u * sig * (1.0 + g * (1.0 - sig))
            du = dh * act
            hid = act * u
            hcat[slot, 0 : 2 * FH, lanes(half, z)] = jnp.concatenate([dg, du], axis=0).astype(BF16)
            hcat[slot, 2 * FH : FP, lanes(half, z)] = jnp.concatenate(
                [hid, jnp.zeros((FP - F3, TOK), F32)], axis=0
            ).astype(BF16)
            gather(half, slot, 0, z).start()
    for half in range(2):
        rows(half, z)

    def pass_on(s, carry):
        for slot in range(SLOTS):
            for half in range(2):
                gather(half, slot, s - 1, origin(half, s)).wait_recv()
                gather(half, slot, s, origin(half, s)).start()
        for half in range(2):
            rows(half, origin(half, s))
        return carry

    lax.fori_loop(1, NZ - 1, pass_on, 0)
    for half in range(2):
        for slot in range(SLOTS):
            gather(half, slot, NZ - 2, origin(half, NZ - 1)).wait_recv()
        rows(half, origin(half, NZ - 1))

    cols = NXH * NZ * TOK
    def expert_row(slot):
        return jnp.concatenate(
            [
                scale[i // NZ, i % NZ, 2 + slot : 3 + slot, :]
                for i in range(NXH * NZ)
            ],
            axis=1,
        )

    id0, id1 = expert_row(0), expert_row(1)
    nt = (((1,), (1,)), ((), ()))

    def weights(e):
        is0 = jnp.broadcast_to(id0 == e.astype(F32), (16, cols))
        is1 = jnp.broadcast_to(id1 == e.astype(F32), (16, cols))
        zero = jnp.zeros((16, cols), BF16)

        def pick(pair, n):
            return jnp.concatenate(
                [
                    jnp.where(
                        is0,
                        pair[0, r * 16 : (r + 1) * 16, :],
                        jnp.where(is1, pair[1, r * 16 : (r + 1) * 16, :], zero),
                    )
                    for r in range(n // 16)
                ],
                axis=0,
            )

        hs = pick(hcat, FP)
        ds = pick(dcat, DZ)
        gu = lax.dot_general(x[0], hs, nt, preferred_element_type=F32)
        dn = lax.dot_general(ds, hs[256:], nt, preferred_element_type=F32)
        column = lax.broadcasted_iota(jnp.int32, (DZ, FP - 256), 1)
        tail = jnp.where(column < 2 * FH - 256, gu[:, 256:], dn)
        for q in range(NXH * NC):
            dw[e, q, :, 0:256] = gu[q * SUB : (q + 1) * SUB, 0:256]
            dw[e, q, :, 256:FP] = tail[q * SUB : (q + 1) * SUB]

    def cross(e, i):
        blk = (1 - xh) if i == 0 else xh
        return remote(dw.at[e, 2 * blk + 1 - c], wgot.at[i, e], ts.at[i, e], tr.at[i, e], twin)

    def away(e):
        return remote(wsnd.at[e], wfar.at[e], fs.at[e], fr.at[e], far)

    def combine(e):
        cross(e, 0).wait_recv()
        wsnd[e] = (dw[e, 2 * (1 - xh) + c] + wgot[0, e]).astype(BF16)
        away(e).start()
        cross(e, 1).wait_recv()
        wgot[1, e] = dw[e, 2 * xh + c] + wgot[1, e]

    def second(i, kind):
        if kind == 0:
            t = (pos + i + 1) % 4
            return remote(sa.at[t // 2, t % 2], a2.at[i], a2s.at[i], a2r.at[i], xp[i])
        t = (y + i + 1) % NY
        return remote(sb.at[t], b2.at[i], b2s.at[i], b2r.at[i], yp[i])

    def rows_second():
        for i in range(3):
            for j in range(NXH):
                for k in range(NXL):
                    remote(
                        dxs.at[0, 0, 0, pl.ds(0, hd)], a1.at[i, j, k], a1s.at[0, 0],
                        a1r.at[i, j, k], up,
                    ).wait_recv()
        for j in range(NXH):
            for k in range(NXL):
                sa[j, k] = dx[j, k, y, 0:hd] + (
                    a1[0, j, k].astype(F32) + a1[1, j, k].astype(F32) + a1[2, j, k].astype(F32)
                )
        for i in range(3):
            second(i, 0).start()
        for i in range(3):
            for j in range(NY):
                remote(
                    dxs.at[0, 0, 0, pl.ds(hd, hd)], b1.at[i, j], b1s.at[0, 0], b1r.at[i, j], up
                ).wait_recv()
        for j in range(NY):
            sb[j] = dx[xh, xl, j, hd:DZ] + (
                b1[0, j].astype(F32) + b1[1, j].astype(F32) + b1[2, j].astype(F32)
            )
        for i in range(3):
            second(i, 1).start()

    def rows_swap():
        for i in range(3):
            second(i, 0).wait_recv()
        done[0:hd] = sa[xh, xl] + a2[0] + a2[1] + a2[2]
        for i in range(3):
            second(i, 1).wait_recv()
        done[hd:DZ] = sb[y] + b2[0] + b2[1] + b2[2]

        @pl.when(pair != z)
        def _():
            first_step().start()

    def first_step():
        return remote(done, mid, ks.at[0], kr.at[0], along)

    def second_step():
        return remote(mid, back, ks.at[1], kr.at[1], across)

    def rows_turn():
        @pl.when(pair != z)
        def _():
            first_step().wait_recv()

        @pl.when(pair == z)
        def _():
            mid[...] = done[...]

        @pl.when(z != 0)
        def _():
            second_step().start()

        @pl.when(z == 0)
        def _():
            back[...] = mid[...]

    def finish(e):
        away(e).wait_recv()
        ours = wgot[1, e]
        theirs = wfar[e].astype(F32)
        low = jnp.where(xh == 0, ours, theirs)
        high = jnp.where(xh == 0, theirs, ours)
        gate[e] = jnp.concatenate([low[:, 0:FH], high[:, 0:FH]], axis=1)
        up_out[e] = jnp.concatenate([low[:, FH : 2 * FH], high[:, FH : 2 * FH]], axis=1)
        down_out[e] = jnp.concatenate([low[:, 2 * FH : F3].T, high[:, 2 * FH : F3].T], axis=0)

    def per_expert(e, carry):
        weights(e)
        cross(e, 0).start()
        cross(e, 1).start()

        @pl.when(e > 0)
        def _():
            combine(e - 1)

        @pl.when(e == 0)
        def _():
            rows_second()

        @pl.when(e == 2)
        def _():
            rows_swap()

        @pl.when(e == 5)
        def _():
            rows_turn()

        @pl.when(e > 4)
        def _():
            finish(e - 5)

        return carry

    lax.fori_loop(0, EXPERTS, per_expert, 0)
    combine(EXPERTS - 1)

    def finish_rest(e, carry):
        finish(e)
        return carry

    lax.fori_loop(EXPERTS - 5, EXPERTS, finish_rest, 0)

    def drain_ring(s, carry):
        for half in range(2):
            for slot in range(SLOTS):
                gather(half, slot, s, origin(half, s)).wait_send()
        return carry

    for half in range(2):
        for slot in range(SLOTS):
            hop16(half, slot, 0, first.at[half, slot]).wait_send()
            for s in range(1, NB):
                hop16(half, slot, s, early.at[half, s - 1, slot]).wait_send()
            hop32(half, slot, NB, turn.at[half, slot]).wait_send()
            for s in range(NB + 1, NZ - 1):
                hop32(half, slot, s, acc.at[half, s - 1 - NB, slot]).wait_send()
    lax.fori_loop(1, NZ - 1, drain_ring, 0)
    for half in range(2):
        for slot in range(SLOTS):
            gather(half, slot, 0, z).wait_send()

    def drain(s, carry):
        for i in range(3):
            spread(s, i).wait_send()
        for half in range(2):
            for i, make in (rows_a(half, s), rows_b(half, s)):

                @pl.when(i != 0)
                def _(make=make):
                    make().wait_send()

        cross(s, 0).wait_send()
        cross(s, 1).wait_send()
        away(s).wait_send()
        return carry

    lax.fori_loop(0, NZ, drain, 0)
    for i in range(3):
        second(i, 0).wait_send()
        second(i, 1).wait_send()

    @pl.when(pair != z)
    def _():
        first_step().wait_send()

    @pl.when(z != 0)
    def _():
        second_step().wait()

    xout[...] = back[...].T


def layer(ids, xin, w, wt, scale):
    dma = pltpu.SemaphoreType.DMA
    vm = pl.BlockSpec(memory_space=pltpu.VMEM)
    hd = DZ // 2
    cols = NXH * NZ * TOK
    block = (EXPERTS, SUB, FP)
    return pl.pallas_call(
        layer_kernel,
        out_shape=(
            jax.ShapeDtypeStruct((EXPERTS, SUB, 2 * FH), F32),
            jax.ShapeDtypeStruct((EXPERTS, SUB, 2 * FH), F32),
            jax.ShapeDtypeStruct((EXPERTS, 2 * FH, SUB), F32),
            jax.ShapeDtypeStruct((TOK, DZ), F32),
        ),
        in_specs=[pl.BlockSpec(memory_space=pltpu.SMEM), vm, vm, vm, vm],
        out_specs=(vm,) * 4,
        scratch_shapes=[
            pltpu.VMEM((2, DZ, cols), BF16),
            pltpu.VMEM((2, NB, SLOTS, FP, TOK), BF16),
            pltpu.VMEM((2, SLOTS, FP, TOK), BF16),
            pltpu.VMEM((2, NZ - 1 - NB, SLOTS, F3, TOK), F32),
            pltpu.VMEM((2, SLOTS, F3, TOK), F32),
            pltpu.VMEM((2, SLOTS, FP, TOK), F32),
            pltpu.VMEM((SLOTS, DZ, cols), BF16),
            pltpu.VMEM((SLOTS, FP, cols), BF16),
            pltpu.VMEM((NXH, NXL, NY, DZ, TOK), F32),
            pltpu.VMEM((NXH, NXL, NY, DZ, TOK), BF16),
            pltpu.VMEM((EXPERTS, NXH * NC, SUB, FP), F32),
            pltpu.VMEM((2,) + block, F32),
            pltpu.VMEM(block, BF16),
            pltpu.VMEM(block, BF16),
            pltpu.VMEM((3, NXH, NXL, hd, TOK), BF16),
            pltpu.VMEM((3, hd, TOK), F32),
            pltpu.VMEM((3, NY, hd, TOK), BF16),
            pltpu.VMEM((3, hd, TOK), F32),
            pltpu.VMEM((NXH, NXL, hd, TOK), F32),
            pltpu.VMEM((NY, hd, TOK), F32),
            pltpu.VMEM((DZ, TOK), F32),
            pltpu.VMEM((DZ, TOK), F32),
            pltpu.VMEM((DZ, TOK), F32),
            dma((NZ, 3)),
            dma((NZ, 3)),
        ]
        + [dma((2, NZ - 1, SLOTS))] * 4
        + [dma((2, NZ)), dma((3, NXH, NXL)), dma((2, NZ)), dma((3, NY))]
        + [dma((3,))] * 4
        + [dma((2, EXPERTS))] * 2
        + [dma((EXPERTS,))] * 2
        + [dma((2,))] * 2,
        compiler_params=pltpu.CompilerParams(
            collective_id=1, has_side_effects=True, vmem_limit_bytes=VMEM_LIMIT
        ),
        name="layer",
    )(ids, xin, w, wt, scale)


def shards(
    activations, cotangent, expert_ids, slot_rows, slot_counts, route_probs, w_gate, w_up, w_down
):
    ex = lax.axis_index("expert")
    dp = lax.axis_index("dp")
    xl, y, xh = ex // NY, ex % NY, (dp // 2) % 2

    down_t = w_down.transpose(0, 2, 1)
    wsend = jnp.stack(
        [
            jnp.concatenate(
                [
                    w_gate[:, :, i * FH : (i + 1) * FH],
                    w_up[:, :, i * FH : (i + 1) * FH],
                    down_t[:, :, i * FH : (i + 1) * FH],
                    jnp.zeros((EXPERTS, SUB, FP - F3), BF16),
                ],
                axis=2,
            )
            for i in range(NXH)
        ]
    )

    source = jnp.where(xl == 0, activations, cotangent).reshape(TOK, NZ, NY, SUB)
    piece = lax.dynamic_index_in_dim(source, y, axis=2, keepdims=False).transpose(1, 2, 0)

    position = jnp.arange(TOK, dtype=jnp.int32)
    weight = jnp.where(position[None, :] < slot_counts[0][:, None], route_probs[0], 0.0)
    hit = slot_rows[0][:, :, None] == position[None, None, :]
    row_scale = jnp.sum(jnp.where(hit, weight[:, :, None], 0.0), axis=1)
    info = jnp.concatenate(
        [
            row_scale,
            jnp.broadcast_to(expert_ids[0].astype(F32)[:, None], (SLOTS, TOK)),
            jnp.zeros((4, TOK), F32),
        ]
    )

    xin, info_all, w_all, wt = exchange(piece, info, wsend)
    ids = info_all[:, :, 2:4, 0].astype(jnp.int32).reshape(-1)
    grad_gate, grad_up, grad_down, rows = layer(
        ids, xin, w_all.reshape(EXPERTS, DZ, FP), wt, info_all
    )
    return rows, grad_gate, grad_up, grad_down


def solution(mesh):
    return jax.shard_map(
        shards,
        mesh=mesh,
        in_specs=(
            P("dp", None),
            P("dp", None),
            P("dp", None),
            P("dp", None, None),
            P("dp", None),
            P("dp", None, None),
            P(None, "dp", "expert"),
            P(None, "dp", "expert"),
            P(None, "expert", "dp"),
        ),
        out_specs=(
            P("dp", "expert"),
            P(None, "dp", "expert"),
            P(None, "dp", "expert"),
            P(None, "expert", "dp"),
        ),
        check_vma=False,
    )
```

```python
import jax
import jax.numpy as jnp
from jax import lax
from jax.experimental import pallas as pl
from jax.experimental.pallas import tpu as pltpu
from jax.sharding import PartitionSpec as P

MESH = pl.DeviceIdType.MESH
F32 = jnp.float32
BF16 = jnp.bfloat16

NZ, NXH, NC, NXL, NY = 8, 2, 2, 2, 4
SLOTS = 2
EXPERTS = 8
TOK = 128
SUB = 112
DZ = 448
FH = 152
F3 = 3 * FH
FP = 464
NB = 3
SWAP_AT = 7
TURN_AT = 4
VMEM_LIMIT = 58 * 1024 * 1024


def place():
    ex = lax.axis_index("expert")
    dp = lax.axis_index("dp")
    return ex // NY, ex % NY, dp // 4, (dp // 2) % 2, dp % 2


def device(xl, y, z, xh, c):
    return (xl * NY + y, z * 4 + xh * 2 + c)


def remote(src, dst, ssem, rsem, dev):
    return pltpu.make_async_remote_copy(
        src_ref=src, dst_ref=dst, send_sem=ssem, recv_sem=rsem, device_id=dev, device_id_type=MESH
    )


def greet(devices):
    barrier = pltpu.get_barrier_semaphore()
    for dev in devices:
        pl.semaphore_signal(barrier, inc=1, device_id=dev, device_id_type=MESH)
    pl.semaphore_wait(barrier, len(devices))


def x_peers(xl, y, z, xh, c):
    pos = xh * 2 + xl
    out = []
    for step in range(1, 4):
        to = (pos + step) % 4
        out.append(device(to % 2, y, z, to // 2, c))
    return out


def y_peers(xl, y, z, xh, c):
    return [device(xl, (y + step) % NY, z, xh, c) for step in range(1, NY)]


def z_peers(xl, y, z, xh, c):
    return [device(xl, y, (z + step) % NZ, xh, c) for step in range(1, NZ)]


def exchange_kernel(
    act, cot, rows, counts, probs, ids, wg, wu, wd, x_out, info_out, w_all, wt_out,
    xt, stack, info, wsrc,
    zs, zr, is_, ir, ys, yr, ixs, ixr, fs, fr, os_, or_, ps, pr, loc,
):
    xl, y, z, xh, c = me = place()
    zp, yp = z_peers(*me), y_peers(*me)
    far = device(xl, y, z, 1 - xh, c)
    twin = device(xl, y, z, xh, 1 - c)
    part = pl.ds(pl.multiple_of(y * SUB, SUB), SUB)
    mine = 2 * xh + c
    other = 2 * (1 - xh) + c
    barrier = pltpu.get_barrier_semaphore()
    peers = zp + yp + [far, twin]
    for dev in peers:
        pl.semaphore_signal(barrier, inc=1, device_id=dev, device_id_type=MESH)

    def pack(e, carry):
        g = wg[e].astype(F32)
        u = wu[e].astype(F32)
        d = wd[e].astype(F32).T
        both = []
        for i in range(NXH):
            pieces = [v[:, i * FH : (i + 1) * FH] for v in (g, u, d)]
            pieces.append(jnp.zeros((SUB, FP - F3), F32))
            both.append(jnp.concatenate(pieces, axis=1))
        wsrc[e] = jnp.where(xh == 0, both[1], both[0]).astype(BF16)
        w_all[e, mine] = jnp.where(xh == 0, both[0], both[1]).astype(BF16)
        return carry

    lax.fori_loop(0, EXPERTS, pack, 0)
    pl.semaphore_wait(barrier, len(peers))

    wfar = []
    for e in range(EXPERTS):
        wfar.append(remote(wsrc.at[e], w_all.at[e, mine], fs.at[e], fr.at[e], far))
        wfar[-1].start()
    wown = []
    for e in range(EXPERTS):
        wown.append(remote(w_all.at[e, mine], w_all.at[e, mine], os_.at[e], or_.at[e], twin))
        wown[-1].start()

    def turn_rows(j, carry):
        cols = pl.ds(pl.multiple_of(j * TOK, TOK), TOK)
        xt[cols, :] = jnp.where(xl == 0, act[:, cols], cot[:, cols]).T
        return carry

    lax.fori_loop(0, NZ * DZ // TOK, turn_rows, 0)

    def piece(gz):
        return xt.at[pl.ds(pl.multiple_of(gz * DZ + y * SUB, 16), SUB)]

    cz = []
    for i in range(NZ - 1):
        to = (z + i + 1) % NZ
        cz.append(remote(piece(to), x_out.at[z, part], zs.at[i], zr.at[i], zp[i]))
        cz[-1].start()

    lane = lax.broadcasted_iota(jnp.int32, (1, TOK), 1)
    column = lax.broadcasted_iota(jnp.int32, (TOK, TOK), 1).astype(F32)
    for slot in range(SLOTS):
        stack[slot : slot + 1, :] = rows[slot : slot + 1, :].astype(F32)
        stack[2 + slot : 3 + slot, :] = jnp.where(
            lane < counts[0, slot], probs[slot : slot + 1, :], 0.0
        )
    stack[4:8, :] = jnp.zeros((4, TOK), F32)
    turned = stack[...].T
    info[4:8, :] = jnp.zeros((4, TOK), F32)
    for slot in range(SLOTS):
        hit = turned[:, slot : slot + 1] == column
        info[slot : slot + 1, :] = jnp.sum(
            jnp.where(hit, turned[:, 2 + slot : 3 + slot], 0.0), axis=0, keepdims=True
        )
        info[2 + slot : 3 + slot, :] = jnp.full((1, TOK), ids[0, slot], jnp.int32).astype(F32)
    ci = []
    for i in range(NZ - 1):
        ci.append(remote(info, info_out.at[xh, z], is_.at[i], ir.at[i], zp[i]))
        ci[-1].start()
    here = [
        pltpu.make_async_copy(piece(z), x_out.at[z, part], loc.at[0]),
        pltpu.make_async_copy(info, info_out.at[xh, z], loc.at[1]),
    ]
    for h in here:
        h.start()
    for h in here:
        h.wait()
    for k in cz:
        k.wait()
    cy = []
    for i in range(3):
        cy.append(remote(x_out.at[:, part], x_out.at[:, part], ys.at[i], yr.at[i], yp[i]))
        cy[-1].start()
    for k in ci:
        k.wait()
    cinf = remote(info_out.at[xh], info_out.at[xh], ixs.at[0], ixr.at[0], far)
    cinf.start()
    wpass = []
    for e in range(EXPERTS):
        wfar[e].wait_recv()
        wpass.append(
            remote(w_all.at[e, other], w_all.at[e, other], ps.at[e], pr.at[e], twin)
        )
        wpass[-1].start()
    for e in range(EXPERTS):
        wown[e].wait_recv()
        wpass[e].wait_recv()
        wt_out[e] = w_all[e].reshape(DZ, FP).T
    for k in cy:
        k.wait()
    cinf.wait()
    for k in wfar + wown + wpass:
        k.wait_send()


def exchange(act, cot, rows, counts, probs, ids, wg, wu, wd):
    dma = pltpu.SemaphoreType.DMA
    vm = pl.BlockSpec(memory_space=pltpu.VMEM)
    sm = pl.BlockSpec(memory_space=pltpu.SMEM)
    return pl.pallas_call(
        exchange_kernel,
        out_shape=(
            jax.ShapeDtypeStruct((NZ, DZ, TOK), BF16),
            jax.ShapeDtypeStruct((NXH, NZ, 8, TOK), F32),
            jax.ShapeDtypeStruct((EXPERTS, NXH * NC, SUB, FP), BF16),
            jax.ShapeDtypeStruct((EXPERTS, FP, DZ), BF16),
        ),
        in_specs=[vm, vm, vm, sm, vm, sm, vm, vm, vm],
        out_specs=(vm,) * 4,
        scratch_shapes=[
            pltpu.VMEM((NZ * DZ, TOK), BF16),
            pltpu.VMEM((8, TOK), F32),
            pltpu.VMEM((8, TOK), F32),
            pltpu.VMEM((EXPERTS, SUB, FP), BF16),
        ]
        + [dma((7,))] * 4 + [dma((3,))] * 2 + [dma((1,))] * 2 + [dma((EXPERTS,))] * 6
        + [dma((2,))],
        compiler_params=pltpu.CompilerParams(
            collective_id=0, has_side_effects=True, vmem_limit_bytes=VMEM_LIMIT
        ),
        name="exchange_in",
    )(act, cot, rows, counts, probs, ids, wg, wu, wd)


def layer_kernel(
    ids, xin, w, wt, scale, gate, up_out, down_out, xout,
    x, early, first, acc, turn, own, dcat, hcat, dx, dxs, dw, wgot, wsnd, wfar, a1, a2, b1, b2, sa, sb, done, mid, back,
    x_s, x_r, rs_s, rs_r, ag_s, ag_r,
    a1s, a1r, b1s, b1r, a2s, a2r, b2s, b2r, ts, tr, fs, fr, ks, kr,
):
    xl, y, z, xh, c = me = place()
    ex = xl * NY + y
    pos = xh * 2 + xl
    hd = DZ // 2
    xp, yp = x_peers(*me), y_peers(*me)
    up = device(xl, y, (z + 1) % NZ, xh, c)
    down = device(xl, y, (z + NZ - 1) % NZ, xh, c)
    to = (up, down)
    far = device(xl, y, z, 1 - xh, c)
    twin = device(xl, y, z, xh, 1 - c)
    pair = (ex + NZ - z) % NZ
    along = device(xl, y, pair, xh, c)
    across = device(pair // NY, pair % NY, z, xh, c)
    before = (ex + z) % NZ
    source = device(before // NY, before % NY, z, xh, c)
    barrier = pltpu.get_barrier_semaphore()
    for dev in xp + yp + [up, down, twin]:
        pl.semaphore_signal(barrier, inc=1, device_id=dev, device_id_type=MESH)

    @pl.when(pair != z)
    def _():
        pl.semaphore_signal(barrier, inc=1, device_id=along, device_id_type=MESH)

    @pl.when(z != 0)
    def _():
        pl.semaphore_signal(barrier, inc=1, device_id=across, device_id_type=MESH)
        pl.semaphore_signal(barrier, inc=1, device_id=source, device_id_type=MESH)

    pl.semaphore_wait(barrier, 9 + jnp.where(pair != z, 1, 0) + jnp.where(z != 0, 2, 0))

    def lanes(half, gz):
        return pl.ds(pl.multiple_of((half * NZ + gz) * TOK, TOK), TOK)

    def chunk(half, s):
        return jnp.where(half == 0, z + 2 * NZ - 1 - s, z + 1 + s) % NZ

    def spread(s, i):
        gz = chunk(xh, s)
        return remote(
            xin.at[gz], x.at[xl, :, lanes(xh, gz)], x_s.at[s, i], x_r.at[s, i], xp[i]
        )

    def spread_all(s):
        for i in range(3):
            spread(s, i).start()

    def await_all(s):
        gz = chunk(xh, s)
        x[xl, :, lanes(xh, gz)] = xin[gz]
        for i in range(3):
            spread(s, i).wait_recv()

    spread_all(0)
    spread_all(1)

    def partial(half, gz):
        at = lanes(half, gz)
        xt = x[0, :, at]
        dyt = x[1, :, at].astype(F32)
        for slot in range(SLOTS):
            e = ids[half * (NZ * SLOTS) + gz * SLOTS + slot]
            dys = (dyt * scale[half, gz, pl.ds(slot, 1), :]).astype(BF16)
            dcat[slot, :, at] = dys
            gu = jnp.dot(wt[e, 0 : 2 * FH, :], xt, preferred_element_type=F32)
            dh = jnp.dot(wt[e, 2 * FH : FP, :], dys, preferred_element_type=F32)
            own[half, slot, 0 : 2 * FH, :] = gu
            own[half, slot, 2 * FH : FP, :] = dh

    def hop(half, slot, s, src, dst):
        return remote(src, dst, rs_s.at[half, s, slot], rs_r.at[half, s, slot], to[half])

    def hop16(half, slot, s, src):
        return hop(half, slot, s, src, early.at[half, s, slot])

    def hop32(half, slot, s, src):
        return hop(half, slot, s, src, acc.at[half, s - NB, slot])

    await_all(0)
    for half in range(2):
        partial(half, chunk(half, 0))
        for slot in range(SLOTS):
            first[half, slot] = own[half, slot].astype(BF16)
            hop16(half, slot, 0, first.at[half, slot]).start()

    def fresh(s):
        spread_all(s + 1)
        await_all(s)
        for half in range(2):
            partial(half, chunk(half, s))

    def ring16(s, carry):
        fresh(s)
        for slot in range(SLOTS):
            for half in range(2):
                here = early.at[half, s - 1, slot]
                hop16(half, slot, s - 1, here).wait_recv()
                total = early[half, s - 1, slot].astype(F32) + own[half, slot]
                early[half, s - 1, slot] = total.astype(BF16)
                hop16(half, slot, s, here).start()
        return carry

    lax.fori_loop(1, NB, ring16, 0)
    fresh(NB)
    for slot in range(SLOTS):
        for half in range(2):
            here = early.at[half, NB - 1, slot]
            hop16(half, slot, NB - 1, here).wait_recv()
            turn[half, slot] = early[half, NB - 1, slot, 0:F3].astype(F32) + own[half, slot, 0:F3]
            hop32(half, slot, NB, turn.at[half, slot]).start()

    def ring32(s, carry):
        fresh(s)
        for slot in range(SLOTS):
            for half in range(2):
                here = acc.at[half, s - 1 - NB, slot]
                hop32(half, slot, s - 1, here).wait_recv()
                acc[half, s - 1 - NB, slot] = acc[half, s - 1 - NB, slot] + own[half, slot, 0:F3]
                hop32(half, slot, s, here).start()
        return carry

    lax.fori_loop(NB + 1, NZ - 1, ring32, 0)
    await_all(NZ - 1)

    def gather(half, slot, s, gz):
        ref = hcat.at[slot, :, lanes(half, gz)]
        return remote(ref, ref, ag_s.at[half, s, slot], ag_r.at[half, s, slot], to[half])

    def origin(half, s):
        return (z + NZ - s) % NZ if half == 0 else (z + s) % NZ

    def spot(gz):
        return (gz + z) % NZ

    def rows_a(half, gz):
        q = spot(gz)
        i = (q % NY - y + NY) % NY
        src = dxs.at[half, q // NY, q % NY, pl.ds(0, hd)]
        return i, lambda: remote(
            src, a1.at[i - 1, half, q // NY], a1s.at[half, gz], a1r.at[i - 1, half, q // NY],
            device(xl, q % NY, z, xh, c),
        )

    def rows_b(half, gz):
        q = spot(gz)
        i = (half * 2 + q // NY - pos + 4) % 4
        src = dxs.at[half, q // NY, q % NY, pl.ds(hd, hd)]
        return i, lambda: remote(
            src, b1.at[i - 1, q % NY], b1s.at[half, gz], b1r.at[i - 1, q % NY],
            device(q // NY, y, z, half, c),
        )

    def rows(half, gz):
        total = jnp.zeros((DZ, TOK), F32)
        for slot in range(SLOTS):
            e = ids[half * (NZ * SLOTS) + gz * SLOTS + slot]
            hs = hcat[slot, 0 : 2 * FH, lanes(half, gz)]
            total = total + jnp.dot(
                w[e, :, 0 : 2 * FH], hs, preferred_element_type=F32
            )
        q = spot(gz)
        dx[half, q // NY, q % NY] = total
        dxs[half, q // NY, q % NY] = total.astype(BF16)
        for i, make in (rows_a(half, gz), rows_b(half, gz)):

            @pl.when(i != 0)
            def _(make=make):
                make().start()

    for half in range(2):
        partial(half, z)
    for slot in range(SLOTS):
        for half in range(2):
            last = acc.at[half, NZ - 2 - NB, slot]
            hop32(half, slot, NZ - 2, last).wait_recv()
            g = acc[half, NZ - 2 - NB, slot, 0:FH, :] + own[half, slot, 0:FH, :]
            u = acc[half, NZ - 2 - NB, slot, FH : 2 * FH, :] + own[half, slot, FH : 2 * FH, :]
            dh = acc[half, NZ - 2 - NB, slot, 2 * FH : F3, :] + own[half, slot, 2 * FH : F3, :]
            sig = 1.0 / (1.0 + jnp.exp(-g))
            act = g * sig
            dg = dh * u * sig * (1.0 + g * (1.0 - sig))
            du = dh * act
            hid = act * u
            hcat[slot, 0 : 2 * FH, lanes(half, z)] = jnp.concatenate([dg, du], axis=0).astype(BF16)
            hcat[slot, 2 * FH : FP, lanes(half, z)] = jnp.concatenate(
                [hid, jnp.zeros((FP - F3, TOK), F32)], axis=0
            ).astype(BF16)
            gather(half, slot, 0, z).start()
    for half in range(2):
        rows(half, z)

    def pass_on(s, carry):
        for slot in range(SLOTS):
            for half in range(2):
                gather(half, slot, s - 1, origin(half, s)).wait_recv()
                gather(half, slot, s, origin(half, s)).start()
        for half in range(2):
            rows(half, origin(half, s))
        return carry

    lax.fori_loop(1, NZ - 1, pass_on, 0)
    for half in range(2):
        for slot in range(SLOTS):
            gather(half, slot, NZ - 2, origin(half, NZ - 1)).wait_recv()
        rows(half, origin(half, NZ - 1))

    cols = NXH * NZ * TOK
    def expert_row(slot):
        return jnp.concatenate(
            [
                scale[i // NZ, i % NZ, 2 + slot : 3 + slot, :]
                for i in range(NXH * NZ)
            ],
            axis=1,
        )

    id0, id1 = expert_row(0), expert_row(1)
    nt = (((1,), (1,)), ((), ()))

    def weights(e):
        is0 = jnp.broadcast_to(id0 == e.astype(F32), (16, cols))
        is1 = jnp.broadcast_to(id1 == e.astype(F32), (16, cols))
        zero = jnp.zeros((16, cols), BF16)

        def pick(pair, n):
            return jnp.concatenate(
                [
                    jnp.where(
                        is0,
                        pair[0, r * 16 : (r + 1) * 16, :],
                        jnp.where(is1, pair[1, r * 16 : (r + 1) * 16, :], zero),
                    )
                    for r in range(n // 16)
                ],
                axis=0,
            )

        hs = pick(hcat, FP)
        ds = pick(dcat, DZ)
        gu = lax.dot_general(x[0], hs, nt, preferred_element_type=F32)
        dn = lax.dot_general(ds, hs[256:], nt, preferred_element_type=F32)
        column = lax.broadcasted_iota(jnp.int32, (DZ, FP - 256), 1)
        tail = jnp.where(column < 2 * FH - 256, gu[:, 256:], dn)
        for q in range(NXH * NC):
            dw[e, q, :, 0:256] = gu[q * SUB : (q + 1) * SUB, 0:256]
            dw[e, q, :, 256:FP] = tail[q * SUB : (q + 1) * SUB]

    def cross(e, i):
        blk = (1 - xh) if i == 0 else xh
        return remote(dw.at[e, 2 * blk + 1 - c], wgot.at[i, e], ts.at[i, e], tr.at[i, e], twin)

    def away(e):
        return remote(wsnd.at[e], wfar.at[e], fs.at[e], fr.at[e], far)

    def combine(e):
        cross(e, 0).wait_recv()
        wsnd[e] = (dw[e, 2 * (1 - xh) + c] + wgot[0, e]).astype(BF16)
        away(e).start()
        cross(e, 1).wait_recv()
        wgot[1, e] = dw[e, 2 * xh + c] + wgot[1, e]

    def second(i, kind):
        if kind == 0:
            t = (pos + i + 1) % 4
            return remote(sa.at[t // 2, t % 2], a2.at[i], a2s.at[i], a2r.at[i], xp[i])
        t = (y + i + 1) % NY
        return remote(sb.at[t], b2.at[i], b2s.at[i], b2r.at[i], yp[i])

    def rows_second():
        for i in range(3):
            for j in range(NXH):
                for k in range(NXL):
                    remote(
                        dxs.at[0, 0, 0, pl.ds(0, hd)], a1.at[i, j, k], a1s.at[0, 0],
                        a1r.at[i, j, k], up,
                    ).wait_recv()
        for j in range(NXH):
            for k in range(NXL):
                sa[j, k] = dx[j, k, y, 0:hd] + (
                    a1[0, j, k].astype(F32) + a1[1, j, k].astype(F32) + a1[2, j, k].astype(F32)
                )
        for i in range(3):
            second(i, 0).start()
        for i in range(3):
            for j in range(NY):
                remote(
                    dxs.at[0, 0, 0, pl.ds(hd, hd)], b1.at[i, j], b1s.at[0, 0], b1r.at[i, j], up
                ).wait_recv()
        for j in range(NY):
            sb[j] = dx[xh, xl, j, hd:DZ] + (
                b1[0, j].astype(F32) + b1[1, j].astype(F32) + b1[2, j].astype(F32)
            )
        for i in range(3):
            second(i, 1).start()

    def rows_swap():
        for i in range(3):
            second(i, 0).wait_recv()
        done[0:hd] = sa[xh, xl] + a2[0] + a2[1] + a2[2]
        for i in range(3):
            second(i, 1).wait_recv()
        done[hd:DZ] = sb[y] + b2[0] + b2[1] + b2[2]

        @pl.when(pair != z)
        def _():
            first_step().start()

    def first_step():
        return remote(done, mid, ks.at[0], kr.at[0], along)

    def second_step():
        return remote(mid, back, ks.at[1], kr.at[1], across)

    def rows_turn():
        @pl.when(pair != z)
        def _():
            first_step().wait_recv()

        @pl.when(pair == z)
        def _():
            mid[...] = done[...]

        @pl.when(z != 0)
        def _():
            second_step().start()

        @pl.when(z == 0)
        def _():
            back[...] = mid[...]

    def finish(e):
        away(e).wait_recv()
        ours = wgot[1, e]
        theirs = wfar[e].astype(F32)
        low = jnp.where(xh == 0, ours, theirs)
        high = jnp.where(xh == 0, theirs, ours)
        gate[e] = jnp.concatenate([low[:, 0:FH], high[:, 0:FH]], axis=1)
        up_out[e] = jnp.concatenate([low[:, FH : 2 * FH], high[:, FH : 2 * FH]], axis=1)
        down_out[e] = jnp.concatenate([low[:, 2 * FH : F3].T, high[:, 2 * FH : F3].T], axis=0)

    def per_expert(e, carry):
        weights(e)
        cross(e, 0).start()
        cross(e, 1).start()

        @pl.when(e > 0)
        def _():
            combine(e - 1)

        @pl.when(e == 0)
        def _():
            rows_second()

        @pl.when(e == SWAP_AT)
        def _():
            rows_swap()

        return carry

    lax.fori_loop(0, EXPERTS, per_expert, 0)
    combine(EXPERTS - 1)

    def finish_all(e, carry):
        finish(e)

        @pl.when(e == TURN_AT)
        def _():
            rows_turn()

        return carry

    lax.fori_loop(0, EXPERTS, finish_all, 0)

    def drain_ring(s, carry):
        for half in range(2):
            for slot in range(SLOTS):
                gather(half, slot, s, origin(half, s)).wait_send()
        return carry

    for half in range(2):
        for slot in range(SLOTS):
            hop16(half, slot, 0, first.at[half, slot]).wait_send()
            for s in range(1, NB):
                hop16(half, slot, s, early.at[half, s - 1, slot]).wait_send()
            hop32(half, slot, NB, turn.at[half, slot]).wait_send()
            for s in range(NB + 1, NZ - 1):
                hop32(half, slot, s, acc.at[half, s - 1 - NB, slot]).wait_send()
    lax.fori_loop(1, NZ - 1, drain_ring, 0)
    for half in range(2):
        for slot in range(SLOTS):
            gather(half, slot, 0, z).wait_send()

    def drain(s, carry):
        for i in range(3):
            spread(s, i).wait_send()
        for half in range(2):
            for i, make in (rows_a(half, s), rows_b(half, s)):

                @pl.when(i != 0)
                def _(make=make):
                    make().wait_send()

        cross(s, 0).wait_send()
        cross(s, 1).wait_send()
        away(s).wait_send()
        return carry

    lax.fori_loop(0, NZ, drain, 0)
    for i in range(3):
        second(i, 0).wait_send()
        second(i, 1).wait_send()

    @pl.when(pair != z)
    def _():
        first_step().wait_send()

    @pl.when(z != 0)
    def _():
        second_step().wait()

    xout[...] = back[...].T


def layer(ids, xin, w, wt, scale):
    dma = pltpu.SemaphoreType.DMA
    vm = pl.BlockSpec(memory_space=pltpu.VMEM)
    hd = DZ // 2
    cols = NXH * NZ * TOK
    block = (EXPERTS, SUB, FP)
    return pl.pallas_call(
        layer_kernel,
        out_shape=(
            jax.ShapeDtypeStruct((EXPERTS, SUB, 2 * FH), F32),
            jax.ShapeDtypeStruct((EXPERTS, SUB, 2 * FH), F32),
            jax.ShapeDtypeStruct((EXPERTS, 2 * FH, SUB), F32),
            jax.ShapeDtypeStruct((TOK, DZ), F32),
        ),
        in_specs=[pl.BlockSpec(memory_space=pltpu.SMEM), vm, vm, vm, vm],
        out_specs=(vm,) * 4,
        scratch_shapes=[
            pltpu.VMEM((2, DZ, cols), BF16),
            pltpu.VMEM((2, NB, SLOTS, FP, TOK), BF16),
            pltpu.VMEM((2, SLOTS, FP, TOK), BF16),
            pltpu.VMEM((2, NZ - 1 - NB, SLOTS, F3, TOK), F32),
            pltpu.VMEM((2, SLOTS, F3, TOK), F32),
            pltpu.VMEM((2, SLOTS, FP, TOK), F32),
            pltpu.VMEM((SLOTS, DZ, cols), BF16),
            pltpu.VMEM((SLOTS, FP, cols), BF16),
            pltpu.VMEM((NXH, NXL, NY, DZ, TOK), F32),
            pltpu.VMEM((NXH, NXL, NY, DZ, TOK), BF16),
            pltpu.VMEM((EXPERTS, NXH * NC, SUB, FP), F32),
            pltpu.VMEM((2,) + block, F32),
            pltpu.VMEM(block, BF16),
            pltpu.VMEM(block, BF16),
            pltpu.VMEM((3, NXH, NXL, hd, TOK), BF16),
            pltpu.VMEM((3, hd, TOK), F32),
            pltpu.VMEM((3, NY, hd, TOK), BF16),
            pltpu.VMEM((3, hd, TOK), F32),
            pltpu.VMEM((NXH, NXL, hd, TOK), F32),
            pltpu.VMEM((NY, hd, TOK), F32),
            pltpu.VMEM((DZ, TOK), F32),
            pltpu.VMEM((DZ, TOK), F32),
            pltpu.VMEM((DZ, TOK), F32),
            dma((NZ, 3)),
            dma((NZ, 3)),
        ]
        + [dma((2, NZ - 1, SLOTS))] * 4
        + [dma((2, NZ)), dma((3, NXH, NXL)), dma((2, NZ)), dma((3, NY))]
        + [dma((3,))] * 4
        + [dma((2, EXPERTS))] * 2
        + [dma((EXPERTS,))] * 2
        + [dma((2,))] * 2,
        compiler_params=pltpu.CompilerParams(
            collective_id=1, has_side_effects=True, vmem_limit_bytes=VMEM_LIMIT
        ),
        name="layer",
    )(ids, xin, w, wt, scale)


def shards(
    activations, cotangent, expert_ids, slot_rows, slot_counts, route_probs, w_gate, w_up, w_down
):
    xin, info_all, w_all, wt = exchange(
        activations, cotangent, slot_rows[0], slot_counts, route_probs[0], expert_ids,
        w_gate, w_up, w_down,
    )
    ids = info_all[:, :, 2:4, 0].astype(jnp.int32).reshape(-1)
    grad_gate, grad_up, grad_down, rows = layer(
        ids, xin, w_all.reshape(EXPERTS, DZ, FP), wt, info_all
    )
    return rows, grad_gate, grad_up, grad_down


def solution(mesh):
    return jax.shard_map(
        shards,
        mesh=mesh,
        in_specs=(
            P("dp", None),
            P("dp", None),
            P("dp", None),
            P("dp", None, None),
            P("dp", None),
            P("dp", None, None),
            P(None, "dp", "expert"),
            P(None, "dp", "expert"),
            P(None, "expert", "dp"),
        ),
        out_specs=(
            P("dp", "expert"),
            P(None, "dp", "expert"),
            P(None, "dp", "expert"),
            P(None, "expert", "dp"),
        ),
        check_vma=False,
    )
```

```python
import jax
import jax.numpy as jnp
from jax import lax
from jax.experimental import pallas as pl
from jax.experimental.pallas import tpu as pltpu
from jax.sharding import PartitionSpec as P

MESH = pl.DeviceIdType.MESH
F32 = jnp.float32
BF16 = jnp.bfloat16

NZ, NXH, NC, NXL, NY = 8, 2, 2, 2, 4
SLOTS = 2
EXPERTS = 8
TOK = 128
SUB = 112
DZ = 448
FH = 152
F3 = 3 * FH
FP = 464
NB = 3
SWAP_AT = 7
TURN_AT = 4
VMEM_LIMIT = 61 * 1024 * 1024


def place():
    ex = lax.axis_index("expert")
    dp = lax.axis_index("dp")
    return ex // NY, ex % NY, dp // 4, (dp // 2) % 2, dp % 2


def device(xl, y, z, xh, c):
    return (xl * NY + y, z * 4 + xh * 2 + c)


def remote(src, dst, ssem, rsem, dev):
    return pltpu.make_async_remote_copy(
        src_ref=src, dst_ref=dst, send_sem=ssem, recv_sem=rsem, device_id=dev, device_id_type=MESH
    )


def greet(devices):
    barrier = pltpu.get_barrier_semaphore()
    for dev in devices:
        pl.semaphore_signal(barrier, inc=1, device_id=dev, device_id_type=MESH)
    pl.semaphore_wait(barrier, len(devices))


def x_peers(xl, y, z, xh, c):
    pos = xh * 2 + xl
    out = []
    for step in range(1, 4):
        to = (pos + step) % 4
        out.append(device(to % 2, y, z, to // 2, c))
    return out


def y_peers(xl, y, z, xh, c):
    return [device(xl, (y + step) % NY, z, xh, c) for step in range(1, NY)]


def z_peers(xl, y, z, xh, c):
    return [device(xl, y, (z + step) % NZ, xh, c) for step in range(1, NZ)]


def layer_kernel(
    act, cot, rows_in, counts, probs, ids, wg, wu, wd, gate, up_out, down_out, xout,
    xt, stack, info, numbers, wsrc, w, wt, xin, scale, experts,
    x, early, first, acc, turn, own, dcat, hcat, dx, dxs, dw, wgot, wsnd, wfar,
    a1, a2, b1, b2, sa, sb, done, mid, back,
    zs, zr, is_, ir, js, jr, ys, yr, ixs, ixr, gs, gr, os_, or_, ps, pr, loc,
    x_s, x_r, rs_s, rs_r, ag_s, ag_r,
    a1s, a1r, b1s, b1r, a2s, a2r, b2s, b2r, ts, tr, fs, fr, ks, kr,
):
    xl, y, z, xh, c = me = place()
    ex = xl * NY + y
    pos = xh * 2 + xl
    hd = DZ // 2
    zp, xp, yp = z_peers(*me), x_peers(*me), y_peers(*me)
    up, down = zp[0], zp[NZ - 2]
    to = (up, down)
    far = device(xl, y, z, 1 - xh, c)
    twin = device(xl, y, z, xh, 1 - c)
    part = pl.ds(pl.multiple_of(y * SUB, SUB), SUB)
    mine = 2 * xh + c
    other = 2 * (1 - xh) + c
    pair = (ex + NZ - z) % NZ
    along = device(xl, y, pair, xh, c)
    across = device(pair // NY, pair % NY, z, xh, c)
    before = (ex + z) % NZ
    source = device(before // NY, before % NY, z, xh, c)
    barrier = pltpu.get_barrier_semaphore()
    peers = zp + xp + yp + [twin]
    for dev in peers:
        pl.semaphore_signal(barrier, inc=1, device_id=dev, device_id_type=MESH)

    @pl.when(z != 0)
    def _():
        pl.semaphore_signal(barrier, inc=1, device_id=across, device_id_type=MESH)
        pl.semaphore_signal(barrier, inc=1, device_id=source, device_id_type=MESH)

    def pack(e, carry):
        g = wg[e].astype(F32)
        u = wu[e].astype(F32)
        d = wd[e].astype(F32).T
        both = []
        for i in range(NXH):
            pieces = [v[:, i * FH : (i + 1) * FH] for v in (g, u, d)]
            pieces.append(jnp.zeros((SUB, FP - F3), F32))
            both.append(jnp.concatenate(pieces, axis=1))
        wsrc[e] = jnp.where(xh == 0, both[1], both[0]).astype(BF16)
        w[e, mine] = jnp.where(xh == 0, both[0], both[1]).astype(BF16)
        return carry

    lax.fori_loop(0, EXPERTS, pack, 0)
    pl.semaphore_wait(barrier, len(peers) + jnp.where(z != 0, 2, 0))

    wgone = []
    for e in range(EXPERTS):
        wgone.append(remote(wsrc.at[e], w.at[e, mine], gs.at[e], gr.at[e], far))
        wgone[-1].start()
    wown = []
    for e in range(EXPERTS):
        wown.append(remote(w.at[e, mine], w.at[e, mine], os_.at[e], or_.at[e], twin))
        wown[-1].start()

    def turn_rows(j, carry):
        cols = pl.ds(pl.multiple_of(j * TOK, TOK), TOK)
        xt[cols, :] = jnp.where(xl == 0, act[:, cols], cot[:, cols]).T
        return carry

    lax.fori_loop(0, NZ * DZ // TOK, turn_rows, 0)

    def piece(gz):
        return xt.at[pl.ds(pl.multiple_of(gz * DZ + y * SUB, 16), SUB)]

    cz = []
    for i in range(NZ - 1):
        cz.append(remote(piece((z + i + 1) % NZ), xin.at[z, part], zs.at[i], zr.at[i], zp[i]))
        cz[-1].start()

    lane = lax.broadcasted_iota(jnp.int32, (1, TOK), 1)
    column = lax.broadcasted_iota(jnp.int32, (TOK, TOK), 1).astype(F32)
    for slot in range(SLOTS):
        stack[slot : slot + 1, :] = rows_in[slot : slot + 1, :].astype(F32)
        stack[2 + slot : 3 + slot, :] = jnp.where(
            lane < counts[0, slot], probs[slot : slot + 1, :], 0.0
        )
    stack[4:8, :] = jnp.zeros((4, TOK), F32)
    turned = stack[...].T
    info[4:8, :] = jnp.zeros((4, TOK), F32)
    numbers[...] = jnp.zeros((8, TOK), jnp.int32)
    for slot in range(SLOTS):
        hit = turned[:, slot : slot + 1] == column
        info[slot : slot + 1, :] = jnp.sum(
            jnp.where(hit, turned[:, 2 + slot : 3 + slot], 0.0), axis=0, keepdims=True
        )
        number = jnp.full((1, TOK), ids[0, slot], jnp.int32)
        numbers[slot : slot + 1, :] = number
        info[2 + slot : 3 + slot, :] = number.astype(F32)
    ci = []
    for i in range(NZ - 1):
        ci.append(remote(info, scale.at[xh, z], is_.at[i], ir.at[i], zp[i]))
        ci[-1].start()
        ci.append(remote(numbers, experts.at[xh, z], js.at[i], jr.at[i], zp[i]))
        ci[-1].start()
    here = [
        pltpu.make_async_copy(piece(z), xin.at[z, part], loc.at[0]),
        pltpu.make_async_copy(info, scale.at[xh, z], loc.at[1]),
        pltpu.make_async_copy(numbers, experts.at[xh, z], loc.at[2]),
    ]
    for h in here:
        h.start()
    for h in here:
        h.wait()
    for k in cz:
        k.wait()
    cy = []
    for i in range(3):
        cy.append(remote(xin.at[:, part], xin.at[:, part], ys.at[i], yr.at[i], yp[i]))
        cy[-1].start()
    for k in ci:
        k.wait()
    cinf = [
        remote(scale.at[xh], scale.at[xh], ixs.at[0], ixr.at[0], far),
        remote(experts.at[xh], experts.at[xh], ixs.at[1], ixr.at[1], far),
    ]
    for k in cinf:
        k.start()
    for k in cy:
        k.wait()

    def lanes(half, gz):
        return pl.ds(pl.multiple_of((half * NZ + gz) * TOK, TOK), TOK)

    def chunk(half, s):
        return jnp.where(half == 0, z + 2 * NZ - 1 - s, z + 1 + s) % NZ

    def spread(s, i):
        gz = chunk(xh, s)
        return remote(
            xin.at[gz], x.at[xl, :, lanes(xh, gz)], x_s.at[s, i], x_r.at[s, i], xp[i]
        )

    def spread_all(s):
        for i in range(3):
            spread(s, i).start()

    def await_all(s):
        gz = chunk(xh, s)
        x[xl, :, lanes(xh, gz)] = xin[gz]
        for i in range(3):
            spread(s, i).wait_recv()
    spread_all(0)
    spread_all(1)
    wpass = []
    for e in range(EXPERTS):
        wgone[e].wait_recv()
        wpass.append(remote(w.at[e, other], w.at[e, other], ps.at[e], pr.at[e], twin))
        wpass[-1].start()
    for e in range(EXPERTS):
        wown[e].wait_recv()
        wpass[e].wait_recv()
        wt[e] = w[e].reshape(DZ, FP).T
    for k in cinf:
        k.wait()
    for k in wgone + wown + wpass:
        k.wait_send()

    def partial(half, gz):
        at = lanes(half, gz)
        xt = x[0, :, at]
        dyt = x[1, :, at].astype(F32)
        for slot in range(SLOTS):
            e = experts[half, gz, slot, 0]
            dys = (dyt * scale[half, gz, pl.ds(slot, 1), :]).astype(BF16)
            dcat[slot, :, at] = dys
            gu = jnp.dot(wt[e, 0 : 2 * FH, :], xt, preferred_element_type=F32)
            dh = jnp.dot(wt[e, 2 * FH : FP, :], dys, preferred_element_type=F32)
            own[half, slot, 0 : 2 * FH, :] = gu
            own[half, slot, 2 * FH : FP, :] = dh

    def hop(half, slot, s, src, dst):
        return remote(src, dst, rs_s.at[half, s, slot], rs_r.at[half, s, slot], to[half])

    def hop16(half, slot, s, src):
        return hop(half, slot, s, src, early.at[half, s, slot])

    def hop32(half, slot, s, src):
        return hop(half, slot, s, src, acc.at[half, s - NB, slot])

    await_all(0)
    for half in range(2):
        partial(half, chunk(half, 0))
        for slot in range(SLOTS):
            first[half, slot] = own[half, slot].astype(BF16)
            hop16(half, slot, 0, first.at[half, slot]).start()

    def fresh(s):
        spread_all(s + 1)
        await_all(s)
        for half in range(2):
            partial(half, chunk(half, s))

    def ring16(s, carry):
        fresh(s)
        for slot in range(SLOTS):
            for half in range(2):
                here = early.at[half, s - 1, slot]
                hop16(half, slot, s - 1, here).wait_recv()
                total = early[half, s - 1, slot].astype(F32) + own[half, slot]
                early[half, s - 1, slot] = total.astype(BF16)
                hop16(half, slot, s, here).start()
        return carry

    lax.fori_loop(1, NB, ring16, 0)
    fresh(NB)
    for slot in range(SLOTS):
        for half in range(2):
            here = early.at[half, NB - 1, slot]
            hop16(half, slot, NB - 1, here).wait_recv()
            turn[half, slot] = early[half, NB - 1, slot, 0:F3].astype(F32) + own[half, slot, 0:F3]
            hop32(half, slot, NB, turn.at[half, slot]).start()

    def ring32(s, carry):
        fresh(s)
        for slot in range(SLOTS):
            for half in range(2):
                here = acc.at[half, s - 1 - NB, slot]
                hop32(half, slot, s - 1, here).wait_recv()
                acc[half, s - 1 - NB, slot] = acc[half, s - 1 - NB, slot] + own[half, slot, 0:F3]
                hop32(half, slot, s, here).start()
        return carry

    lax.fori_loop(NB + 1, NZ - 1, ring32, 0)
    await_all(NZ - 1)

    def gather(half, slot, s, gz):
        ref = hcat.at[slot, :, lanes(half, gz)]
        return remote(ref, ref, ag_s.at[half, s, slot], ag_r.at[half, s, slot], to[half])

    def origin(half, s):
        return (z + NZ - s) % NZ if half == 0 else (z + s) % NZ

    def spot(gz):
        return (gz + z) % NZ

    def rows_a(half, gz):
        q = spot(gz)
        i = (q % NY - y + NY) % NY
        src = dxs.at[half, q // NY, q % NY, pl.ds(0, hd)]
        return i, lambda: remote(
            src, a1.at[i - 1, half, q // NY], a1s.at[half, gz], a1r.at[i - 1, half, q // NY],
            device(xl, q % NY, z, xh, c),
        )

    def rows_b(half, gz):
        q = spot(gz)
        i = (half * 2 + q // NY - pos + 4) % 4
        src = dxs.at[half, q // NY, q % NY, pl.ds(hd, hd)]
        return i, lambda: remote(
            src, b1.at[i - 1, q % NY], b1s.at[half, gz], b1r.at[i - 1, q % NY],
            device(q // NY, y, z, half, c),
        )

    def rows(half, gz):
        total = jnp.zeros((DZ, TOK), F32)
        for slot in range(SLOTS):
            e = experts[half, gz, slot, 0]
            hs = hcat[slot, 0 : 2 * FH, lanes(half, gz)]
            total = total + jnp.dot(
                w[e, :, :, 0 : 2 * FH].reshape(DZ, 2 * FH), hs, preferred_element_type=F32
            )
        q = spot(gz)
        dx[half, q // NY, q % NY] = total
        dxs[half, q // NY, q % NY] = total.astype(BF16)
        for i, make in (rows_a(half, gz), rows_b(half, gz)):

            @pl.when(i != 0)
            def _(make=make):
                make().start()

    for half in range(2):
        partial(half, z)
    for slot in range(SLOTS):
        for half in range(2):
            last = acc.at[half, NZ - 2 - NB, slot]
            hop32(half, slot, NZ - 2, last).wait_recv()
            g = acc[half, NZ - 2 - NB, slot, 0:FH, :] + own[half, slot, 0:FH, :]
            u = acc[half, NZ - 2 - NB, slot, FH : 2 * FH, :] + own[half, slot, FH : 2 * FH, :]
            dh = acc[half, NZ - 2 - NB, slot, 2 * FH : F3, :] + own[half, slot, 2 * FH : F3, :]
            sig = 1.0 / (1.0 + jnp.exp(-g))
            act = g * sig
            dg = dh * u * sig * (1.0 + g * (1.0 - sig))
            du = dh * act
            hid = act * u
            hcat[slot, 0 : 2 * FH, lanes(half, z)] = jnp.concatenate([dg, du], axis=0).astype(BF16)
            hcat[slot, 2 * FH : FP, lanes(half, z)] = jnp.concatenate(
                [hid, jnp.zeros((FP - F3, TOK), F32)], axis=0
            ).astype(BF16)
            gather(half, slot, 0, z).start()
    for half in range(2):
        rows(half, z)

    def pass_on(s, carry):
        for slot in range(SLOTS):
            for half in range(2):
                gather(half, slot, s - 1, origin(half, s)).wait_recv()
                gather(half, slot, s, origin(half, s)).start()
        for half in range(2):
            rows(half, origin(half, s))
        return carry

    lax.fori_loop(1, NZ - 1, pass_on, 0)
    for half in range(2):
        for slot in range(SLOTS):
            gather(half, slot, NZ - 2, origin(half, NZ - 1)).wait_recv()
        rows(half, origin(half, NZ - 1))

    cols = NXH * NZ * TOK
    def expert_row(slot):
        return jnp.concatenate(
            [
                scale[i // NZ, i % NZ, 2 + slot : 3 + slot, :]
                for i in range(NXH * NZ)
            ],
            axis=1,
        )

    id0, id1 = expert_row(0), expert_row(1)
    nt = (((1,), (1,)), ((), ()))

    def weights(e):
        is0 = jnp.broadcast_to(id0 == e.astype(F32), (16, cols))
        is1 = jnp.broadcast_to(id1 == e.astype(F32), (16, cols))
        zero = jnp.zeros((16, cols), BF16)

        def pick(pair, n):
            return jnp.concatenate(
                [
                    jnp.where(
                        is0,
                        pair[0, r * 16 : (r + 1) * 16, :],
                        jnp.where(is1, pair[1, r * 16 : (r + 1) * 16, :], zero),
                    )
                    for r in range(n // 16)
                ],
                axis=0,
            )

        hs = pick(hcat, FP)
        ds = pick(dcat, DZ)
        gu = lax.dot_general(x[0], hs, nt, preferred_element_type=F32)
        dn = lax.dot_general(ds, hs[256:], nt, preferred_element_type=F32)
        column = lax.broadcasted_iota(jnp.int32, (DZ, FP - 256), 1)
        tail = jnp.where(column < 2 * FH - 256, gu[:, 256:], dn)
        for q in range(NXH * NC):
            dw[e, q, :, 0:256] = gu[q * SUB : (q + 1) * SUB, 0:256]
            dw[e, q, :, 256:FP] = tail[q * SUB : (q + 1) * SUB]

    def cross(e, i):
        blk = (1 - xh) if i == 0 else xh
        return remote(dw.at[e, 2 * blk + 1 - c], wgot.at[i, e], ts.at[i, e], tr.at[i, e], twin)

    def away(e):
        return remote(wsnd.at[e], wfar.at[e], fs.at[e], fr.at[e], far)

    def combine(e):
        cross(e, 0).wait_recv()
        wsnd[e] = (dw[e, 2 * (1 - xh) + c] + wgot[0, e]).astype(BF16)
        away(e).start()
        cross(e, 1).wait_recv()
        wgot[1, e] = dw[e, 2 * xh + c] + wgot[1, e]

    def second(i, kind):
        if kind == 0:
            t = (pos + i + 1) % 4
            return remote(sa.at[t // 2, t % 2], a2.at[i], a2s.at[i], a2r.at[i], xp[i])
        t = (y + i + 1) % NY
        return remote(sb.at[t], b2.at[i], b2s.at[i], b2r.at[i], yp[i])

    def rows_second():
        for i in range(3):
            for j in range(NXH):
                for k in range(NXL):
                    remote(
                        dxs.at[0, 0, 0, pl.ds(0, hd)], a1.at[i, j, k], a1s.at[0, 0],
                        a1r.at[i, j, k], up,
                    ).wait_recv()
        for j in range(NXH):
            for k in range(NXL):
                sa[j, k] = dx[j, k, y, 0:hd] + (
                    a1[0, j, k].astype(F32) + a1[1, j, k].astype(F32) + a1[2, j, k].astype(F32)
                )
        for i in range(3):
            second(i, 0).start()
        for i in range(3):
            for j in range(NY):
                remote(
                    dxs.at[0, 0, 0, pl.ds(hd, hd)], b1.at[i, j], b1s.at[0, 0], b1r.at[i, j], up
                ).wait_recv()
        for j in range(NY):
            sb[j] = dx[xh, xl, j, hd:DZ] + (
                b1[0, j].astype(F32) + b1[1, j].astype(F32) + b1[2, j].astype(F32)
            )
        for i in range(3):
            second(i, 1).start()

    def rows_swap():
        for i in range(3):
            second(i, 0).wait_recv()
        done[0:hd] = sa[xh, xl] + a2[0] + a2[1] + a2[2]
        for i in range(3):
            second(i, 1).wait_recv()
        done[hd:DZ] = sb[y] + b2[0] + b2[1] + b2[2]

        @pl.when(pair != z)
        def _():
            first_step().start()

    def first_step():
        return remote(done, mid, ks.at[0], kr.at[0], along)

    def second_step():
        return remote(mid, back, ks.at[1], kr.at[1], across)

    def rows_turn():
        @pl.when(pair != z)
        def _():
            first_step().wait_recv()

        @pl.when(pair == z)
        def _():
            mid[...] = done[...]

        @pl.when(z != 0)
        def _():
            second_step().start()

        @pl.when(z == 0)
        def _():
            back[...] = mid[...]

    def finish(e):
        away(e).wait_recv()
        ours = wgot[1, e]
        theirs = wfar[e].astype(F32)
        low = jnp.where(xh == 0, ours, theirs)
        high = jnp.where(xh == 0, theirs, ours)
        gate[e] = jnp.concatenate([low[:, 0:FH], high[:, 0:FH]], axis=1)
        up_out[e] = jnp.concatenate([low[:, FH : 2 * FH], high[:, FH : 2 * FH]], axis=1)
        down_out[e] = jnp.concatenate([low[:, 2 * FH : F3].T, high[:, 2 * FH : F3].T], axis=0)

    def per_expert(e, carry):
        weights(e)
        cross(e, 0).start()
        cross(e, 1).start()

        @pl.when(e > 0)
        def _():
            combine(e - 1)

        @pl.when(e == 0)
        def _():
            rows_second()

        @pl.when(e == SWAP_AT)
        def _():
            rows_swap()

        return carry

    lax.fori_loop(0, EXPERTS, per_expert, 0)
    combine(EXPERTS - 1)

    def finish_all(e, carry):
        finish(e)

        @pl.when(e == TURN_AT)
        def _():
            rows_turn()

        return carry

    lax.fori_loop(0, EXPERTS, finish_all, 0)

    def drain_ring(s, carry):
        for half in range(2):
            for slot in range(SLOTS):
                gather(half, slot, s, origin(half, s)).wait_send()
        return carry

    for half in range(2):
        for slot in range(SLOTS):
            hop16(half, slot, 0, first.at[half, slot]).wait_send()
            for s in range(1, NB):
                hop16(half, slot, s, early.at[half, s - 1, slot]).wait_send()
            hop32(half, slot, NB, turn.at[half, slot]).wait_send()
            for s in range(NB + 1, NZ - 1):
                hop32(half, slot, s, acc.at[half, s - 1 - NB, slot]).wait_send()
    lax.fori_loop(1, NZ - 1, drain_ring, 0)
    for half in range(2):
        for slot in range(SLOTS):
            gather(half, slot, 0, z).wait_send()

    def drain(s, carry):
        for i in range(3):
            spread(s, i).wait_send()
        for half in range(2):
            for i, make in (rows_a(half, s), rows_b(half, s)):

                @pl.when(i != 0)
                def _(make=make):
                    make().wait_send()

        cross(s, 0).wait_send()
        cross(s, 1).wait_send()
        away(s).wait_send()
        return carry

    lax.fori_loop(0, NZ, drain, 0)
    for i in range(3):
        second(i, 0).wait_send()
        second(i, 1).wait_send()

    @pl.when(pair != z)
    def _():
        first_step().wait_send()

    @pl.when(z != 0)
    def _():
        second_step().wait()

    xout[...] = back[...].T


def layer(act, cot, rows, counts, probs, ids, wg, wu, wd):
    dma = pltpu.SemaphoreType.DMA
    vm = pl.BlockSpec(memory_space=pltpu.VMEM)
    sm = pl.BlockSpec(memory_space=pltpu.SMEM)
    hd = DZ // 2
    cols = NXH * NZ * TOK
    block = (EXPERTS, SUB, FP)
    return pl.pallas_call(
        layer_kernel,
        out_shape=(
            jax.ShapeDtypeStruct((EXPERTS, SUB, 2 * FH), F32),
            jax.ShapeDtypeStruct((EXPERTS, SUB, 2 * FH), F32),
            jax.ShapeDtypeStruct((EXPERTS, 2 * FH, SUB), F32),
            jax.ShapeDtypeStruct((TOK, DZ), F32),
        ),
        in_specs=[vm, vm, vm, sm, vm, sm, vm, vm, vm],
        out_specs=(vm,) * 4,
        scratch_shapes=[
            pltpu.VMEM((NZ * DZ, TOK), BF16),
            pltpu.VMEM((8, TOK), F32),
            pltpu.VMEM((8, TOK), F32),
            pltpu.VMEM((8, TOK), jnp.int32),
            pltpu.VMEM(block, BF16),
            pltpu.VMEM((EXPERTS, NXH * NC, SUB, FP), BF16),
            pltpu.VMEM((EXPERTS, FP, DZ), BF16),
            pltpu.VMEM((NZ, DZ, TOK), BF16),
            pltpu.VMEM((NXH, NZ, 8, TOK), F32),
            pltpu.VMEM((NXH, NZ, 8, TOK), jnp.int32),
            pltpu.VMEM((2, DZ, cols), BF16),
            pltpu.VMEM((2, NB, SLOTS, FP, TOK), BF16),
            pltpu.VMEM((2, SLOTS, FP, TOK), BF16),
            pltpu.VMEM((2, NZ - 1 - NB, SLOTS, F3, TOK), F32),
            pltpu.VMEM((2, SLOTS, F3, TOK), F32),
            pltpu.VMEM((2, SLOTS, FP, TOK), F32),
            pltpu.VMEM((SLOTS, DZ, cols), BF16),
            pltpu.VMEM((SLOTS, FP, cols), BF16),
            pltpu.VMEM((NXH, NXL, NY, DZ, TOK), F32),
            pltpu.VMEM((NXH, NXL, NY, DZ, TOK), BF16),
            pltpu.VMEM((EXPERTS, NXH * NC, SUB, FP), F32),
            pltpu.VMEM((2,) + block, F32),
            pltpu.VMEM(block, BF16),
            pltpu.VMEM(block, BF16),
            pltpu.VMEM((3, NXH, NXL, hd, TOK), BF16),
            pltpu.VMEM((3, hd, TOK), F32),
            pltpu.VMEM((3, NY, hd, TOK), BF16),
            pltpu.VMEM((3, hd, TOK), F32),
            pltpu.VMEM((NXH, NXL, hd, TOK), F32),
            pltpu.VMEM((NY, hd, TOK), F32),
            pltpu.VMEM((DZ, TOK), F32),
            pltpu.VMEM((DZ, TOK), F32),
            pltpu.VMEM((DZ, TOK), F32),
        ]
        + [dma((NZ - 1,))] * 6 + [dma((3,))] * 2 + [dma((2,))] * 2 + [dma((EXPERTS,))] * 6
        + [dma((3,))]
        + [dma((NZ, 3))] * 2
        + [dma((2, NZ - 1, SLOTS))] * 4
        + [dma((2, NZ)), dma((3, NXH, NXL)), dma((2, NZ)), dma((3, NY))]
        + [dma((3,))] * 4
        + [dma((2, EXPERTS))] * 2
        + [dma((EXPERTS,))] * 2
        + [dma((2,))] * 2,
        compiler_params=pltpu.CompilerParams(
            collective_id=0, has_side_effects=True, vmem_limit_bytes=VMEM_LIMIT
        ),
        name="layer",
    )(act, cot, rows, counts, probs, ids, wg, wu, wd)


def shards(
    activations, cotangent, expert_ids, slot_rows, slot_counts, route_probs, w_gate, w_up, w_down
):
    grad_gate, grad_up, grad_down, rows = layer(
        activations, cotangent, slot_rows[0], slot_counts, route_probs[0], expert_ids,
        w_gate, w_up, w_down,
    )
    return rows, grad_gate, grad_up, grad_down


def solution(mesh):
    return jax.shard_map(
        shards,
        mesh=mesh,
        in_specs=(
            P("dp", None),
            P("dp", None),
            P("dp", None),
            P("dp", None, None),
            P("dp", None),
            P("dp", None, None),
            P(None, "dp", "expert"),
            P(None, "dp", "expert"),
            P(None, "expert", "dp"),
        ),
        out_specs=(
            P("dp", "expert"),
            P(None, "dp", "expert"),
            P(None, "dp", "expert"),
            P(None, "expert", "dp"),
        ),
        check_vma=False,
    )
```

```python
import jax
import jax.numpy as jnp
from jax import lax
from jax.experimental import pallas as pl
from jax.experimental.pallas import tpu as pltpu
from jax.sharding import PartitionSpec as P

MESH = pl.DeviceIdType.MESH
F32 = jnp.float32
BF16 = jnp.bfloat16

NZ, NXH, NC, NXL, NY = 8, 2, 2, 2, 4
SLOTS = 2
EXPERTS = 8
TOK = 128
SUB = 112
DZ = 448
FH = 152
F3 = 3 * FH
FP = 464
NB = 3
SWAP_AT = 7
TURN_AT = 4
VMEM_LIMIT = 61 * 1024 * 1024


def place():
    ex = lax.axis_index("expert")
    dp = lax.axis_index("dp")
    return ex // NY, ex % NY, dp // 4, (dp // 2) % 2, dp % 2


def device(xl, y, z, xh, c):
    return (xl * NY + y, z * 4 + xh * 2 + c)


def remote(src, dst, ssem, rsem, dev):
    return pltpu.make_async_remote_copy(
        src_ref=src, dst_ref=dst, send_sem=ssem, recv_sem=rsem, device_id=dev, device_id_type=MESH
    )


def greet(devices):
    barrier = pltpu.get_barrier_semaphore()
    for dev in devices:
        pl.semaphore_signal(barrier, inc=1, device_id=dev, device_id_type=MESH)
    pl.semaphore_wait(barrier, len(devices))


def x_peers(xl, y, z, xh, c):
    pos = xh * 2 + xl
    out = []
    for step in range(1, 4):
        to = (pos + step) % 4
        out.append(device(to % 2, y, z, to // 2, c))
    return out


def y_peers(xl, y, z, xh, c):
    return [device(xl, (y + step) % NY, z, xh, c) for step in range(1, NY)]


def z_peers(xl, y, z, xh, c):
    return [device(xl, y, (z + step) % NZ, xh, c) for step in range(1, NZ)]


def layer_kernel(
    act, cot, rows_in, counts, probs, ids, wg, wu, wd, gate, up_out, down_out, back,
    xt, stack, info, numbers, wsrc, w, wt, xin, scale, experts,
    x, early, first, acc, turn, own, dcat, hcat, dx, dxs, dw, wgot, wsnd, wfar,
    a1, a2, b1, b2, sa, sb, done, mid,
    zs, zr, is_, ir, js, jr, ys, yr, ixs, ixr, gs, gr, os_, or_, ps, pr, loc,
    x_s, x_r, rs_s, rs_r, ag_s, ag_r,
    a1s, a1r, b1s, b1r, a2s, a2r, b2s, b2r, ts, tr, fs, fr, ks, kr,
):
    xl, y, z, xh, c = me = place()
    ex = xl * NY + y
    pos = xh * 2 + xl
    hd = DZ // 2
    zp, xp, yp = z_peers(*me), x_peers(*me), y_peers(*me)
    up, down = zp[0], zp[NZ - 2]
    to = (up, down)
    far = device(xl, y, z, 1 - xh, c)
    twin = device(xl, y, z, xh, 1 - c)
    part = pl.ds(pl.multiple_of(y * SUB, SUB), SUB)
    mine = 2 * xh + c
    other = 2 * (1 - xh) + c
    pair = (ex + NZ - z) % NZ
    along = device(xl, y, pair, xh, c)
    across = device(pair // NY, pair % NY, z, xh, c)
    before = (ex + z) % NZ
    source = device(before // NY, before % NY, z, xh, c)
    barrier = pltpu.get_barrier_semaphore()
    peers = zp + xp + yp + [twin]
    for dev in peers:
        pl.semaphore_signal(barrier, inc=1, device_id=dev, device_id_type=MESH)

    @pl.when(z != 0)
    def _():
        pl.semaphore_signal(barrier, inc=1, device_id=across, device_id_type=MESH)
        pl.semaphore_signal(barrier, inc=1, device_id=source, device_id_type=MESH)

    def pack(e, carry):
        g = wg[e].astype(F32)
        u = wu[e].astype(F32)
        d = wd[e].astype(F32)
        both = []
        for i in range(NXH):
            pieces = [v[i * FH : (i + 1) * FH] for v in (g, u, d)]
            pieces.append(jnp.zeros((FP - F3, SUB), F32))
            both.append(jnp.concatenate(pieces, axis=0))
        wsrc[e] = jnp.where(xh == 0, both[1], both[0]).T.astype(BF16)
        w[e, mine] = jnp.where(xh == 0, both[0], both[1]).T.astype(BF16)
        return carry

    lax.fori_loop(0, EXPERTS, pack, 0)
    pl.semaphore_wait(barrier, len(peers) + jnp.where(z != 0, 2, 0))

    wgone = []
    for e in range(EXPERTS):
        wgone.append(remote(wsrc.at[e], w.at[e, mine], gs.at[e], gr.at[e], far))
        wgone[-1].start()
    wown = []
    for e in range(EXPERTS):
        wown.append(remote(w.at[e, mine], w.at[e, mine], os_.at[e], or_.at[e], twin))
        wown[-1].start()

    def turn_rows(j, carry):
        cols = pl.ds(pl.multiple_of(j * TOK, TOK), TOK)
        xt[cols, :] = jnp.where(xl == 0, act[:, cols], cot[:, cols]).T
        return carry

    lax.fori_loop(0, NZ * DZ // TOK, turn_rows, 0)

    def piece(gz):
        return xt.at[pl.ds(pl.multiple_of(gz * DZ + y * SUB, 16), SUB)]

    cz = []
    for i in range(NZ - 1):
        cz.append(remote(piece((z + i + 1) % NZ), xin.at[z, part], zs.at[i], zr.at[i], zp[i]))
        cz[-1].start()

    lane = lax.broadcasted_iota(jnp.int32, (1, TOK), 1)
    column = lax.broadcasted_iota(jnp.int32, (TOK, TOK), 1).astype(F32)
    for slot in range(SLOTS):
        stack[slot : slot + 1, :] = rows_in[slot : slot + 1, :].astype(F32)
        stack[2 + slot : 3 + slot, :] = jnp.where(
            lane < counts[0, slot], probs[slot : slot + 1, :], 0.0
        )
    stack[4:8, :] = jnp.zeros((4, TOK), F32)
    turned = stack[...].T
    info[4:8, :] = jnp.zeros((4, TOK), F32)
    numbers[...] = jnp.zeros((8, TOK), jnp.int32)
    for slot in range(SLOTS):
        hit = turned[:, slot : slot + 1] == column
        info[slot : slot + 1, :] = jnp.sum(
            jnp.where(hit, turned[:, 2 + slot : 3 + slot], 0.0), axis=0, keepdims=True
        )
        number = jnp.full((1, TOK), ids[0, slot], jnp.int32)
        numbers[slot : slot + 1, :] = number
        info[2 + slot : 3 + slot, :] = number.astype(F32)
    ci = []
    for i in range(NZ - 1):
        ci.append(remote(info, scale.at[xh, z], is_.at[i], ir.at[i], zp[i]))
        ci[-1].start()
        ci.append(remote(numbers, experts.at[xh, z], js.at[i], jr.at[i], zp[i]))
        ci[-1].start()
    here = [
        pltpu.make_async_copy(piece(z), xin.at[z, part], loc.at[0]),
        pltpu.make_async_copy(info, scale.at[xh, z], loc.at[1]),
        pltpu.make_async_copy(numbers, experts.at[xh, z], loc.at[2]),
    ]
    for h in here:
        h.start()
    for h in here:
        h.wait()
    for k in cz:
        k.wait()
    cy = []
    for i in range(3):
        cy.append(remote(xin.at[:, part], xin.at[:, part], ys.at[i], yr.at[i], yp[i]))
        cy[-1].start()
    for k in ci:
        k.wait()
    cinf = [
        remote(scale.at[xh], scale.at[xh], ixs.at[0], ixr.at[0], far),
        remote(experts.at[xh], experts.at[xh], ixs.at[1], ixr.at[1], far),
    ]
    for k in cinf:
        k.start()
    for k in cy:
        k.wait()

    def lanes(half, gz):
        return pl.ds(pl.multiple_of((half * NZ + gz) * TOK, TOK), TOK)

    def chunk(half, s):
        return jnp.where(half == 0, z + 2 * NZ - 1 - s, z + 1 + s) % NZ

    def spread(s, i):
        gz = chunk(xh, s)
        return remote(
            xin.at[gz], x.at[xl, :, lanes(xh, gz)], x_s.at[s, i], x_r.at[s, i], xp[i]
        )

    def spread_all(s):
        for i in range(3):
            spread(s, i).start()

    def await_all(s):
        gz = chunk(xh, s)
        x[xl, :, lanes(xh, gz)] = xin[gz]
        for i in range(3):
            spread(s, i).wait_recv()
    spread_all(0)
    spread_all(1)
    wpass = []
    for e in range(EXPERTS):
        wgone[e].wait_recv()
        wpass.append(remote(w.at[e, other], w.at[e, other], ps.at[e], pr.at[e], twin))
        wpass[-1].start()
    for e in range(EXPERTS):
        wown[e].wait_recv()
        wpass[e].wait_recv()
        wt[e] = w[e].reshape(DZ, FP).T
    for k in cinf:
        k.wait()
    for k in wgone + wown + wpass:
        k.wait_send()

    def partial(half, gz):
        at = lanes(half, gz)
        xt = x[0, :, at]
        dyt = x[1, :, at].astype(F32)
        for slot in range(SLOTS):
            e = experts[half, gz, slot, 0]
            dys = (dyt * scale[half, gz, pl.ds(slot, 1), :]).astype(BF16)
            dcat[slot, :, at] = dys
            gu = jnp.dot(wt[e, 0 : 2 * FH, :], xt, preferred_element_type=F32)
            dh = jnp.dot(wt[e, 2 * FH : FP, :], dys, preferred_element_type=F32)
            own[half, slot, 0 : 2 * FH, :] = gu
            own[half, slot, 2 * FH : FP, :] = dh

    def hop(half, slot, s, src, dst):
        return remote(src, dst, rs_s.at[half, s, slot], rs_r.at[half, s, slot], to[half])

    def hop16(half, slot, s, src):
        return hop(half, slot, s, src, early.at[half, s, slot])

    def hop32(half, slot, s, src):
        return hop(half, slot, s, src, acc.at[half, s - NB, slot])

    await_all(0)
    for half in range(2):
        partial(half, chunk(half, 0))
        for slot in range(SLOTS):
            first[half, slot] = own[half, slot].astype(BF16)
            hop16(half, slot, 0, first.at[half, slot]).start()

    def fresh(s):
        spread_all(s + 1)
        await_all(s)
        for half in range(2):
            partial(half, chunk(half, s))

    def ring16(s, carry):
        fresh(s)
        for slot in range(SLOTS):
            for half in range(2):
                here = early.at[half, s - 1, slot]
                hop16(half, slot, s - 1, here).wait_recv()
                total = early[half, s - 1, slot].astype(F32) + own[half, slot]
                early[half, s - 1, slot] = total.astype(BF16)
                hop16(half, slot, s, here).start()
        return carry

    lax.fori_loop(1, NB, ring16, 0)
    fresh(NB)
    for slot in range(SLOTS):
        for half in range(2):
            here = early.at[half, NB - 1, slot]
            hop16(half, slot, NB - 1, here).wait_recv()
            turn[half, slot] = early[half, NB - 1, slot, 0:F3].astype(F32) + own[half, slot, 0:F3]
            hop32(half, slot, NB, turn.at[half, slot]).start()

    def ring32(s, carry):
        fresh(s)
        for slot in range(SLOTS):
            for half in range(2):
                here = acc.at[half, s - 1 - NB, slot]
                hop32(half, slot, s - 1, here).wait_recv()
                acc[half, s - 1 - NB, slot] = acc[half, s - 1 - NB, slot] + own[half, slot, 0:F3]
                hop32(half, slot, s, here).start()
        return carry

    lax.fori_loop(NB + 1, NZ - 1, ring32, 0)
    await_all(NZ - 1)

    def gather(half, slot, s, gz):
        ref = hcat.at[slot, :, lanes(half, gz)]
        return remote(ref, ref, ag_s.at[half, s, slot], ag_r.at[half, s, slot], to[half])

    def origin(half, s):
        return (z + NZ - s) % NZ if half == 0 else (z + s) % NZ

    def spot(gz):
        return (gz + z) % NZ

    def rows_a(half, gz):
        q = spot(gz)
        i = (q % NY - y + NY) % NY
        src = dxs.at[half, q // NY, q % NY, pl.ds(0, hd)]
        return i, lambda: remote(
            src, a1.at[i - 1, half, q // NY], a1s.at[half, gz], a1r.at[i - 1, half, q // NY],
            device(xl, q % NY, z, xh, c),
        )

    def rows_b(half, gz):
        q = spot(gz)
        i = (half * 2 + q // NY - pos + 4) % 4
        src = dxs.at[half, q // NY, q % NY, pl.ds(hd, hd)]
        return i, lambda: remote(
            src, b1.at[i - 1, q % NY], b1s.at[half, gz], b1r.at[i - 1, q % NY],
            device(q // NY, y, z, half, c),
        )

    def rows(half, gz):
        total = jnp.zeros((DZ, TOK), F32)
        for slot in range(SLOTS):
            e = experts[half, gz, slot, 0]
            hs = hcat[slot, 0 : 2 * FH, lanes(half, gz)]
            total = total + jnp.dot(
                w[e, :, :, 0 : 2 * FH].reshape(DZ, 2 * FH), hs, preferred_element_type=F32
            )
        q = spot(gz)
        dx[half, q // NY, q % NY] = total
        dxs[half, q // NY, q % NY] = total.astype(BF16)
        for i, make in (rows_a(half, gz), rows_b(half, gz)):

            @pl.when(i != 0)
            def _(make=make):
                make().start()

    for half in range(2):
        partial(half, z)
    for slot in range(SLOTS):
        for half in range(2):
            last = acc.at[half, NZ - 2 - NB, slot]
            hop32(half, slot, NZ - 2, last).wait_recv()
            g = acc[half, NZ - 2 - NB, slot, 0:FH, :] + own[half, slot, 0:FH, :]
            u = acc[half, NZ - 2 - NB, slot, FH : 2 * FH, :] + own[half, slot, FH : 2 * FH, :]
            dh = acc[half, NZ - 2 - NB, slot, 2 * FH : F3, :] + own[half, slot, 2 * FH : F3, :]
            sig = 1.0 / (1.0 + jnp.exp(-g))
            act = g * sig
            dg = dh * u * sig * (1.0 + g * (1.0 - sig))
            du = dh * act
            hid = act * u
            hcat[slot, 0 : 2 * FH, lanes(half, z)] = jnp.concatenate([dg, du], axis=0).astype(BF16)
            hcat[slot, 2 * FH : FP, lanes(half, z)] = jnp.concatenate(
                [hid, jnp.zeros((FP - F3, TOK), F32)], axis=0
            ).astype(BF16)
            gather(half, slot, 0, z).start()
    for half in range(2):
        rows(half, z)

    def pass_on(s, carry):
        for slot in range(SLOTS):
            for half in range(2):
                gather(half, slot, s - 1, origin(half, s)).wait_recv()
                gather(half, slot, s, origin(half, s)).start()
        for half in range(2):
            rows(half, origin(half, s))
        return carry

    lax.fori_loop(1, NZ - 1, pass_on, 0)
    for half in range(2):
        for slot in range(SLOTS):
            gather(half, slot, NZ - 2, origin(half, NZ - 1)).wait_recv()
        rows(half, origin(half, NZ - 1))

    cols = NXH * NZ * TOK
    def expert_row(slot):
        return jnp.concatenate(
            [
                scale[i // NZ, i % NZ, 2 + slot : 3 + slot, :]
                for i in range(NXH * NZ)
            ],
            axis=1,
        )

    id0, id1 = expert_row(0), expert_row(1)
    nt = (((1,), (1,)), ((), ()))

    def weights(e):
        is0 = jnp.broadcast_to(id0 == e.astype(F32), (16, cols))
        is1 = jnp.broadcast_to(id1 == e.astype(F32), (16, cols))
        zero = jnp.zeros((16, cols), BF16)

        def pick(pair, n):
            return jnp.concatenate(
                [
                    jnp.where(
                        is0,
                        pair[0, r * 16 : (r + 1) * 16, :],
                        jnp.where(is1, pair[1, r * 16 : (r + 1) * 16, :], zero),
                    )
                    for r in range(n // 16)
                ],
                axis=0,
            )

        hs = pick(hcat, FP)
        ds = pick(dcat, DZ)
        gu = lax.dot_general(x[0], hs, nt, preferred_element_type=F32)
        dn = lax.dot_general(ds, hs[256:], nt, preferred_element_type=F32)
        column = lax.broadcasted_iota(jnp.int32, (DZ, FP - 256), 1)
        tail = jnp.where(column < 2 * FH - 256, gu[:, 256:], dn)
        for q in range(NXH * NC):
            dw[e, q, :, 0:256] = gu[q * SUB : (q + 1) * SUB, 0:256]
            dw[e, q, :, 256:FP] = tail[q * SUB : (q + 1) * SUB]

    def cross(e, i):
        blk = (1 - xh) if i == 0 else xh
        return remote(dw.at[e, 2 * blk + 1 - c], wgot.at[i, e], ts.at[i, e], tr.at[i, e], twin)

    def away(e):
        return remote(wsnd.at[e], wfar.at[e], fs.at[e], fr.at[e], far)

    def combine(e):
        cross(e, 0).wait_recv()
        wsnd[e] = (dw[e, 2 * (1 - xh) + c] + wgot[0, e]).astype(BF16)
        away(e).start()
        cross(e, 1).wait_recv()
        wgot[1, e] = dw[e, 2 * xh + c] + wgot[1, e]

    def second(i, kind):
        if kind == 0:
            t = (pos + i + 1) % 4
            return remote(sa.at[t // 2, t % 2], a2.at[i], a2s.at[i], a2r.at[i], xp[i])
        t = (y + i + 1) % NY
        return remote(sb.at[t], b2.at[i], b2s.at[i], b2r.at[i], yp[i])

    def rows_second():
        for i in range(3):
            for j in range(NXH):
                for k in range(NXL):
                    remote(
                        dxs.at[0, 0, 0, pl.ds(0, hd)], a1.at[i, j, k], a1s.at[0, 0],
                        a1r.at[i, j, k], up,
                    ).wait_recv()
        for j in range(NXH):
            for k in range(NXL):
                sa[j, k] = dx[j, k, y, 0:hd] + (
                    a1[0, j, k].astype(F32) + a1[1, j, k].astype(F32) + a1[2, j, k].astype(F32)
                )
        for i in range(3):
            second(i, 0).start()
        for i in range(3):
            for j in range(NY):
                remote(
                    dxs.at[0, 0, 0, pl.ds(hd, hd)], b1.at[i, j], b1s.at[0, 0], b1r.at[i, j], up
                ).wait_recv()
        for j in range(NY):
            sb[j] = dx[xh, xl, j, hd:DZ] + (
                b1[0, j].astype(F32) + b1[1, j].astype(F32) + b1[2, j].astype(F32)
            )
        for i in range(3):
            second(i, 1).start()

    def rows_swap():
        for i in range(3):
            second(i, 0).wait_recv()
        done[0:hd] = sa[xh, xl] + a2[0] + a2[1] + a2[2]
        for i in range(3):
            second(i, 1).wait_recv()
        done[hd:DZ] = sb[y] + b2[0] + b2[1] + b2[2]

        @pl.when(pair != z)
        def _():
            first_step().start()

    def first_step():
        return remote(done, mid, ks.at[0], kr.at[0], along)

    def second_step():
        return remote(mid, back, ks.at[1], kr.at[1], across)

    def rows_turn():
        @pl.when(pair != z)
        def _():
            first_step().wait_recv()

        @pl.when(pair == z)
        def _():
            mid[...] = done[...]

        @pl.when(z != 0)
        def _():
            second_step().start()

        @pl.when(z == 0)
        def _():
            back[...] = mid[...]

    def finish(e):
        away(e).wait_recv()
        ours = wgot[1, e]
        theirs = wfar[e].astype(F32)
        low = jnp.where(xh == 0, ours, theirs).T
        high = jnp.where(xh == 0, theirs, ours).T
        for i, out in enumerate((gate, up_out, down_out)):
            out[e, 0:FH, :] = low[i * FH : (i + 1) * FH]
            out[e, FH : 2 * FH, :] = high[i * FH : (i + 1) * FH]

    def per_expert(e, carry):
        weights(e)
        cross(e, 0).start()
        cross(e, 1).start()

        @pl.when(e > 0)
        def _():
            combine(e - 1)

        @pl.when(e == 0)
        def _():
            rows_second()

        @pl.when(e == SWAP_AT)
        def _():
            rows_swap()

        return carry

    lax.fori_loop(0, EXPERTS, per_expert, 0)
    combine(EXPERTS - 1)

    def finish_all(e, carry):
        finish(e)

        @pl.when(e == TURN_AT)
        def _():
            rows_turn()

        return carry

    lax.fori_loop(0, EXPERTS, finish_all, 0)

    def drain_ring(s, carry):
        for half in range(2):
            for slot in range(SLOTS):
                gather(half, slot, s, origin(half, s)).wait_send()
        return carry

    for half in range(2):
        for slot in range(SLOTS):
            hop16(half, slot, 0, first.at[half, slot]).wait_send()
            for s in range(1, NB):
                hop16(half, slot, s, early.at[half, s - 1, slot]).wait_send()
            hop32(half, slot, NB, turn.at[half, slot]).wait_send()
            for s in range(NB + 1, NZ - 1):
                hop32(half, slot, s, acc.at[half, s - 1 - NB, slot]).wait_send()
    lax.fori_loop(1, NZ - 1, drain_ring, 0)
    for half in range(2):
        for slot in range(SLOTS):
            gather(half, slot, 0, z).wait_send()

    def drain(s, carry):
        for i in range(3):
            spread(s, i).wait_send()
        for half in range(2):
            for i, make in (rows_a(half, s), rows_b(half, s)):

                @pl.when(i != 0)
                def _(make=make):
                    make().wait_send()

        cross(s, 0).wait_send()
        cross(s, 1).wait_send()
        away(s).wait_send()
        return carry

    lax.fori_loop(0, NZ, drain, 0)
    for i in range(3):
        second(i, 0).wait_send()
        second(i, 1).wait_send()

    @pl.when(pair != z)
    def _():
        first_step().wait_send()

    @pl.when(z != 0)
    def _():
        second_step().wait()


def layer(act, cot, rows, counts, probs, ids, wg, wu, wd):
    dma = pltpu.SemaphoreType.DMA
    vm = pl.BlockSpec(memory_space=pltpu.VMEM)
    sm = pl.BlockSpec(memory_space=pltpu.SMEM)
    hd = DZ // 2
    cols = NXH * NZ * TOK
    block = (EXPERTS, SUB, FP)
    return pl.pallas_call(
        layer_kernel,
        out_shape=(
            jax.ShapeDtypeStruct((EXPERTS, 2 * FH, SUB), F32),
            jax.ShapeDtypeStruct((EXPERTS, 2 * FH, SUB), F32),
            jax.ShapeDtypeStruct((EXPERTS, 2 * FH, SUB), F32),
            jax.ShapeDtypeStruct((DZ, TOK), F32),
        ),
        in_specs=[vm, vm, vm, sm, vm, sm, vm, vm, vm],
        out_specs=(vm,) * 4,
        scratch_shapes=[
            pltpu.VMEM((NZ * DZ, TOK), BF16),
            pltpu.VMEM((8, TOK), F32),
            pltpu.VMEM((8, TOK), F32),
            pltpu.VMEM((8, TOK), jnp.int32),
            pltpu.VMEM(block, BF16),
            pltpu.VMEM((EXPERTS, NXH * NC, SUB, FP), BF16),
            pltpu.VMEM((EXPERTS, FP, DZ), BF16),
            pltpu.VMEM((NZ, DZ, TOK), BF16),
            pltpu.VMEM((NXH, NZ, 8, TOK), F32),
            pltpu.VMEM((NXH, NZ, 8, TOK), jnp.int32),
            pltpu.VMEM((2, DZ, cols), BF16),
            pltpu.VMEM((2, NB, SLOTS, FP, TOK), BF16),
            pltpu.VMEM((2, SLOTS, FP, TOK), BF16),
            pltpu.VMEM((2, NZ - 1 - NB, SLOTS, F3, TOK), F32),
            pltpu.VMEM((2, SLOTS, F3, TOK), F32),
            pltpu.VMEM((2, SLOTS, FP, TOK), F32),
            pltpu.VMEM((SLOTS, DZ, cols), BF16),
            pltpu.VMEM((SLOTS, FP, cols), BF16),
            pltpu.VMEM((NXH, NXL, NY, DZ, TOK), F32),
            pltpu.VMEM((NXH, NXL, NY, DZ, TOK), BF16),
            pltpu.VMEM((EXPERTS, NXH * NC, SUB, FP), F32),
            pltpu.VMEM((2,) + block, F32),
            pltpu.VMEM(block, BF16),
            pltpu.VMEM(block, BF16),
            pltpu.VMEM((3, NXH, NXL, hd, TOK), BF16),
            pltpu.VMEM((3, hd, TOK), F32),
            pltpu.VMEM((3, NY, hd, TOK), BF16),
            pltpu.VMEM((3, hd, TOK), F32),
            pltpu.VMEM((NXH, NXL, hd, TOK), F32),
            pltpu.VMEM((NY, hd, TOK), F32),
            pltpu.VMEM((DZ, TOK), F32),
            pltpu.VMEM((DZ, TOK), F32),
        ]
        + [dma((NZ - 1,))] * 6 + [dma((3,))] * 2 + [dma((2,))] * 2 + [dma((EXPERTS,))] * 6
        + [dma((3,))]
        + [dma((NZ, 3))] * 2
        + [dma((2, NZ - 1, SLOTS))] * 4
        + [dma((2, NZ)), dma((3, NXH, NXL)), dma((2, NZ)), dma((3, NY))]
        + [dma((3,))] * 4
        + [dma((2, EXPERTS))] * 2
        + [dma((EXPERTS,))] * 2
        + [dma((2,))] * 2,
        compiler_params=pltpu.CompilerParams(
            collective_id=0, has_side_effects=True, vmem_limit_bytes=VMEM_LIMIT
        ),
        name="layer",
    )(act, cot, rows, counts, probs, ids, wg, wu, wd)


def shards(
    activations, cotangent, expert_ids, slot_rows, slot_counts, route_probs, w_gate, w_up, w_down
):
    grad_gate, grad_up, grad_down, rows = layer(
        activations, cotangent, slot_rows[0], slot_counts, route_probs[0], expert_ids,
        w_gate.transpose(0, 2, 1), w_up.transpose(0, 2, 1), w_down,
    )
    return rows.T, grad_gate.transpose(0, 2, 1), grad_up.transpose(0, 2, 1), grad_down


def solution(mesh):
    return jax.shard_map(
        shards,
        mesh=mesh,
        in_specs=(
            P("dp", None),
            P("dp", None),
            P("dp", None),
            P("dp", None, None),
            P("dp", None),
            P("dp", None, None),
            P(None, "dp", "expert"),
            P(None, "dp", "expert"),
            P(None, "expert", "dp"),
        ),
        out_specs=(
            P("dp", "expert"),
            P(None, "dp", "expert"),
            P(None, "dp", "expert"),
            P(None, "expert", "dp"),
        ),
        check_vma=False,
    )
```

```python
import jax
import jax.numpy as jnp
from jax import lax
from jax.experimental import pallas as pl
from jax.experimental.pallas import tpu as pltpu
from jax.sharding import PartitionSpec as P

MESH = pl.DeviceIdType.MESH
F32 = jnp.float32
BF16 = jnp.bfloat16

NZ, NXH, NC, NXL, NY = 8, 2, 2, 2, 4
SLOTS = 2
EXPERTS = 8
TOK = 128
SUB = 112
DZ = 448
FH = 152
F3 = 3 * FH
FP = 464
NB = 4
SWAP_AT = 7
TURN_AT = 4
VMEM_LIMIT = 61 * 1024 * 1024


def place():
    ex = lax.axis_index("expert")
    dp = lax.axis_index("dp")
    return ex // NY, ex % NY, dp // 4, (dp // 2) % 2, dp % 2


def device(xl, y, z, xh, c):
    return (xl * NY + y, z * 4 + xh * 2 + c)


def remote(src, dst, ssem, rsem, dev):
    return pltpu.make_async_remote_copy(
        src_ref=src, dst_ref=dst, send_sem=ssem, recv_sem=rsem, device_id=dev, device_id_type=MESH
    )


def greet(devices):
    barrier = pltpu.get_barrier_semaphore()
    for dev in devices:
        pl.semaphore_signal(barrier, inc=1, device_id=dev, device_id_type=MESH)
    pl.semaphore_wait(barrier, len(devices))


def x_peers(xl, y, z, xh, c):
    pos = xh * 2 + xl
    out = []
    for step in range(1, 4):
        to = (pos + step) % 4
        out.append(device(to % 2, y, z, to // 2, c))
    return out


def y_peers(xl, y, z, xh, c):
    return [device(xl, (y + step) % NY, z, xh, c) for step in range(1, NY)]


def z_peers(xl, y, z, xh, c):
    return [device(xl, y, (z + step) % NZ, xh, c) for step in range(1, NZ)]


def layer_kernel(
    act, cot, rows_in, counts, probs, ids, wg, wu, wd, gate, up_out, down_out, back,
    xt, stack, info, numbers, wsrc, w, wt, xin, scale, experts,
    x, early, first, acc, turn, own, dcat, hcat, dx, dxs, dw, wgot, wsnd, wfar,
    a1, a2, b1, b2, sa, sb, done, mid,
    zs, zr, is_, ir, js, jr, ys, yr, ixs, ixr, gs, gr, os_, or_, ps, pr, loc,
    x_s, x_r, rs_s, rs_r, ag_s, ag_r,
    a1s, a1r, b1s, b1r, a2s, a2r, b2s, b2r, ts, tr, fs, fr, ks, kr,
):
    xl, y, z, xh, c = me = place()
    ex = xl * NY + y
    pos = xh * 2 + xl
    hd = DZ // 2
    zp, xp, yp = z_peers(*me), x_peers(*me), y_peers(*me)
    up, down = zp[0], zp[NZ - 2]
    to = (up, down)
    far = device(xl, y, z, 1 - xh, c)
    twin = device(xl, y, z, xh, 1 - c)
    part = pl.ds(pl.multiple_of(y * SUB, SUB), SUB)
    mine = 2 * xh + c
    other = 2 * (1 - xh) + c
    pair = (ex + NZ - z) % NZ
    along = device(xl, y, pair, xh, c)
    across = device(pair // NY, pair % NY, z, xh, c)
    before = (ex + z) % NZ
    source = device(before // NY, before % NY, z, xh, c)
    barrier = pltpu.get_barrier_semaphore()
    peers = zp + xp + yp + [twin]
    for dev in peers:
        pl.semaphore_signal(barrier, inc=1, device_id=dev, device_id_type=MESH)

    @pl.when(z != 0)
    def _():
        pl.semaphore_signal(barrier, inc=1, device_id=across, device_id_type=MESH)
        pl.semaphore_signal(barrier, inc=1, device_id=source, device_id_type=MESH)

    def pack(e, carry):
        g = wg[e].astype(F32)
        u = wu[e].astype(F32)
        d = wd[e].astype(F32)
        both = []
        for i in range(NXH):
            pieces = [v[i * FH : (i + 1) * FH] for v in (g, u, d)]
            pieces.append(jnp.zeros((FP - F3, SUB), F32))
            both.append(jnp.concatenate(pieces, axis=0))
        wsrc[e] = jnp.where(xh == 0, both[1], both[0]).T.astype(BF16)
        w[e, mine] = jnp.where(xh == 0, both[0], both[1]).T.astype(BF16)
        return carry

    lax.fori_loop(0, EXPERTS, pack, 0)
    pl.semaphore_wait(barrier, len(peers) + jnp.where(z != 0, 2, 0))

    wgone = []
    for e in range(EXPERTS):
        wgone.append(remote(wsrc.at[e], w.at[e, mine], gs.at[e], gr.at[e], far))
        wgone[-1].start()
    wown = []
    for e in range(EXPERTS):
        wown.append(remote(w.at[e, mine], w.at[e, mine], os_.at[e], or_.at[e], twin))
        wown[-1].start()

    def turn_rows(j, carry):
        cols = pl.ds(pl.multiple_of(j * TOK, TOK), TOK)
        xt[cols, :] = jnp.where(xl == 0, act[:, cols], cot[:, cols]).T
        return carry

    lax.fori_loop(0, NZ * DZ // TOK, turn_rows, 0)

    def piece(gz):
        return xt.at[pl.ds(pl.multiple_of(gz * DZ + y * SUB, 16), SUB)]

    cz = []
    for i in range(NZ - 1):
        cz.append(remote(piece((z + i + 1) % NZ), xin.at[z, part], zs.at[i], zr.at[i], zp[i]))
        cz[-1].start()

    lane = lax.broadcasted_iota(jnp.int32, (1, TOK), 1)
    column = lax.broadcasted_iota(jnp.int32, (TOK, TOK), 1).astype(F32)
    for slot in range(SLOTS):
        stack[slot : slot + 1, :] = rows_in[slot : slot + 1, :].astype(F32)
        stack[2 + slot : 3 + slot, :] = jnp.where(
            lane < counts[0, slot], probs[slot : slot + 1, :], 0.0
        )
    stack[4:8, :] = jnp.zeros((4, TOK), F32)
    turned = stack[...].T
    info[4:8, :] = jnp.zeros((4, TOK), F32)
    numbers[...] = jnp.zeros((8, TOK), jnp.int32)
    for slot in range(SLOTS):
        hit = turned[:, slot : slot + 1] == column
        info[slot : slot + 1, :] = jnp.sum(
            jnp.where(hit, turned[:, 2 + slot : 3 + slot], 0.0), axis=0, keepdims=True
        )
        number = jnp.full((1, TOK), ids[0, slot], jnp.int32)
        numbers[slot : slot + 1, :] = number
        info[2 + slot : 3 + slot, :] = number.astype(F32)
    ci = []
    for i in range(NZ - 1):
        ci.append(remote(info, scale.at[xh, z], is_.at[i], ir.at[i], zp[i]))
        ci[-1].start()
        ci.append(remote(numbers, experts.at[xh, z], js.at[i], jr.at[i], zp[i]))
        ci[-1].start()
    here = [
        pltpu.make_async_copy(piece(z), xin.at[z, part], loc.at[0]),
        pltpu.make_async_copy(info, scale.at[xh, z], loc.at[1]),
        pltpu.make_async_copy(numbers, experts.at[xh, z], loc.at[2]),
    ]
    for h in here:
        h.start()
    for h in here:
        h.wait()
    for k in cz:
        k.wait()
    cy = []
    for i in range(3):
        cy.append(remote(xin.at[:, part], xin.at[:, part], ys.at[i], yr.at[i], yp[i]))
        cy[-1].start()
    for k in ci:
        k.wait()
    cinf = [
        remote(scale.at[xh], scale.at[xh], ixs.at[0], ixr.at[0], far),
        remote(experts.at[xh], experts.at[xh], ixs.at[1], ixr.at[1], far),
    ]
    for k in cinf:
        k.start()
    for k in cy:
        k.wait()

    def lanes(half, gz):
        return pl.ds(pl.multiple_of((half * NZ + gz) * TOK, TOK), TOK)

    def chunk(half, s):
        return jnp.where(half == 0, z + 2 * NZ - 1 - s, z + 1 + s) % NZ

    def spread(s, i):
        gz = chunk(xh, s)
        return remote(
            xin.at[gz], x.at[xl, :, lanes(xh, gz)], x_s.at[s, i], x_r.at[s, i], xp[i]
        )

    def spread_all(s):
        for i in range(3):
            spread(s, i).start()

    def await_all(s):
        gz = chunk(xh, s)
        x[xl, :, lanes(xh, gz)] = xin[gz]
        for i in range(3):
            spread(s, i).wait_recv()
    spread_all(0)
    spread_all(1)
    wpass = []
    for e in range(EXPERTS):
        wgone[e].wait_recv()
        wpass.append(remote(w.at[e, other], w.at[e, other], ps.at[e], pr.at[e], twin))
        wpass[-1].start()
    for e in range(EXPERTS):
        wown[e].wait_recv()
        wpass[e].wait_recv()
        wt[e] = w[e].reshape(DZ, FP).T
    for k in cinf:
        k.wait()
    for k in wgone + wown + wpass:
        k.wait_send()

    def partial(half, gz):
        at = lanes(half, gz)
        xt = x[0, :, at]
        dyt = x[1, :, at].astype(F32)
        for slot in range(SLOTS):
            e = experts[half, gz, slot, 0]
            dys = (dyt * scale[half, gz, pl.ds(slot, 1), :]).astype(BF16)
            dcat[slot, :, at] = dys
            gu = jnp.dot(wt[e, 0 : 2 * FH, :], xt, preferred_element_type=F32)
            dh = jnp.dot(wt[e, 2 * FH : FP, :], dys, preferred_element_type=F32)
            own[half, slot, 0 : 2 * FH, :] = gu
            own[half, slot, 2 * FH : FP, :] = dh

    def hop(half, slot, s, src, dst):
        return remote(src, dst, rs_s.at[half, s, slot], rs_r.at[half, s, slot], to[half])

    def hop16(half, slot, s, src):
        return hop(half, slot, s, src, early.at[half, s, slot])

    def hop32(half, slot, s, src):
        return hop(half, slot, s, src, acc.at[half, s - NB, slot])

    await_all(0)
    for half in range(2):
        partial(half, chunk(half, 0))
        for slot in range(SLOTS):
            first[half, slot] = own[half, slot].astype(BF16)
            hop16(half, slot, 0, first.at[half, slot]).start()

    def fresh(s):
        spread_all(s + 1)
        await_all(s)
        for half in range(2):
            partial(half, chunk(half, s))

    def ring16(s, carry):
        fresh(s)
        for slot in range(SLOTS):
            for half in range(2):
                here = early.at[half, s - 1, slot]
                hop16(half, slot, s - 1, here).wait_recv()
                total = early[half, s - 1, slot].astype(F32) + own[half, slot]
                early[half, s - 1, slot] = total.astype(BF16)
                hop16(half, slot, s, here).start()
        return carry

    lax.fori_loop(1, NB, ring16, 0)
    fresh(NB)
    for slot in range(SLOTS):
        for half in range(2):
            here = early.at[half, NB - 1, slot]
            hop16(half, slot, NB - 1, here).wait_recv()
            turn[half, slot] = early[half, NB - 1, slot, 0:F3].astype(F32) + own[half, slot, 0:F3]
            hop32(half, slot, NB, turn.at[half, slot]).start()

    def ring32(s, carry):
        fresh(s)
        for slot in range(SLOTS):
            for half in range(2):
                here = acc.at[half, s - 1 - NB, slot]
                hop32(half, slot, s - 1, here).wait_recv()
                acc[half, s - 1 - NB, slot] = acc[half, s - 1 - NB, slot] + own[half, slot, 0:F3]
                hop32(half, slot, s, here).start()
        return carry

    lax.fori_loop(NB + 1, NZ - 1, ring32, 0)
    await_all(NZ - 1)

    def gather(half, slot, s, gz):
        ref = hcat.at[slot, :, lanes(half, gz)]
        return remote(ref, ref, ag_s.at[half, s, slot], ag_r.at[half, s, slot], to[half])

    def origin(half, s):
        return (z + NZ - s) % NZ if half == 0 else (z + s) % NZ

    def spot(gz):
        return (gz + z) % NZ

    def rows_a(half, gz):
        q = spot(gz)
        i = (q % NY - y + NY) % NY
        src = dxs.at[half, q // NY, q % NY, pl.ds(0, hd)]
        return i, lambda: remote(
            src, a1.at[i - 1, half, q // NY], a1s.at[half, gz], a1r.at[i - 1, half, q // NY],
            device(xl, q % NY, z, xh, c),
        )

    def rows_b(half, gz):
        q = spot(gz)
        i = (half * 2 + q // NY - pos + 4) % 4
        src = dxs.at[half, q // NY, q % NY, pl.ds(hd, hd)]
        return i, lambda: remote(
            src, b1.at[i - 1, q % NY], b1s.at[half, gz], b1r.at[i - 1, q % NY],
            device(q // NY, y, z, half, c),
        )

    def rows(half, gz):
        total = jnp.zeros((DZ, TOK), F32)
        for slot in range(SLOTS):
            e = experts[half, gz, slot, 0]
            hs = hcat[slot, 0 : 2 * FH, lanes(half, gz)]
            total = total + jnp.dot(
                w[e, :, :, 0 : 2 * FH].reshape(DZ, 2 * FH), hs, preferred_element_type=F32
            )
        q = spot(gz)
        dx[half, q // NY, q % NY] = total
        dxs[half, q // NY, q % NY] = total.astype(BF16)
        for i, make in (rows_a(half, gz), rows_b(half, gz)):

            @pl.when(i != 0)
            def _(make=make):
                make().start()

    for half in range(2):
        partial(half, z)
    for slot in range(SLOTS):
        for half in range(2):
            last = acc.at[half, NZ - 2 - NB, slot]
            hop32(half, slot, NZ - 2, last).wait_recv()
            g = acc[half, NZ - 2 - NB, slot, 0:FH, :] + own[half, slot, 0:FH, :]
            u = acc[half, NZ - 2 - NB, slot, FH : 2 * FH, :] + own[half, slot, FH : 2 * FH, :]
            dh = acc[half, NZ - 2 - NB, slot, 2 * FH : F3, :] + own[half, slot, 2 * FH : F3, :]
            sig = 1.0 / (1.0 + jnp.exp(-g))
            act = g * sig
            dg = dh * u * sig * (1.0 + g * (1.0 - sig))
            du = dh * act
            hid = act * u
            hcat[slot, 0 : 2 * FH, lanes(half, z)] = jnp.concatenate([dg, du], axis=0).astype(BF16)
            hcat[slot, 2 * FH : FP, lanes(half, z)] = jnp.concatenate(
                [hid, jnp.zeros((FP - F3, TOK), F32)], axis=0
            ).astype(BF16)
            gather(half, slot, 0, z).start()
    for half in range(2):
        rows(half, z)

    def pass_on(s, carry):
        for slot in range(SLOTS):
            for half in range(2):
                gather(half, slot, s - 1, origin(half, s)).wait_recv()
                gather(half, slot, s, origin(half, s)).start()
        for half in range(2):
            rows(half, origin(half, s))
        return carry

    lax.fori_loop(1, NZ - 1, pass_on, 0)
    for half in range(2):
        for slot in range(SLOTS):
            gather(half, slot, NZ - 2, origin(half, NZ - 1)).wait_recv()
        rows(half, origin(half, NZ - 1))

    cols = NXH * NZ * TOK
    def expert_row(slot):
        return jnp.concatenate(
            [
                scale[i // NZ, i % NZ, 2 + slot : 3 + slot, :]
                for i in range(NXH * NZ)
            ],
            axis=1,
        )

    id0, id1 = expert_row(0), expert_row(1)
    nt = (((1,), (1,)), ((), ()))

    def weights(e):
        is0 = jnp.broadcast_to(id0 == e.astype(F32), (16, cols))
        is1 = jnp.broadcast_to(id1 == e.astype(F32), (16, cols))
        zero = jnp.zeros((16, cols), BF16)

        def pick(pair, n):
            return jnp.concatenate(
                [
                    jnp.where(
                        is0,
                        pair[0, r * 16 : (r + 1) * 16, :],
                        jnp.where(is1, pair[1, r * 16 : (r + 1) * 16, :], zero),
                    )
                    for r in range(n // 16)
                ],
                axis=0,
            )

        hs = pick(hcat, FP)
        ds = pick(dcat, DZ)
        gu = lax.dot_general(x[0], hs, nt, preferred_element_type=F32)
        dn = lax.dot_general(ds, hs[256:], nt, preferred_element_type=F32)
        column = lax.broadcasted_iota(jnp.int32, (DZ, FP - 256), 1)
        tail = jnp.where(column < 2 * FH - 256, gu[:, 256:], dn)
        for q in range(NXH * NC):
            dw[e, q, :, 0:256] = gu[q * SUB : (q + 1) * SUB, 0:256]
            dw[e, q, :, 256:FP] = tail[q * SUB : (q + 1) * SUB]

    def cross(e, i):
        blk = (1 - xh) if i == 0 else xh
        return remote(dw.at[e, 2 * blk + 1 - c], wgot.at[i, e], ts.at[i, e], tr.at[i, e], twin)

    def away(e):
        return remote(wsnd.at[e], wfar.at[e], fs.at[e], fr.at[e], far)

    def combine(e):
        cross(e, 0).wait_recv()
        wsnd[e] = (dw[e, 2 * (1 - xh) + c] + wgot[0, e]).astype(BF16)
        away(e).start()
        cross(e, 1).wait_recv()
        wgot[1, e] = dw[e, 2 * xh + c] + wgot[1, e]

    def second(i, kind):
        if kind == 0:
            t = (pos + i + 1) % 4
            return remote(sa.at[t // 2, t % 2], a2.at[i], a2s.at[i], a2r.at[i], xp[i])
        t = (y + i + 1) % NY
        return remote(sb.at[t], b2.at[i], b2s.at[i], b2r.at[i], yp[i])

    def rows_second():
        for i in range(3):
            for j in range(NXH):
                for k in range(NXL):
                    remote(
                        dxs.at[0, 0, 0, pl.ds(0, hd)], a1.at[i, j, k], a1s.at[0, 0],
                        a1r.at[i, j, k], up,
                    ).wait_recv()
        for j in range(NXH):
            for k in range(NXL):
                sa[j, k] = dx[j, k, y, 0:hd] + (
                    a1[0, j, k].astype(F32) + a1[1, j, k].astype(F32) + a1[2, j, k].astype(F32)
                )
        for i in range(3):
            second(i, 0).start()
        for i in range(3):
            for j in range(NY):
                remote(
                    dxs.at[0, 0, 0, pl.ds(hd, hd)], b1.at[i, j], b1s.at[0, 0], b1r.at[i, j], up
                ).wait_recv()
        for j in range(NY):
            sb[j] = dx[xh, xl, j, hd:DZ] + (
                b1[0, j].astype(F32) + b1[1, j].astype(F32) + b1[2, j].astype(F32)
            )
        for i in range(3):
            second(i, 1).start()

    def rows_swap():
        for i in range(3):
            second(i, 0).wait_recv()
        done[0:hd] = sa[xh, xl] + a2[0] + a2[1] + a2[2]
        for i in range(3):
            second(i, 1).wait_recv()
        done[hd:DZ] = sb[y] + b2[0] + b2[1] + b2[2]

        @pl.when(pair != z)
        def _():
            first_step().start()

    def first_step():
        return remote(done, mid, ks.at[0], kr.at[0], along)

    def second_step():
        return remote(mid, back, ks.at[1], kr.at[1], across)

    def rows_turn():
        @pl.when(pair != z)
        def _():
            first_step().wait_recv()

        @pl.when(pair == z)
        def _():
            mid[...] = done[...]

        @pl.when(z != 0)
        def _():
            second_step().start()

        @pl.when(z == 0)
        def _():
            back[...] = mid[...]

    def finish(e):
        away(e).wait_recv()
        ours = wgot[1, e]
        theirs = wfar[e].astype(F32)
        low = jnp.where(xh == 0, ours, theirs).T
        high = jnp.where(xh == 0, theirs, ours).T
        for i, out in enumerate((gate, up_out, down_out)):
            out[e, 0:FH, :] = low[i * FH : (i + 1) * FH]
            out[e, FH : 2 * FH, :] = high[i * FH : (i + 1) * FH]

    def per_expert(e, carry):
        weights(e)
        cross(e, 0).start()
        cross(e, 1).start()

        @pl.when(e > 0)
        def _():
            combine(e - 1)

        @pl.when(e == 0)
        def _():
            rows_second()

        @pl.when(e == SWAP_AT)
        def _():
            rows_swap()

        return carry

    lax.fori_loop(0, EXPERTS, per_expert, 0)
    combine(EXPERTS - 1)

    def finish_all(e, carry):
        finish(e)

        @pl.when(e == TURN_AT)
        def _():
            rows_turn()

        return carry

    lax.fori_loop(0, EXPERTS, finish_all, 0)

    def drain_ring(s, carry):
        for half in range(2):
            for slot in range(SLOTS):
                gather(half, slot, s, origin(half, s)).wait_send()
        return carry

    for half in range(2):
        for slot in range(SLOTS):
            hop16(half, slot, 0, first.at[half, slot]).wait_send()
            for s in range(1, NB):
                hop16(half, slot, s, early.at[half, s - 1, slot]).wait_send()
            hop32(half, slot, NB, turn.at[half, slot]).wait_send()
            for s in range(NB + 1, NZ - 1):
                hop32(half, slot, s, acc.at[half, s - 1 - NB, slot]).wait_send()
    lax.fori_loop(1, NZ - 1, drain_ring, 0)
    for half in range(2):
        for slot in range(SLOTS):
            gather(half, slot, 0, z).wait_send()

    def drain(s, carry):
        for i in range(3):
            spread(s, i).wait_send()
        for half in range(2):
            for i, make in (rows_a(half, s), rows_b(half, s)):

                @pl.when(i != 0)
                def _(make=make):
                    make().wait_send()

        cross(s, 0).wait_send()
        cross(s, 1).wait_send()
        away(s).wait_send()
        return carry

    lax.fori_loop(0, NZ, drain, 0)
    for i in range(3):
        second(i, 0).wait_send()
        second(i, 1).wait_send()

    @pl.when(pair != z)
    def _():
        first_step().wait_send()

    @pl.when(z != 0)
    def _():
        second_step().wait()


def layer(act, cot, rows, counts, probs, ids, wg, wu, wd):
    dma = pltpu.SemaphoreType.DMA
    vm = pl.BlockSpec(memory_space=pltpu.VMEM)
    sm = pl.BlockSpec(memory_space=pltpu.SMEM)
    hd = DZ // 2
    cols = NXH * NZ * TOK
    block = (EXPERTS, SUB, FP)
    return pl.pallas_call(
        layer_kernel,
        out_shape=(
            jax.ShapeDtypeStruct((EXPERTS, 2 * FH, SUB), F32),
            jax.ShapeDtypeStruct((EXPERTS, 2 * FH, SUB), F32),
            jax.ShapeDtypeStruct((EXPERTS, 2 * FH, SUB), F32),
            jax.ShapeDtypeStruct((DZ, TOK), F32),
        ),
        in_specs=[vm, vm, vm, sm, vm, sm, vm, vm, vm],
        out_specs=(vm,) * 4,
        scratch_shapes=[
            pltpu.VMEM((NZ * DZ, TOK), BF16),
            pltpu.VMEM((8, TOK), F32),
            pltpu.VMEM((8, TOK), F32),
            pltpu.VMEM((8, TOK), jnp.int32),
            pltpu.VMEM(block, BF16),
            pltpu.VMEM((EXPERTS, NXH * NC, SUB, FP), BF16),
            pltpu.VMEM((EXPERTS, FP, DZ), BF16),
            pltpu.VMEM((NZ, DZ, TOK), BF16),
            pltpu.VMEM((NXH, NZ, 8, TOK), F32),
            pltpu.VMEM((NXH, NZ, 8, TOK), jnp.int32),
            pltpu.VMEM((2, DZ, cols), BF16),
            pltpu.VMEM((2, NB, SLOTS, FP, TOK), BF16),
            pltpu.VMEM((2, SLOTS, FP, TOK), BF16),
            pltpu.VMEM((2, NZ - 1 - NB, SLOTS, F3, TOK), F32),
            pltpu.VMEM((2, SLOTS, F3, TOK), F32),
            pltpu.VMEM((2, SLOTS, FP, TOK), F32),
            pltpu.VMEM((SLOTS, DZ, cols), BF16),
            pltpu.VMEM((SLOTS, FP, cols), BF16),
            pltpu.VMEM((NXH, NXL, NY, DZ, TOK), F32),
            pltpu.VMEM((NXH, NXL, NY, DZ, TOK), BF16),
            pltpu.VMEM((EXPERTS, NXH * NC, SUB, FP), F32),
            pltpu.VMEM((2,) + block, F32),
            pltpu.VMEM(block, BF16),
            pltpu.VMEM(block, BF16),
            pltpu.VMEM((3, NXH, NXL, hd, TOK), BF16),
            pltpu.VMEM((3, hd, TOK), F32),
            pltpu.VMEM((3, NY, hd, TOK), BF16),
            pltpu.VMEM((3, hd, TOK), F32),
            pltpu.VMEM((NXH, NXL, hd, TOK), F32),
            pltpu.VMEM((NY, hd, TOK), F32),
            pltpu.VMEM((DZ, TOK), F32),
            pltpu.VMEM((DZ, TOK), F32),
        ]
        + [dma((NZ - 1,))] * 6 + [dma((3,))] * 2 + [dma((2,))] * 2 + [dma((EXPERTS,))] * 6
        + [dma((3,))]
        + [dma((NZ, 3))] * 2
        + [dma((2, NZ - 1, SLOTS))] * 4
        + [dma((2, NZ)), dma((3, NXH, NXL)), dma((2, NZ)), dma((3, NY))]
        + [dma((3,))] * 4
        + [dma((2, EXPERTS))] * 2
        + [dma((EXPERTS,))] * 2
        + [dma((2,))] * 2,
        compiler_params=pltpu.CompilerParams(
            collective_id=0, has_side_effects=True, vmem_limit_bytes=VMEM_LIMIT
        ),
        name="layer",
    )(act, cot, rows, counts, probs, ids, wg, wu, wd)


def shards(
    activations, cotangent, expert_ids, slot_rows, slot_counts, route_probs, w_gate, w_up, w_down
):
    grad_gate, grad_up, grad_down, rows = layer(
        activations, cotangent, slot_rows[0], slot_counts, route_probs[0], expert_ids,
        w_gate.transpose(0, 2, 1), w_up.transpose(0, 2, 1), w_down,
    )
    return rows.T, grad_gate.transpose(0, 2, 1), grad_up.transpose(0, 2, 1), grad_down


def solution(mesh):
    return jax.shard_map(
        shards,
        mesh=mesh,
        in_specs=(
            P("dp", None),
            P("dp", None),
            P("dp", None),
            P("dp", None, None),
            P("dp", None),
            P("dp", None, None),
            P(None, "dp", "expert"),
            P(None, "dp", "expert"),
            P(None, "expert", "dp"),
        ),
        out_specs=(
            P("dp", "expert"),
            P(None, "dp", "expert"),
            P(None, "dp", "expert"),
            P(None, "expert", "dp"),
        ),
        check_vma=False,
    )
```
